128 devices in a mesh: dx: 16 (over y, z), dy: 8 (over x, core).
Axes of the slice: x: 4, y: 4, z: 4, core: 2. Of those that a mesh axis runs over, the one named last changes fastest.
Arguments:
- coarse_states: bfloat16 [2048, 125, 128], P(('dx', 'dy')), may hold values from -50 to 50
- record_target: int32 [2048], P(('dx', 'dy')), may hold values from 0 to 2047, as said below
- cell_matrix: bfloat16 [343, 343], replicated, may hold values from -0.5 to 2.25, as said below
- mass_scale: float32 [192, 96, 24], P('dx', 'dy'), may hold values from 0.6 to 1.2
- potential: float32 [192, 96, 24], P('dx', 'dy'), may hold values from -2 to 1
- filter_window: float32 [2], replicated, may hold values from 1.5 to 30, as said below
Outputs:
- states: float32 [192, 96, 24, 128], P('dx', 'dy')
- gram: float32 [128, 128], replicated
The draws below stay inside these ranges and needn't reach their ends.
Inputs may be any that keep to these rules, and one draw needn't show every extreme that they name: record_target is a permutation of the 2048 fine cells; each device receives records for exactly its 16 cells; the records of the device with dx index i and dy index j name only cells of the four devices with dx index i + a and dy index j + b (taken modulo the axes' sizes), a and b each 0 or 1, at least one and at most 8 cells of each of the four; the four counts are the same on every device, and one of them is exactly 8 in every draw. `cell_matrix`: symmetric. filter_window[0] < filter_window[1].
All inputs are finite; a program needn't handle non-finite values.
Results may differ from the reference program's by a relative error of at most 0.0038.
Values may be sent and summed in bfloat16 or wider, within the bound.
A program may use at most 64 MiB of HBM per device.

```python
import math
import jax
import jax.numpy as jnp
import numpy as np
from jax import lax

STATES = 128
ORDER = 6
COARSE_ORDER = 4
CHEB_DEGREE = 3
EX = 2
EY = 2
EZ = 4
CELLS_DEV = 16
CELLS = 2048
CAP = 8
CELL_NODES = 343
COARSE_NODES = 125
NZ = 24
NX = 192
NY = 96
NODES = 442368
N_DX = 16
N_DY = 8
DEVICES = 128


def draw_coarse_states(key, part):
    key = jax.random.fold_in(key, 11)
    key_base, key_rows, key_cols = jax.random.split(key, 3)
    full_shape = (CELLS, COARSE_NODES, STATES)
    row_scale = jnp.exp(jax.random.uniform(key_rows, (CELLS, 1, 1), minval=0.0, maxval=math.log(10.0)))
    columns = jnp.exp(jax.random.uniform(key_cols, (1, 1, STATES), minval=0.0, maxval=math.log(10.0)))
    base_values = jax.random.truncated_normal(key_base, -4.0, 4.0, full_shape)
    return (base_values * row_scale * columns / 8.0).astype(jnp.bfloat16)


def one_order(order_key):
    return jax.random.permutation(order_key, CELLS_DEV).astype(jnp.int32)


def draw_record_target(key, part):
    key = jax.random.fold_in(key, 23)
    key_first, key_low, key_high, key_cells, key_slots = jax.random.split(key, 5)
    first = jax.random.randint(key_first, (), 0, 4).astype(jnp.int32)
    low_cut = jax.random.randint(key_low, (), 1, CAP - 1).astype(jnp.int32)
    high_raw = jax.random.randint(key_high, (), 0, CAP).astype(jnp.int32)
    high_cut = low_cut + 1 + high_raw % (CAP - 1 - low_cut)
    rest = jnp.stack([low_cut, high_cut - low_cut, CAP - high_cut]).astype(jnp.int32)
    others = (first + 1 + jnp.arange(3, dtype=jnp.int32)) % 4
    counts = jnp.zeros((4,), jnp.int32).at[first].set(CAP).at[others].set(rest)
    ends = jnp.cumsum(counts)
    starts = ends - counts
    slot_index = jnp.arange(CELLS_DEV, dtype=jnp.int32)
    bucket = jnp.sum((ends[None, :] <= slot_index[:, None]).astype(jnp.int32), axis=1)
    rank = slot_index - starts[bucket]
    sender = jnp.arange(DEVICES, dtype=jnp.int32)
    sender_x = sender // N_DY
    sender_y = sender % N_DY
    receiver = (sender_x[:, None] + bucket[None, :] // 2) % N_DX * N_DY + (sender_y[:, None] + bucket[None, :] % 2) % N_DY
    cell_orders = jax.vmap(one_order)(jax.random.split(key_cells, DEVICES))
    local_cell = cell_orders[receiver, (starts[bucket] + rank)[None, :]]
    target = receiver * CELLS_DEV + local_cell
    slot_orders = jax.vmap(one_order)(jax.random.split(key_slots, DEVICES))
    target = jnp.take_along_axis(target, slot_orders, axis=1)
    return target.reshape(-1).astype(jnp.int32)


def draw_cell_matrix(key, part):
    key = jax.random.fold_in(key, 31)
    key_off, key_diag = jax.random.split(key)
    raw_values = jax.random.truncated_normal(key_off, -4.0, 4.0, (CELL_NODES, CELL_NODES))
    diagonal = jax.random.uniform(key_diag, (CELL_NODES,), minval=1.0, maxval=2.0)
    coupling = (raw_values + raw_values.T) * (0.45 / math.sqrt(CELL_NODES))
    on_diagonal = jnp.arange(CELL_NODES)[:, None] == jnp.arange(CELL_NODES)[None, :]
    full_diagonal = diagonal[:, None] * jnp.ones((1, CELL_NODES), jnp.float32)
    return jnp.where(on_diagonal, full_diagonal, coupling).astype(jnp.bfloat16)


def draw_filter_window(key, part):
    key = jax.random.fold_in(key, 47)
    key_low, key_high = jax.random.split(key)
    low_end = jax.random.uniform(key_low, (), minval=2.0, maxval=3.0)
    high_end = jax.random.uniform(key_high, (), minval=24.0, maxval=28.0)
    return jnp.stack([low_end, high_end]).astype(jnp.float32)


def shard_levels(stream_key, dims, cuts, low, largest):
    def one(axis_at, blocks):
        steps = jax.random.uniform(jax.random.fold_in(jax.random.fold_in(stream_key, 6), axis_at), (blocks,), jnp.float32, low / len(cuts), largest / len(cuts))
        return jnp.repeat(jnp.exp(steps), dims[axis_at] // blocks).reshape((-1,) + (1,) * (len(dims) - axis_at - 1))

    gain = one(*cuts[0])
    for cut in cuts[1:]:
        gain = gain * one(*cut)
    return gain


def setup_inputs(seed: int = 0) -> dict:
    arg_keys = jax.random.split(jax.random.key(seed), 7)
    return {
        "coarse_states": draw_coarse_states(jax.random.fold_in(arg_keys[6], 71), 0),
        "record_target": draw_record_target(jax.random.fold_in(arg_keys[6], 71), 0),
        "cell_matrix": draw_cell_matrix(jax.random.fold_in(arg_keys[6], 71), 0),
        "mass_scale": jnp.clip(jnp.exp(math.log(1.2) - 0.6931472 * jax.random.uniform(arg_keys[3], (NX, NY, NZ), jnp.float32) ** shard_levels(arg_keys[3], (NX, NY, NZ), ((0, 16), (1, 8)), -0.2, 0.2)), 0.6, 1.2),
        "potential": jnp.clip(-2.0 + 3.0 * jax.random.uniform(arg_keys[4], (NX, NY, NZ), jnp.float32) ** shard_levels(arg_keys[4], (NX, NY, NZ), ((0, 16), (1, 8)), -0.2, 0.2), -2.0, 1.0),
        "filter_window": draw_filter_window(jax.random.fold_in(arg_keys[6], 71), 0),
    }


def node_points(degree_value):
    return -np.cos(np.pi * np.arange(degree_value + 1) / degree_value)

def lagrange_table(fine_degree, coarse_degree):
    targets = node_points(fine_degree)
    sources = node_points(coarse_degree)
    matrix = np.ones((fine_degree + 1, coarse_degree + 1))
    for p in range(coarse_degree + 1):
        for m in range(coarse_degree + 1):
            if m != p:
                matrix[:, p] = matrix[:, p] * (targets - sources[m]) / (sources[p] - sources[m])
    owned_rows = matrix[:fine_degree]
    first = owned_rows[:, None, None, :, None, None]
    second = owned_rows[None, :, None, None, :, None]
    third = owned_rows[None, None, :, None, None, :]
    product = first * second * third
    return product.reshape(fine_degree ** 3, (coarse_degree + 1) ** 3)

def cell_windows(values, dim_index, cell_count):
    pieces = [lax.slice_in_dim(values, offset, offset + ORDER * (cell_count - 1) + 1, stride=ORDER, axis=dim_index) for offset in range(ORDER + 1)]
    return jnp.stack(pieces, axis=dim_index + 1)

def fold_periodic(values, dim_index):
    reordered = jnp.moveaxis(values, (dim_index, dim_index + 1), (0, 1))
    interior = reordered[:, :ORDER]
    interior = interior.at[:, 0].add(jnp.roll(reordered[:, ORDER], 1, axis=0))
    merged = interior.reshape((interior.shape[0] * ORDER,) + interior.shape[2:])
    return jnp.moveaxis(merged, 0, dim_index)

def apply_h(values, mass_scale, potential, cell_matrix):
    scaled = (mass_scale[..., None] * values).astype(jnp.bfloat16)
    extended = jnp.concatenate([scaled, scaled[:1]], axis=0)
    extended = jnp.concatenate([extended, extended[:, :1]], axis=1)
    extended = jnp.concatenate([extended, extended[:, :, :1]], axis=2)
    count_x = NX // ORDER
    count_y = NY // ORDER
    count_z = NZ // ORDER
    points = ORDER + 1
    state_count = values.shape[-1]
    matrix = cell_matrix.astype(jnp.float32)

    def one_slab(slab_index):
        slab_nodes = lax.dynamic_slice_in_dim(extended, slab_index * ORDER, points, 0)
        gathered = cell_windows(slab_nodes, 1, count_y)
        gathered = cell_windows(gathered, 3, count_z)
        flattened = gathered.transpose(1, 3, 0, 2, 4, 5).reshape(count_y * count_z, points ** 3, state_count)
        partials = jnp.einsum('mn,kns->kms', matrix, flattened.astype(jnp.float32))
        partials = partials.reshape(count_y, count_z, points, points, points, state_count).transpose(2, 0, 3, 1, 4, 5)
        partials = fold_periodic(partials, 3)
        return fold_periodic(partials, 1)
    slabs = lax.map(one_slab, jnp.arange(count_x, dtype=jnp.int32))
    assembled = fold_periodic(slabs, 0)
    return mass_scale[..., None] * assembled + potential[..., None] * values

def cheb_filter(current_block, mass_scale, potential, cell_matrix, filter_window):
    center = (filter_window[0] + filter_window[1]) / 2.0
    radius = (filter_window[1] - filter_window[0]) / 2.0
    previous = current_block
    current = (apply_h(current_block, mass_scale, potential, cell_matrix) - center * current_block) / radius
    for degree_step in range(CHEB_DEGREE - 1):
        following = 2.0 * (apply_h(current, mass_scale, potential, cell_matrix) - center * current) / radius - previous
        previous, current = (current, following)
    return current

def orthonormal(filtered):
    state_count = filtered.shape[-1]
    flattened = filtered.reshape(-1, state_count)
    gram_matrix = jnp.dot(flattened.T.astype(jnp.float32), flattened.astype(jnp.float32), precision=lax.Precision.HIGHEST, preferred_element_type=jnp.float32) / NODES
    factor = jnp.linalg.cholesky(gram_matrix)
    inverse = lax.linalg.triangular_solve(factor, jnp.eye(state_count, dtype=jnp.float32), left_side=True, lower=True)
    result = jnp.dot(flattened.astype(jnp.float32), inverse.T.astype(jnp.float32), precision=lax.Precision.HIGHEST, preferred_element_type=jnp.float32)
    return (result.reshape(filtered.shape), gram_matrix)

def reference(coarse_states, record_target, cell_matrix, mass_scale, potential, filter_window):
    interp_table = jnp.asarray(lagrange_table(ORDER, COARSE_ORDER), jnp.float32).astype(jnp.bfloat16)
    state_count = coarse_states.shape[-1]
    placed = jnp.zeros_like(coarse_states).at[record_target].set(coarse_states)
    grouped = placed.reshape(DEVICES, CELLS_DEV, COARSE_NODES, state_count)

    def interpolate(records):
        return jnp.einsum('on,kns->kos', interp_table.astype(jnp.float32), records.astype(jnp.float32)).astype(jnp.bfloat16)
    cell_values = lax.map(interpolate, grouped)
    start_block = cell_values.reshape(N_DX, N_DY, EX, EY, EZ, ORDER, ORDER, ORDER, state_count)
    start_block = start_block.transpose(0, 2, 5, 1, 3, 6, 4, 7, 8).reshape(NX, NY, NZ, state_count)
    current_block = start_block.astype(jnp.float32)
    gram_matrix = jnp.zeros((state_count, state_count), jnp.float32)
    for filter_pass in range(2):
        filtered = cheb_filter(current_block, mass_scale, potential, cell_matrix, filter_window)
        current_block, gram_matrix = orthonormal(filtered)
    return (current_block, gram_matrix)
```

```python
import functools

import jax
import jax.numpy as jnp
import numpy as np
from jax import lax
from jax.experimental import pallas as pl
from jax.experimental.pallas import tpu as pltpu
from jax.sharding import PartitionSpec as P

ORDER = 6
COARSE_ORDER = 4
CHEB_DEGREE = 3
POINTS = ORDER + 1
COUNT_Z = 4
SLOT = 8
COLUMN = COUNT_Z * SLOT
ROWS = 12
STATES = 128
PAIRS = 4
KDIM = POINTS * SLOT * SLOT
MESH = pl.DeviceIdType.MESH
F32 = jnp.float32
BF16 = jnp.bfloat16


def shifted(block, axis, distance):
    devices = range(lax.axis_size(axis))
    route = [((i - distance) % len(devices), i) for i in devices]
    return lax.ppermute(block, axis, route)


def node_points(degree_value):
    return -np.cos(np.pi * np.arange(degree_value + 1) / degree_value)


def lagrange_table(fine_degree, coarse_degree):
    targets = node_points(fine_degree)
    sources = node_points(coarse_degree)
    matrix = np.ones((fine_degree + 1, coarse_degree + 1))
    for p in range(coarse_degree + 1):
        for m in range(coarse_degree + 1):
            if m != p:
                matrix[:, p] = matrix[:, p] * (targets - sources[m]) / (sources[p] - sources[m])
    owned_rows = matrix[:fine_degree]
    first = owned_rows[:, None, None, :, None, None]
    second = owned_rows[None, :, None, None, :, None]
    third = owned_rows[None, None, :, None, None, :]
    product = first * second * third
    return product.reshape(fine_degree**3, (coarse_degree + 1) ** 3)


def row_in_slot(shape, axis):
    return lax.broadcasted_iota(jnp.int32, shape, axis) % SLOT


def dot_nn(a, b):
    return lax.dot_general(a, b, (((1,), (0,)), ((), ())), preferred_element_type=F32)


def dot_tn(a, b):
    return lax.dot_general(a, b, (((0,), (0,)), ((), ())), preferred_element_type=F32)


def dot_nt(a, b):
    return lax.dot_general(a, b, (((1,), (1,)), ((), ())), preferred_element_type=F32)


def split_two(value):
    high = value.astype(BF16)
    return high, (value - high.astype(F32)).astype(BF16)


def split_three(value):
    high = value.astype(BF16)
    rest = value - high.astype(F32)
    middle = rest.astype(BF16)
    return high, middle, (rest - middle.astype(F32)).astype(BF16)


def factor_rows(work):
    size = STATES
    sub = lax.broadcasted_iota(jnp.int32, (SLOT, size), 0)
    lane = lax.broadcasted_iota(jnp.int32, (SLOT, size), 1)

    def panel(j, carry):
        base = pl.multiple_of(j * SLOT, SLOT)
        left = work[pl.ds(base, SLOT), 0:size]
        right = work[pl.ds(base, SLOT), size : 2 * size]
        turned = pltpu.roll(left, lax.rem(size - base, size), 1)
        columns = [jnp.broadcast_to(turned[:, m : m + 1], (SLOT, size)) for m in range(SLOT)]
        for m in range(SLOT):
            pivot = jnp.broadcast_to(columns[m][m : m + 1, :], (SLOT, size))
            scale = lax.rsqrt(pivot)
            scale = scale * (1.5 - 0.5 * pivot * scale * scale)
            below = sub > m
            at = sub == m
            coef = columns[m] * scale
            row_left = jnp.broadcast_to(left[m : m + 1, :], (SLOT, size)) * scale
            row_right = jnp.broadcast_to(right[m : m + 1, :], (SLOT, size)) * scale
            for n in range(m + 1, SLOT):
                entry = jnp.broadcast_to(columns[n][m : m + 1, :], (SLOT, size)) * scale
                columns[n] = jnp.where(below, columns[n] - coef * entry, columns[n])
            left = jnp.where(below, left - coef * row_left, jnp.where(at, row_left, left))
            right = jnp.where(below, right - coef * row_right, jnp.where(at, row_right, right))
        work[pl.ds(base, SLOT), 0:size] = left
        work[pl.ds(base, SLOT), size : 2 * size] = right
        later = jnp.where(lane >= base + SLOT, left, 0.0)
        l1, l2, l3 = [v.astype(F32) for v in split_three(later)]
        both = jnp.concatenate([left, right], axis=1)
        b1, b2, b3 = [v.astype(F32) for v in split_three(both)]
        lhs = jnp.concatenate([l1, l1, l2, l1, l3, l2], axis=0).astype(BF16)
        rhs = jnp.concatenate([b1, b2, b1, b3, b1, b2], axis=0).astype(BF16)
        work[...] = work[...] - dot_tn(lhs, rhs)
        return carry

    lax.fori_loop(0, size // SLOT, panel, 0)


def filter_kernel(
    size_x,
    size_y,
    node_total,
    window,
    start,
    mass,
    pot,
    matrix,
    filtered,
    inverse_out,
    gram_out,
    block,
    total,
    rhs,
    send_x,
    send_y,
    take_x,
    take_y,
    take_c,
    back_x,
    back_y,
    back_c,
    got_x,
    got_y,
    got_c,
    split,
    partial,
    piece_in,
    ring_in,
    gram_sum,
    work,
    start_sem,
    send_sems,
    recv_sems,
    sum_send,
    sum_recv,
):
    me_x = lax.axis_index("dx")
    me_y = lax.axis_index("dy")

    def at(step_x, step_y):
        return (lax.rem(me_x + step_x + size_x, size_x), lax.rem(me_y + step_y + size_y, size_y))

    partners = [at(0, d) for d in range(1, size_y)] + [at(d, 0) for d in range(1, size_x)]
    partners += [at(1, 1), at(-1, -1)]
    barrier = pltpu.get_barrier_semaphore()
    for partner in partners:
        pl.semaphore_signal(barrier, inc=1, device_id=partner, device_id_type=MESH)
    fetch = pltpu.make_async_copy(start, block.at[0, 0:ROWS, 0:ROWS], start_sem)
    fetch.start()
    block[1] = jnp.zeros(block.shape[1:], F32)
    total[...] = jnp.zeros(total.shape, F32)
    fetch.wait()
    pl.semaphore_wait(barrier, len(partners))

    low = window[0]
    high = window[1]
    center = (low + high) / 2.0
    radius = (high - low) / 2.0

    def remote(index, src, dst, step_x, step_y):
        return pltpu.make_async_remote_copy(
            src_ref=src,
            dst_ref=dst,
            send_sem=send_sems.at[index],
            recv_sem=recv_sems.at[index],
            device_id=at(step_x, step_y),
            device_id_type=MESH,
        )

    def column(q, e, f):
        base_x = e * ORDER
        base_y = f * ORDER
        for a in range(POINTS):
            for i in range(PAIRS):
                for h in range(COUNT_Z):
                    parts = []
                    for b in (2 * i, 2 * i + 1):
                        if b < POINTS:
                            rows = pl.ds(h * SLOT, SLOT)
                            parts.append(
                                mass[base_x + a, base_y + b, rows]
                                * block[q, base_x + a, base_y + b, rows]
                            )
                        else:
                            parts.append(jnp.zeros((SLOT, STATES), F32))
                    rhs[
                        pl.ds((a * PAIRS + i) * 2 * SLOT, 2 * SLOT), pl.ds(h * STATES, STATES)
                    ] = jnp.concatenate(parts, axis=0).astype(BF16)
        product = dot_nn(matrix[...], rhs[...])
        for a in range(POINTS):
            for b in range(POINTS):
                first = (a * SLOT + b) * SLOT
                for h in range(COUNT_Z):
                    rows = pl.ds(h * SLOT, SLOT)
                    total[base_x + a, base_y + b, rows] += product[
                        first : first + SLOT, h * STATES : (h + 1) * STATES
                    ]

    def finish(q, x, y, count, alpha, beta):
        shape = (count, COLUMN, STATES)
        slot_row = row_in_slot(shape, 1)
        ys = pl.ds(y, count)
        raw = total[x, ys]
        total[x, ys] = jnp.zeros(shape, F32)
        summed = raw + jnp.where(slot_row == 0, pltpu.roll(raw, SLOT - ORDER, 1), 0.0)
        again = pltpu.roll(summed, COLUMN - SLOT + ORDER, 1)
        full = jnp.where(slot_row < ORDER, summed, jnp.where(slot_row == ORDER, again, 0.0))
        value = block[q, x, ys]
        result = mass[x, ys] * full + (pot[x, ys] - center) * value
        block[1 - q, x, ys] = alpha * result - beta * block[1 - q, x, ys]

    def one_apply(k, p):
        q = lax.rem(p * CHEB_DEGREE + k, 2)
        first = k == 0
        alpha = jnp.where(first, 1.0, 2.0) / radius
        beta = jnp.where(first, 0.0, 1.0)
        send_x[...] = (mass[0, 0:ROWS] * block[q, 0, 0:ROWS]).astype(BF16)
        send_y[...] = (mass[0:ROWS, 0] * block[q, 0:ROWS, 0]).astype(BF16)
        values = [
            remote(0, send_x, take_x, -1, 0),
            remote(1, send_y, take_y, 0, -1),
            remote(2, send_x.at[0], take_c, -1, -1),
        ]
        for copy in values:
            copy.start()
        column(q, 0, 0)
        for copy in values:
            copy.wait()
        block[q, ROWS, 0:ROWS] = take_x[...].astype(F32)
        block[q, 0:ROWS, ROWS] = take_y[...].astype(F32)
        block[q, ROWS, ROWS] = take_c[...].astype(F32)

        def others(index, carry):
            column(q, index // 2, lax.rem(index, 2))
            return carry

        lax.fori_loop(1, 4, others, 0)
        back_x[...] = total[ROWS, 0:ROWS].astype(BF16)
        back_y[...] = total[0:ROWS, ROWS].astype(BF16)
        back_c[...] = total[ROWS, ROWS].astype(BF16)
        sums = [
            remote(3, back_x, got_x, 1, 0),
            remote(4, back_y, got_y, 0, 1),
            remote(5, back_c, got_c, 1, 1),
        ]
        for copy in sums:
            copy.start()
        total[ROWS] = jnp.zeros(total.shape[1:], F32)
        total[0:ROWS, ROWS] = jnp.zeros((ROWS, COLUMN, STATES), F32)

        def interior(x, carry):
            finish(q, x, 1, ROWS - 1, alpha, beta)
            return carry

        lax.fori_loop(1, ROWS, interior, 0)
        for copy in sums:
            copy.wait()
        total[0, 0:ROWS] += got_x[...].astype(F32)
        total[0:ROWS, 0] += got_y[...].astype(F32)
        total[0, 0] += got_c[...].astype(F32)
        finish(q, 0, 0, ROWS, alpha, beta)

        def edge(x, carry):
            finish(q, x, 0, 1, alpha, beta)
            return carry

        lax.fori_loop(1, ROWS, edge, 0)

    def sum_everywhere(p):
        share = STATES // size_y

        def move(index, src, dst, device):
            return pltpu.make_async_remote_copy(
                src_ref=src,
                dst_ref=dst,
                send_sem=sum_send.at[p, index],
                recv_sem=sum_recv.at[p, index],
                device_id=device,
                device_id_type=MESH,
            )

        def rows_of(owner):
            return pl.ds(pl.multiple_of(owner * share, SLOT), share)

        mine = rows_of(me_y)
        copies = []
        for d in range(1, size_y):
            device = at(0, d)
            copies.append(
                move(d - 1, partial.at[rows_of(device[1])], piece_in.at[p, d - 1], device)
            )
        for copy in copies:
            copy.start()
        for copy in copies:
            copy.wait()
        piece = partial[mine, :]
        for d in range(1, size_y):
            piece = piece + piece_in[p, d - 1]
        ring_in[p, me_x] = piece
        copies = []
        for d in range(1, size_x):
            copies.append(
                move(size_y + d - 2, ring_in.at[p, me_x], ring_in.at[p, me_x], at(d, 0))
            )
        for copy in copies:
            copy.start()
        for copy in copies:
            copy.wait()
        piece = ring_in[p, 0]
        for d in range(1, size_x):
            piece = piece + ring_in[p, d]
        gram_sum[p, mine] = piece / node_total
        copies = []
        for d in range(1, size_y):
            copies.append(
                move(
                    size_y + size_x + d - 3, gram_sum.at[p, mine], gram_sum.at[p, mine], at(0, d)
                )
            )
        for copy in copies:
            copy.start()
        for copy in copies:
            copy.wait()

    def one_pass(p, carry):
        def step(k, inner):
            one_apply(k, p)
            return inner

        lax.fori_loop(0, CHEB_DEGREE, step, 0)
        q = lax.rem((p + 1) * CHEB_DEGREE, 2)

        def divide(x, inner):
            shape = (ROWS, COLUMN, STATES)
            value = jnp.where(row_in_slot(shape, 1) < ORDER, block[q, x, 0:ROWS], 0.0)
            high_part, low_part = split_two(value.reshape(ROWS * COLUMN, STATES))
            rows = pl.ds(pl.multiple_of(x * ROWS * COLUMN, ROWS * COLUMN), ROWS * COLUMN)
            split[rows, 0:STATES] = high_part
            split[rows, STATES : 2 * STATES] = low_part
            return inner

        lax.fori_loop(0, ROWS, divide, 0)
        products = dot_tn(split[:, 0:STATES], split[...])
        cross = products[:, STATES : 2 * STATES]
        partial[...] = products[:, 0:STATES] + cross + cross.T
        sum_everywhere(p)
        whole = gram_sum[p]
        work[:, 0:STATES] = whole
        diagonal = lax.broadcasted_iota(jnp.int32, (STATES, STATES), 0) == lax.broadcasted_iota(
            jnp.int32, (STATES, STATES), 1
        )
        work[:, STATES : 2 * STATES] = jnp.where(diagonal, 1.0, 0.0)
        factor_rows(work)
        inverse = work[:, STATES : 2 * STATES]
        inverse_out[...] = inverse
        gram_out[...] = whole

        @pl.when(p == 0)
        def _():
            pair = stacked_inverse(inverse)

            def turn(x, inner):
                value = block[q, x, 0:ROWS].reshape(ROWS * COLUMN, STATES)
                block[q, x, 0:ROWS] = times_inverse(value, pair).reshape(ROWS, COLUMN, STATES)
                return inner

            lax.fori_loop(0, ROWS, turn, 0)

        return carry

    lax.fori_loop(0, 2, one_pass, 0)
    store = pltpu.make_async_copy(block.at[0, 0:ROWS, 0:ROWS], filtered, start_sem)
    store.start()
    store.wait()


def stacked_inverse(inverse):
    high, low = split_two(inverse)
    return jnp.concatenate(
        [jnp.concatenate([high, high], axis=1), jnp.concatenate([low, low], axis=1)], axis=0
    )


def times_inverse(value, pair):
    high, low = split_two(value)
    both = dot_nt(jnp.concatenate([high, low], axis=1), pair)
    return both[:, 0:STATES] + both[:, STATES : 2 * STATES]


def states_kernel(filtered, inverse, out):
    value = filtered[...].reshape(ROWS * COLUMN, STATES)
    result = times_inverse(value, stacked_inverse(inverse[...])).reshape(ROWS, COLUMN, STATES)
    for h in range(COUNT_Z):
        out[0, :, h * ORDER : (h + 1) * ORDER, :] = result[:, h * SLOT : h * SLOT + ORDER, :]


def with_shared_rows(values):
    shape = values.shape
    cells = values.reshape(shape[:2] + (COUNT_Z, ORDER) + shape[3:])
    following = jnp.roll(cells[:, :, :, :1], -1, axis=2)
    cells = jnp.concatenate([cells, following, jnp.zeros_like(following)], axis=3)
    return cells.reshape(shape[:2] + (COLUMN,) + shape[3:])


def place_records(coarse_states, record_target, rows_x, rows_y, rows_z):
    per_device, coarse_count, state_count = coarse_states.shape
    size_x = lax.axis_size("dx")
    size_y = lax.axis_size("dy")
    capacity = per_device // 2
    interp_table = jnp.asarray(lagrange_table(ORDER, COARSE_ORDER), F32).astype(BF16)
    own_x = lax.axis_index("dx")
    own_y = lax.axis_index("dy")
    target = record_target // per_device
    local_cell = record_target % per_device
    step_x = (target // size_y - own_x) % size_x
    step_y = (target % size_y - own_y) % size_y
    bucket = 2 * step_x + step_y
    onehot = (bucket[:, None] == jnp.arange(4, dtype=jnp.int32)[None, :]).astype(jnp.int32)
    before = jnp.cumsum(onehot, axis=0) - onehot
    slot_rank = jnp.sum(before * onehot, axis=1)
    position = bucket * capacity + slot_rank
    payload = jnp.einsum(
        "on,kns->kos", interp_table, coarse_states, preferred_element_type=F32
    ).astype(BF16)
    record_rows = payload.shape[1]
    buffer = jnp.zeros((4 * capacity, record_rows, state_count), BF16).at[position].set(payload)
    buffer = buffer.reshape(4, capacity, record_rows, state_count)
    labels = (
        jnp.full((4 * capacity,), per_device, jnp.int32)
        .at[position]
        .set(local_cell)
        .reshape(4, capacity)
    )
    from_x, labels_x = shifted((buffer[2], labels[2]), "dx", 1)
    from_y, labels_y = shifted((buffer[1], labels[1]), "dy", 1)
    partway, partway_labels = shifted((buffer[3], labels[3]), "dx", 1)
    from_xy, labels_xy = shifted((partway, partway_labels), "dy", 1)
    arrived = jnp.concatenate([buffer[0], from_x, from_y, from_xy], axis=0)
    arrived_labels = jnp.concatenate([labels[0], labels_x, labels_y, labels_xy], axis=0)
    placed = (
        jnp.zeros((per_device + 1, record_rows, state_count), BF16)
        .at[arrived_labels]
        .set(arrived)[:per_device]
    )
    start_block = placed.reshape(2, 2, COUNT_Z, ORDER, ORDER, ORDER, state_count)
    return start_block.transpose(0, 3, 1, 4, 2, 5, 6).reshape(rows_x, rows_y, rows_z, state_count)


def local(coarse_states, record_target, cell_matrix, mass_scale, potential, filter_window):
    rows_x, rows_y, rows_z = mass_scale.shape
    size_x = lax.axis_size("dx")
    size_y = lax.axis_size("dy")
    node_total = float(rows_x * rows_y * rows_z * size_x * size_y)
    start_block = place_records(coarse_states, record_target, rows_x, rows_y, rows_z)
    start_block = with_shared_rows(start_block).astype(F32)
    mass = jnp.pad(
        with_shared_rows(mass_scale), ((0, 1), (0, 1), (0, 0)), constant_values=1.0
    )
    mass = jnp.broadcast_to(mass[..., None], mass.shape + (STATES,))
    pot = with_shared_rows(potential)
    pot = jnp.broadcast_to(pot[..., None], pot.shape + (STATES,))
    plane = POINTS * POINTS
    spread = jnp.pad(
        cell_matrix.reshape((POINTS,) * 6), ((0, 0), (0, 1), (0, 1), (0, 0), (0, 1), (0, 1))
    ).reshape(KDIM, KDIM)
    padded = (ROWS + 1, ROWS + 1, COLUMN, STATES)
    inside = (ROWS, ROWS, COLUMN, STATES)
    face = (ROWS, COLUMN, STATES)
    line = (COLUMN, STATES)
    share = STATES // size_y
    messages = 2 * size_y + size_x - 3
    vmem = pl.BlockSpec(memory_space=pltpu.VMEM)
    anywhere = pl.BlockSpec(memory_space=pl.ANY)
    filtered, inverse, gram_matrix = pl.pallas_call(
        functools.partial(filter_kernel, size_x, size_y, node_total),
        out_shape=(
            jax.ShapeDtypeStruct(inside, F32),
            jax.ShapeDtypeStruct((STATES, STATES), F32),
            jax.ShapeDtypeStruct((STATES, STATES), F32),
        ),
        in_specs=[pl.BlockSpec(memory_space=pltpu.SMEM), anywhere, vmem, vmem, vmem],
        out_specs=(anywhere, vmem, vmem),
        scratch_shapes=[
            pltpu.VMEM((2,) + padded, F32),
            pltpu.VMEM(padded, F32),
            pltpu.VMEM((KDIM, COUNT_Z * STATES), BF16),
            pltpu.VMEM(face, BF16),
            pltpu.VMEM(face, BF16),
            pltpu.VMEM(face, BF16),
            pltpu.VMEM(face, BF16),
            pltpu.VMEM(line, BF16),
            pltpu.VMEM(face, BF16),
            pltpu.VMEM(face, BF16),
            pltpu.VMEM(line, BF16),
            pltpu.VMEM(face, BF16),
            pltpu.VMEM(face, BF16),
            pltpu.VMEM(line, BF16),
            pltpu.VMEM((ROWS * ROWS * COLUMN, 2 * STATES), BF16),
            pltpu.VMEM((STATES, STATES), F32),
            pltpu.VMEM((2, size_y - 1, share, STATES), F32),
            pltpu.VMEM((2, size_x, share, STATES), F32),
            pltpu.VMEM((2, STATES, STATES), F32),
            pltpu.VMEM((STATES, 2 * STATES), F32),
            pltpu.SemaphoreType.DMA,
            pltpu.SemaphoreType.DMA((6,)),
            pltpu.SemaphoreType.DMA((6,)),
            pltpu.SemaphoreType.DMA((2, messages)),
            pltpu.SemaphoreType.DMA((2, messages)),
        ],
        compiler_params=pltpu.CompilerParams(
            collective_id=0, has_side_effects=True, vmem_limit_bytes=52 * 1024 * 1024
        ),
        cost_estimate=pl.CostEstimate(
            flops=6 * 4 * 2 * KDIM * KDIM * 512, bytes_accessed=10_000_000, transcendentals=0
        ),
        name="filter_twice",
    )(filter_window, start_block, mass, pot, spread)
    states = pl.pallas_call(
        states_kernel,
        out_shape=jax.ShapeDtypeStruct((rows_x, rows_y, rows_z, STATES), F32),
        grid=(rows_x,),
        in_specs=[
            pl.BlockSpec((1, ROWS, COLUMN, STATES), lambda x: (x, 0, 0, 0)),
            pl.BlockSpec((STATES, STATES), lambda x: (0, 0)),
        ],
        out_specs=pl.BlockSpec((1, ROWS, rows_z, STATES), lambda x: (x, 0, 0, 0)),
        name="orthonormal_states",
    )(filtered, inverse)
    return (states, gram_matrix)


def solution(mesh):
    in_specs = (
        P(("dx", "dy"), None, None),
        P(("dx", "dy")),
        P(),
        P("dx", "dy", None),
        P("dx", "dy", None),
        P(),
    )
    out_specs = (P("dx", "dy", None, None), P())
    return jax.shard_map(local, mesh=mesh, in_specs=in_specs, out_specs=out_specs, check_vma=False)
```

```python
import functools

import jax
import jax.numpy as jnp
import numpy as np
from jax import lax
from jax.experimental import pallas as pl
from jax.experimental.pallas import tpu as pltpu
from jax.sharding import PartitionSpec as P

ORDER = 6
COARSE_ORDER = 4
CHEB_DEGREE = 3
POINTS = ORDER + 1
COUNT_Z = 4
SLOT = 8
COLUMN = COUNT_Z * SLOT
ROWS = 12
STATES = 128
PAIRS = 4
KDIM = POINTS * SLOT * SLOT
CELLS = 16
CAPACITY = CELLS // 2
COARSE_ROWS = 128
MESH = pl.DeviceIdType.MESH
F32 = jnp.float32
BF16 = jnp.bfloat16


def node_points(degree_value):
    return -np.cos(np.pi * np.arange(degree_value + 1) / degree_value)


def lagrange_table(fine_degree, coarse_degree):
    targets = node_points(fine_degree)
    sources = node_points(coarse_degree)
    matrix = np.ones((fine_degree + 1, coarse_degree + 1))
    for p in range(coarse_degree + 1):
        for m in range(coarse_degree + 1):
            if m != p:
                matrix[:, p] = matrix[:, p] * (targets - sources[m]) / (sources[p] - sources[m])
    owned_rows = matrix[:fine_degree]
    first = owned_rows[:, None, None, :, None, None]
    second = owned_rows[None, :, None, None, :, None]
    third = owned_rows[None, None, :, None, None, :]
    product = first * second * third
    return product.reshape(fine_degree**3, (coarse_degree + 1) ** 3)


def row_in_slot(shape, axis):
    return lax.broadcasted_iota(jnp.int32, shape, axis) % SLOT


def dot_nn(a, b):
    return lax.dot_general(a, b, (((1,), (0,)), ((), ())), preferred_element_type=F32)


def dot_tn(a, b):
    return lax.dot_general(a, b, (((0,), (0,)), ((), ())), preferred_element_type=F32)


def dot_nt(a, b):
    return lax.dot_general(a, b, (((1,), (1,)), ((), ())), preferred_element_type=F32)


def split_two(value):
    high = value.astype(BF16)
    return high, (value - high.astype(F32)).astype(BF16)


def split_three(value):
    high = value.astype(BF16)
    rest = value - high.astype(F32)
    middle = rest.astype(BF16)
    return high, middle, (rest - middle.astype(F32)).astype(BF16)


def factor_rows(work):
    size = STATES
    sub = lax.broadcasted_iota(jnp.int32, (SLOT, size), 0)
    lane = lax.broadcasted_iota(jnp.int32, (SLOT, size), 1)

    def panel(j, carry):
        base = pl.multiple_of(j * SLOT, SLOT)
        left = work[pl.ds(base, SLOT), 0:size]
        right = work[pl.ds(base, SLOT), size : 2 * size]
        turned = pltpu.roll(left, lax.rem(size - base, size), 1)
        columns = [jnp.broadcast_to(turned[:, m : m + 1], (SLOT, size)) for m in range(SLOT)]
        for m in range(SLOT):
            pivot = jnp.broadcast_to(columns[m][m : m + 1, :], (SLOT, size))
            scale = lax.rsqrt(pivot)
            scale = scale * (1.5 - 0.5 * pivot * scale * scale)
            below = sub > m
            at = sub == m
            coef = columns[m] * scale
            row_left = jnp.broadcast_to(left[m : m + 1, :], (SLOT, size)) * scale
            row_right = jnp.broadcast_to(right[m : m + 1, :], (SLOT, size)) * scale
            for n in range(m + 1, SLOT):
                entry = jnp.broadcast_to(columns[n][m : m + 1, :], (SLOT, size)) * scale
                columns[n] = jnp.where(below, columns[n] - coef * entry, columns[n])
            left = jnp.where(below, left - coef * row_left, jnp.where(at, row_left, left))
            right = jnp.where(below, right - coef * row_right, jnp.where(at, row_right, right))
        work[pl.ds(base, SLOT), 0:size] = left
        work[pl.ds(base, SLOT), size : 2 * size] = right
        later = jnp.where(lane >= base + SLOT, left, 0.0)
        l1, l2, l3 = [v.astype(F32) for v in split_three(later)]
        both = jnp.concatenate([left, right], axis=1)
        b1, b2, b3 = [v.astype(F32) for v in split_three(both)]
        lhs = jnp.concatenate([l1, l1, l2, l1, l3, l2], axis=0).astype(BF16)
        rhs = jnp.concatenate([b1, b2, b1, b3, b1, b2], axis=0).astype(BF16)
        work[...] = work[...] - dot_tn(lhs, rhs)
        return carry

    lax.fori_loop(0, size // SLOT, panel, 0)


def filter_kernel(
    size_x,
    size_y,
    node_total,
    window,
    targets,
    target_tile,
    coarse,
    table,
    node_values,
    cell_matrix,
    states_out,
    gram_out,
    mass,
    pot,
    matrix,
    slots,
    arrived,
    target_in,
    target_list,
    block,
    total,
    rhs,
    send_x,
    send_y,
    take_x,
    take_y,
    take_c,
    back_x,
    back_y,
    back_c,
    got_x,
    got_y,
    got_c,
    split,
    partial,
    piece_in,
    ring_in,
    gram_sum,
    work,
    target_send,
    target_recv,
    list_sems,
    record_send,
    record_recv,
    send_sems,
    recv_sems,
    sum_send,
    sum_recv,
):
    me_x = lax.axis_index("dx")
    me_y = lax.axis_index("dy")

    def at(step_x, step_y):
        return (lax.rem(me_x + step_x + size_x, size_x), lax.rem(me_y + step_y + size_y, size_y))

    partners = [at(0, d) for d in range(1, size_y)] + [at(d, 0) for d in range(1, size_x)]
    partners += [at(1, 1), at(-1, -1)]
    barrier = pltpu.get_barrier_semaphore()
    for partner in partners:
        pl.semaphore_signal(barrier, inc=1, device_id=partner, device_id_type=MESH)
    steps = (None, (0, 1), (1, 0), (1, 1))
    buckets, ranks = [], []
    counts = [0, 0, 0, 0]
    for r in range(CELLS):
        device = targets[r] // CELLS
        step_x = lax.rem(device // size_y - me_x + size_x, size_x)
        step_y = lax.rem(lax.rem(device, size_y) - me_y + size_y, size_y)
        bucket = 2 * step_x + step_y
        rank = 0
        for index in range(4):
            rank = rank + jnp.where(bucket == index, counts[index], 0)
            counts[index] = counts[index] + jnp.where(bucket == index, 1, 0)
        buckets.append(bucket)
        ranks.append(bucket * CAPACITY + rank)

    def record_of(slot):
        found = 0
        for r in range(CELLS):
            found = found + jnp.where(ranks[r] == slot, r, 0)
        return jnp.minimum(jnp.maximum(found, 0), CELLS - 1)

    last = COARSE_ROWS - 16
    for index in range(3):
        slots[index, :, last:COARSE_ROWS] = jnp.zeros((CAPACITY, 16, STATES), BF16)
    arrived[0:CAPACITY, last:COARSE_ROWS] = jnp.zeros((CAPACITY, 16, STATES), BF16)
    coarse_count = coarse.shape[1]
    pl.semaphore_wait(barrier, len(partners))
    target_copies, record_copies = {}, {}
    for index in (3, 2, 1):
        target_copies[index] = pltpu.make_async_remote_copy(
            src_ref=target_tile,
            dst_ref=target_in.at[index - 1],
            send_sem=target_send.at[index - 1],
            recv_sem=target_recv.at[index - 1],
            device_id=at(*steps[index]),
            device_id_type=MESH,
        )
        target_copies[index].start()
    for index in (3, 2, 1):
        for k in range(CAPACITY):
            slots[index - 1, k, 0:coarse_count] = coarse[record_of(index * CAPACITY + k)]
        record_copies[index] = pltpu.make_async_remote_copy(
            src_ref=slots.at[index - 1],
            dst_ref=arrived.at[pl.ds(index * CAPACITY, CAPACITY)],
            send_sem=record_send.at[index - 1],
            recv_sem=record_recv.at[index - 1],
            device_id=at(*steps[index]),
            device_id_type=MESH,
        )
        record_copies[index].start()
    for k in range(CAPACITY):
        arrived[k, 0:coarse_count] = coarse[record_of(k)]

    place_nodes(node_values, mass, pot)
    spread_matrix(cell_matrix, matrix)
    block[1] = jnp.zeros(block.shape[1:], F32)
    total[...] = jnp.zeros(total.shape, F32)

    for index in (3, 2, 1):
        target_copies[index].wait()
    lists = [
        pltpu.make_async_copy(target_in.at[i], target_list.at[i], list_sems.at[i]) for i in range(3)
    ]
    for copy in lists:
        copy.start()
    for copy in lists:
        copy.wait()
    own = me_x * size_y + me_y
    places = [0] * CELLS
    for index in range(4):
        seen = 0
        for r in range(CELLS):
            target = targets[r] if index == 0 else target_list[index - 1, 0, r]
            hit = target // CELLS == own
            cell = jnp.where(hit, lax.rem(target, CELLS), -1)
            slot = index * CAPACITY + seen
            for g in range(CELLS):
                places[g] = places[g] + jnp.where(cell == g, slot, 0)
            seen = seen + jnp.where(hit, 1, 0)
    places = [jnp.minimum(jnp.maximum(p, 0), 4 * CAPACITY - 1) for p in places]
    for index in (3, 2, 1):
        record_copies[index].wait()
    slot_row = row_in_slot((COLUMN, STATES), 0)
    for e in range(2):
        for f in range(2):
            for h in range(COUNT_Z):
                rhs[0:COARSE_ROWS, h * STATES : (h + 1) * STATES] = arrived[
                    places[(2 * e + f) * COUNT_Z + h]
                ]
            fine = dot_nn(table[...], rhs[0:COARSE_ROWS, :]).astype(BF16).astype(F32)
            for a in range(ORDER):
                for b in range(ORDER):
                    first = (a * ORDER + b) * SLOT
                    lines = [
                        fine[first : first + SLOT, h * STATES : (h + 1) * STATES]
                        for h in range(COUNT_Z)
                    ]
                    lines = jnp.concatenate(lines, axis=0)
                    again = pltpu.roll(lines, COLUMN - SLOT + ORDER, 0)
                    block[0, e * ORDER + a, f * ORDER + b] = jnp.where(
                        slot_row == ORDER, again, lines
                    )

    low = window[0]
    high = window[1]
    center = (low + high) / 2.0
    radius = (high - low) / 2.0

    def remote(index, src, dst, step_x, step_y):
        return pltpu.make_async_remote_copy(
            src_ref=src,
            dst_ref=dst,
            send_sem=send_sems.at[index],
            recv_sem=recv_sems.at[index],
            device_id=at(step_x, step_y),
            device_id_type=MESH,
        )

    def column(q, e, f):
        base_x = e * ORDER
        base_y = f * ORDER
        for a in range(POINTS):
            for i in range(PAIRS):
                for h in range(COUNT_Z):
                    parts = []
                    for b in (2 * i, 2 * i + 1):
                        if b < POINTS:
                            rows = pl.ds(h * SLOT, SLOT)
                            parts.append(
                                mass[base_x + a, base_y + b, rows]
                                * block[q, base_x + a, base_y + b, rows]
                            )
                        else:
                            parts.append(jnp.zeros((SLOT, STATES), F32))
                    rhs[
                        pl.ds((a * PAIRS + i) * 2 * SLOT, 2 * SLOT), pl.ds(h * STATES, STATES)
                    ] = jnp.concatenate(parts, axis=0).astype(BF16)
        product = dot_nn(matrix[...], rhs[...])
        for a in range(POINTS):
            for b in range(POINTS):
                first = (a * SLOT + b) * SLOT
                for h in range(COUNT_Z):
                    rows = pl.ds(h * SLOT, SLOT)
                    total[base_x + a, base_y + b, rows] += product[
                        first : first + SLOT, h * STATES : (h + 1) * STATES
                    ]

    def finish(q, x, y, count, alpha, beta):
        shape = (count, COLUMN, STATES)
        slot_row = row_in_slot(shape, 1)
        ys = pl.ds(y, count)
        raw = total[x, ys]
        total[x, ys] = jnp.zeros(shape, F32)
        summed = raw + jnp.where(slot_row == 0, pltpu.roll(raw, SLOT - ORDER, 1), 0.0)
        again = pltpu.roll(summed, COLUMN - SLOT + ORDER, 1)
        full = jnp.where(slot_row < ORDER, summed, jnp.where(slot_row == ORDER, again, 0.0))
        value = block[q, x, ys]
        result = mass[x, ys] * full + (pot[x, ys] - center) * value
        block[1 - q, x, ys] = alpha * result - beta * block[1 - q, x, ys]

    def one_apply(k, p):
        q = lax.rem(p * CHEB_DEGREE + k, 2)
        first = k == 0
        alpha = jnp.where(first, 1.0, 2.0) / radius
        beta = jnp.where(first, 0.0, 1.0)
        send_x[...] = (mass[0, 0:ROWS] * block[q, 0, 0:ROWS]).astype(BF16)
        send_y[...] = (mass[0:ROWS, 0] * block[q, 0:ROWS, 0]).astype(BF16)
        values = [
            remote(0, send_x, take_x, -1, 0),
            remote(1, send_y, take_y, 0, -1),
            remote(2, send_x.at[0], take_c, -1, -1),
        ]
        for copy in values:
            copy.start()
        column(q, 0, 0)
        for copy in values:
            copy.wait()
        block[q, ROWS, 0:ROWS] = take_x[...].astype(F32)
        block[q, 0:ROWS, ROWS] = take_y[...].astype(F32)
        block[q, ROWS, ROWS] = take_c[...].astype(F32)

        def others(index, carry):
            column(q, index // 2, lax.rem(index, 2))
            return carry

        lax.fori_loop(1, 4, others, 0)
        back_x[...] = total[ROWS, 0:ROWS].astype(BF16)
        back_y[...] = total[0:ROWS, ROWS].astype(BF16)
        back_c[...] = total[ROWS, ROWS].astype(BF16)
        sums = [
            remote(3, back_x, got_x, 1, 0),
            remote(4, back_y, got_y, 0, 1),
            remote(5, back_c, got_c, 1, 1),
        ]
        for copy in sums:
            copy.start()
        total[ROWS] = jnp.zeros(total.shape[1:], F32)
        total[0:ROWS, ROWS] = jnp.zeros((ROWS, COLUMN, STATES), F32)

        def interior(x, carry):
            finish(q, x, 1, ROWS - 1, alpha, beta)
            return carry

        lax.fori_loop(1, ROWS, interior, 0)
        for copy in sums:
            copy.wait()
        total[0, 0:ROWS] += got_x[...].astype(F32)
        total[0:ROWS, 0] += got_y[...].astype(F32)
        total[0, 0] += got_c[...].astype(F32)
        finish(q, 0, 0, ROWS, alpha, beta)

        def edge(x, carry):
            finish(q, x, 0, 1, alpha, beta)
            return carry

        lax.fori_loop(1, ROWS, edge, 0)

    def sum_everywhere(p):
        share = STATES // size_y

        def move(index, src, dst, device):
            return pltpu.make_async_remote_copy(
                src_ref=src,
                dst_ref=dst,
                send_sem=sum_send.at[p, index],
                recv_sem=sum_recv.at[p, index],
                device_id=device,
                device_id_type=MESH,
            )

        def rows_of(owner):
            return pl.ds(pl.multiple_of(owner * share, SLOT), share)

        mine = rows_of(me_y)
        copies = []
        for d in range(1, size_y):
            device = at(0, d)
            copies.append(
                move(d - 1, partial.at[rows_of(device[1])], piece_in.at[p, d - 1], device)
            )
        for copy in copies:
            copy.start()
        for copy in copies:
            copy.wait()
        piece = partial[mine, :]
        for d in range(1, size_y):
            piece = piece + piece_in[p, d - 1]
        ring_in[p, me_x] = piece
        copies = []
        for d in range(1, size_x):
            copies.append(
                move(size_y + d - 2, ring_in.at[p, me_x], ring_in.at[p, me_x], at(d, 0))
            )
        for copy in copies:
            copy.start()
        for copy in copies:
            copy.wait()
        piece = ring_in[p, 0]
        for d in range(1, size_x):
            piece = piece + ring_in[p, d]
        gram_sum[p, mine] = piece / node_total
        copies = []
        for d in range(1, size_y):
            copies.append(
                move(
                    size_y + size_x + d - 3, gram_sum.at[p, mine], gram_sum.at[p, mine], at(0, d)
                )
            )
        for copy in copies:
            copy.start()
        for copy in copies:
            copy.wait()

    def one_pass(p, carry):
        def step(k, inner):
            one_apply(k, p)
            return inner

        lax.fori_loop(0, CHEB_DEGREE, step, 0)
        q = lax.rem((p + 1) * CHEB_DEGREE, 2)

        def divide(x, inner):
            shape = (ROWS, COLUMN, STATES)
            value = jnp.where(row_in_slot(shape, 1) < ORDER, block[q, x, 0:ROWS], 0.0)
            high_part, low_part = split_two(value.reshape(ROWS * COLUMN, STATES))
            rows = pl.ds(pl.multiple_of(x * ROWS * COLUMN, ROWS * COLUMN), ROWS * COLUMN)
            split[rows, 0:STATES] = high_part
            split[rows, STATES : 2 * STATES] = low_part
            return inner

        lax.fori_loop(0, ROWS, divide, 0)
        products = dot_tn(split[:, 0:STATES], split[...])
        cross = products[:, STATES : 2 * STATES]
        partial[...] = products[:, 0:STATES] + cross + cross.T
        sum_everywhere(p)
        whole = gram_sum[p]
        work[:, 0:STATES] = whole
        diagonal = lax.broadcasted_iota(jnp.int32, (STATES, STATES), 0) == lax.broadcasted_iota(
            jnp.int32, (STATES, STATES), 1
        )
        work[:, STATES : 2 * STATES] = jnp.where(diagonal, 1.0, 0.0)
        factor_rows(work)
        inverse = work[:, STATES : 2 * STATES]
        gram_out[...] = whole
        pair = stacked_inverse(inverse)

        def turned(x):
            value = block[q, x, 0:ROWS].reshape(ROWS * COLUMN, STATES)
            return times_inverse(value, pair).reshape(ROWS, COLUMN, STATES)

        @pl.when(p == 0)
        def _():
            def turn(x, inner):
                block[q, x, 0:ROWS] = turned(x)
                return inner

            lax.fori_loop(0, ROWS, turn, 0)

        @pl.when(p == 1)
        def _():
            def turn(x, inner):
                result = turned(x)
                for h in range(COUNT_Z):
                    states_out[x, :, h * ORDER : (h + 1) * ORDER, :] = result[
                        :, h * SLOT : h * SLOT + ORDER, :
                    ]
                return inner

            lax.fori_loop(0, ROWS, turn, 0)

        return carry

    lax.fori_loop(0, 2, one_pass, 0)


def stacked_inverse(inverse):
    high, low = split_two(inverse)
    return jnp.concatenate(
        [jnp.concatenate([high, high], axis=1), jnp.concatenate([low, low], axis=1)], axis=0
    )


def times_inverse(value, pair):
    high, low = split_two(value)
    both = dot_nt(jnp.concatenate([high, low], axis=1), pair)
    return both[:, 0:STATES] + both[:, STATES : 2 * STATES]


def place_nodes(node_values, mass, pot):
    count_z = COUNT_Z * ORDER
    width = 3 * count_z
    row = lax.broadcasted_iota(jnp.int32, (COLUMN, width), 0)
    lane = lax.broadcasted_iota(jnp.int32, (COLUMN, width), 1)
    within = row % SLOT
    source = lax.rem((row // SLOT) * ORDER + within, count_z)
    pick = jnp.where((lax.rem(lane, count_z) == source) & (within < POINTS), 1.0, 0.0)
    ones = jnp.ones((width, STATES), BF16)
    third = lax.broadcasted_iota(jnp.int32, (2 * ROWS, width), 1) // count_z

    def one(x, carry):
        for base, out in ((0, mass), (ROWS * ROWS, pot)):
            start = pl.multiple_of(base + 2 * ROWS * x, SLOT)
            values = node_values[pl.ds(start, 2 * ROWS), :]
            high, middle, low = [v.astype(F32) for v in split_three(values)]
            parts = jnp.where(third == 0, high, jnp.where(third == 1, middle, low))
            spread = [
                jnp.broadcast_to(parts[y : y + 1, :], (COLUMN, width)) * pick
                for y in range(2 * ROWS)
            ]
            lines = dot_nn(jnp.concatenate(spread, axis=0).astype(BF16), ones)
            lines = lines.reshape(2, ROWS, COLUMN, STATES)
            out[2 * x, 0:ROWS] = lines[0]
            out[2 * x + 1, 0:ROWS] = lines[1]
        return carry

    lax.fori_loop(0, ROWS // 2, one, 0)
    mass[ROWS] = jnp.ones(mass.shape[1:], F32)
    mass[0:ROWS, ROWS] = jnp.ones((ROWS, COLUMN, STATES), F32)


def spread_matrix(cell_matrix, matrix):
    nodes = POINTS**3
    row = lax.broadcasted_iota(jnp.int32, (KDIM, nodes), 0)
    col = lax.broadcasted_iota(jnp.int32, (KDIM, nodes), 1)
    b = (row // SLOT) % SLOT
    c = row % SLOT
    source = (row // (SLOT * SLOT)) * POINTS * POINTS + b * POINTS + c
    pick = jnp.where((col == source) & (b < POINTS) & (c < POINTS), 1.0, 0.0).astype(BF16)
    half = dot_nn(pick, cell_matrix[...]).astype(BF16)
    matrix[...] = dot_nt(half, pick).astype(BF16)


def padded_table():
    table = lagrange_table(ORDER, COARSE_ORDER).astype(np.float32)
    table = table.reshape(ORDER * ORDER, ORDER, -1)
    table = np.pad(table, ((0, 0), (0, SLOT - ORDER), (0, COARSE_ROWS - table.shape[-1])))
    return jnp.asarray(table.reshape(-1, COARSE_ROWS), F32).astype(BF16)


def local(coarse_states, record_target, cell_matrix, mass_scale, potential, filter_window):
    rows_x, rows_y, rows_z = mass_scale.shape
    size_x = lax.axis_size("dx")
    size_y = lax.axis_size("dy")
    node_total = float(rows_x * rows_y * rows_z * size_x * size_y)
    lines = [v.reshape(rows_x * rows_y, rows_z) for v in (mass_scale, potential)]
    node_values = jnp.concatenate(lines, axis=0)
    node_values = jnp.concatenate([node_values] * 3, axis=1)
    target_tile = jnp.pad(record_target[None, :], ((0, SLOT - 1), (0, STATES - CELLS)))
    padded = (ROWS + 1, ROWS + 1, COLUMN, STATES)
    inside = (ROWS, ROWS, COLUMN, STATES)
    face = (ROWS, COLUMN, STATES)
    line = (COLUMN, STATES)
    share = STATES // size_y
    messages = 2 * size_y + size_x - 3
    vmem = pl.BlockSpec(memory_space=pltpu.VMEM)
    return pl.pallas_call(
        functools.partial(filter_kernel, size_x, size_y, node_total),
        out_shape=(
            jax.ShapeDtypeStruct((rows_x, rows_y, rows_z, STATES), F32),
            jax.ShapeDtypeStruct((STATES, STATES), F32),
        ),
        in_specs=[pl.BlockSpec(memory_space=pltpu.SMEM)] * 2 + [vmem] * 5,
        out_specs=(vmem, vmem),
        scratch_shapes=[
            pltpu.VMEM(padded, F32),
            pltpu.VMEM(inside, F32),
            pltpu.VMEM((KDIM, KDIM), BF16),
            pltpu.VMEM((3, CAPACITY, COARSE_ROWS, STATES), BF16),
            pltpu.VMEM((4 * CAPACITY, COARSE_ROWS, STATES), BF16),
            pltpu.VMEM((3, SLOT, STATES), jnp.int32),
            pltpu.SMEM((3, SLOT, STATES), jnp.int32),
            pltpu.VMEM((2,) + padded, F32),
            pltpu.VMEM(padded, F32),
            pltpu.VMEM((KDIM, COUNT_Z * STATES), BF16),
            pltpu.VMEM(face, BF16),
            pltpu.VMEM(face, BF16),
            pltpu.VMEM(face, BF16),
            pltpu.VMEM(face, BF16),
            pltpu.VMEM(line, BF16),
            pltpu.VMEM(face, BF16),
            pltpu.VMEM(face, BF16),
            pltpu.VMEM(line, BF16),
            pltpu.VMEM(face, BF16),
            pltpu.VMEM(face, BF16),
            pltpu.VMEM(line, BF16),
            pltpu.VMEM((ROWS * ROWS * COLUMN, 2 * STATES), BF16),
            pltpu.VMEM((STATES, STATES), F32),
            pltpu.VMEM((2, size_y - 1, share, STATES), F32),
            pltpu.VMEM((2, size_x, share, STATES), F32),
            pltpu.VMEM((2, STATES, STATES), F32),
            pltpu.VMEM((STATES, 2 * STATES), F32),
            pltpu.SemaphoreType.DMA((3,)),
            pltpu.SemaphoreType.DMA((3,)),
            pltpu.SemaphoreType.DMA((3,)),
            pltpu.SemaphoreType.DMA((3,)),
            pltpu.SemaphoreType.DMA((3,)),
            pltpu.SemaphoreType.DMA((6,)),
            pltpu.SemaphoreType.DMA((6,)),
            pltpu.SemaphoreType.DMA((2, messages)),
            pltpu.SemaphoreType.DMA((2, messages)),
        ],
        compiler_params=pltpu.CompilerParams(
            collective_id=0, has_side_effects=True, vmem_limit_bytes=52 * 1024 * 1024
        ),
        cost_estimate=pl.CostEstimate(
            flops=6 * 4 * 2 * KDIM * KDIM * 512, bytes_accessed=10_000_000, transcendentals=0
        ),
        name="filter_twice",
    )(filter_window, record_target, target_tile, coarse_states, padded_table(), node_values, cell_matrix)


def solution(mesh):
    in_specs = (
        P(("dx", "dy"), None, None),
        P(("dx", "dy")),
        P(),
        P("dx", "dy", None),
        P("dx", "dy", None),
        P(),
    )
    out_specs = (P("dx", "dy", None, None), P())
    return jax.shard_map(local, mesh=mesh, in_specs=in_specs, out_specs=out_specs, check_vma=False)
```

```python
import functools

import jax
import jax.numpy as jnp
import numpy as np
from jax import lax
from jax.experimental import pallas as pl
from jax.experimental.pallas import tpu as pltpu
from jax.sharding import PartitionSpec as P

ORDER = 6
COARSE_ORDER = 4
CHEB_DEGREE = 3
POINTS = ORDER + 1
COUNT_Z = 4
SLOT = 8
COLUMN = COUNT_Z * SLOT
ROWS = 12
STATES = 128
PAIRS = 4
KDIM = POINTS * SLOT * SLOT
FACE = SLOT * SLOT
CELLS = 16
CAPACITY = CELLS // 2
COARSE_ROWS = 128
MESH = pl.DeviceIdType.MESH
F32 = jnp.float32
BF16 = jnp.bfloat16


def node_points(degree_value):
    return -np.cos(np.pi * np.arange(degree_value + 1) / degree_value)


def lagrange_table(fine_degree, coarse_degree):
    targets = node_points(fine_degree)
    sources = node_points(coarse_degree)
    matrix = np.ones((fine_degree + 1, coarse_degree + 1))
    for p in range(coarse_degree + 1):
        for m in range(coarse_degree + 1):
            if m != p:
                matrix[:, p] = matrix[:, p] * (targets - sources[m]) / (sources[p] - sources[m])
    owned_rows = matrix[:fine_degree]
    first = owned_rows[:, None, None, :, None, None]
    second = owned_rows[None, :, None, None, :, None]
    third = owned_rows[None, None, :, None, None, :]
    product = first * second * third
    return product.reshape(fine_degree**3, (coarse_degree + 1) ** 3)


def row_in_slot(shape, axis):
    return lax.broadcasted_iota(jnp.int32, shape, axis) % SLOT


def dot_nn(a, b):
    return lax.dot_general(a, b, (((1,), (0,)), ((), ())), preferred_element_type=F32)


def dot_tn(a, b):
    return lax.dot_general(a, b, (((0,), (0,)), ((), ())), preferred_element_type=F32)


def dot_nt(a, b):
    return lax.dot_general(a, b, (((1,), (1,)), ((), ())), preferred_element_type=F32)


def split_two(value):
    high = value.astype(BF16)
    return high, (value - high.astype(F32)).astype(BF16)


def split_three(value):
    high = value.astype(BF16)
    rest = value - high.astype(F32)
    middle = rest.astype(BF16)
    return high, middle, (rest - middle.astype(F32)).astype(BF16)


def factor_rows(work):
    size = STATES
    sub = lax.broadcasted_iota(jnp.int32, (SLOT, size), 0)
    lane = lax.broadcasted_iota(jnp.int32, (SLOT, size), 1)

    def panel(j, carry):
        base = pl.multiple_of(j * SLOT, SLOT)
        left = work[pl.ds(base, SLOT), 0:size]
        right = work[pl.ds(base, SLOT), size : 2 * size]
        turned = pltpu.roll(left, lax.rem(size - base, size), 1)
        columns = [jnp.broadcast_to(turned[:, m : m + 1], (SLOT, size)) for m in range(SLOT)]
        for m in range(SLOT):
            pivot = jnp.broadcast_to(columns[m][m : m + 1, :], (SLOT, size))
            scale = lax.rsqrt(pivot)
            scale = scale * (1.5 - 0.5 * pivot * scale * scale)
            below = sub > m
            at = sub == m
            coef = columns[m] * scale
            row_left = jnp.broadcast_to(left[m : m + 1, :], (SLOT, size)) * scale
            row_right = jnp.broadcast_to(right[m : m + 1, :], (SLOT, size)) * scale
            for n in range(m + 1, SLOT):
                entry = jnp.broadcast_to(columns[n][m : m + 1, :], (SLOT, size)) * scale
                columns[n] = jnp.where(below, columns[n] - coef * entry, columns[n])
            left = jnp.where(below, left - coef * row_left, jnp.where(at, row_left, left))
            right = jnp.where(below, right - coef * row_right, jnp.where(at, row_right, right))
        work[pl.ds(base, SLOT), 0:size] = left
        work[pl.ds(base, SLOT), size : 2 * size] = right
        later = jnp.where(lane >= base + SLOT, left, 0.0)
        l1, l2, l3 = [v.astype(F32) for v in split_three(later)]
        both = jnp.concatenate([left, right], axis=1)
        b1, b2, b3 = [v.astype(F32) for v in split_three(both)]
        lhs = jnp.concatenate([l1, l1, l2, l1, l3, l2], axis=0).astype(BF16)
        rhs = jnp.concatenate([b1, b2, b1, b3, b1, b2], axis=0).astype(BF16)
        work[...] = work[...] - dot_tn(lhs, rhs)
        return carry

    lax.fori_loop(0, size // SLOT, panel, 0)


def filter_kernel(
    size_x,
    size_y,
    node_total,
    window,
    targets,
    target_tile,
    coarse,
    table,
    node_values,
    cell_matrix,
    states_out,
    gram_out,
    mass,
    pot,
    matrix,
    from_x,
    from_y,
    from_xy,
    slots,
    arrived,
    target_in,
    target_list,
    block,
    total,
    rhs,
    rhs_taken,
    send_x,
    send_y,
    take_x,
    take_y,
    back_x,
    back_y,
    back_c,
    got_x,
    got_y,
    got_c,
    split,
    partial,
    piece_in,
    ring_in,
    gram_sum,
    work,
    target_send,
    target_recv,
    list_sems,
    record_send,
    record_recv,
    send_sems,
    recv_sems,
    sum_send,
    sum_recv,
):
    me_x = lax.axis_index("dx")
    me_y = lax.axis_index("dy")

    def at(step_x, step_y):
        return (lax.rem(me_x + step_x + size_x, size_x), lax.rem(me_y + step_y + size_y, size_y))

    partners = [at(0, d) for d in range(1, size_y)] + [at(d, 0) for d in range(1, size_x)]
    partners += [at(1, 1), at(-1, -1), at(1, -1), at(-1, 1)]
    barrier = pltpu.get_barrier_semaphore()
    for partner in partners:
        pl.semaphore_signal(barrier, inc=1, device_id=partner, device_id_type=MESH)
    steps = (None, (0, 1), (1, 0), (1, 1))
    buckets, ranks = [], []
    counts = [0, 0, 0, 0]
    for r in range(CELLS):
        device = targets[r] // CELLS
        step_x = lax.rem(device // size_y - me_x + size_x, size_x)
        step_y = lax.rem(lax.rem(device, size_y) - me_y + size_y, size_y)
        bucket = 2 * step_x + step_y
        rank = 0
        for index in range(4):
            rank = rank + jnp.where(bucket == index, counts[index], 0)
            counts[index] = counts[index] + jnp.where(bucket == index, 1, 0)
        buckets.append(bucket)
        ranks.append(bucket * CAPACITY + rank)

    def record_of(slot):
        found = 0
        for r in range(CELLS):
            found = found + jnp.where(ranks[r] == slot, r, 0)
        return jnp.minimum(jnp.maximum(found, 0), CELLS - 1)

    last = COARSE_ROWS - 16
    for index in range(3):
        slots[index, :, last:COARSE_ROWS] = jnp.zeros((CAPACITY, 16, STATES), BF16)
    arrived[0:CAPACITY, last:COARSE_ROWS] = jnp.zeros((CAPACITY, 16, STATES), BF16)
    coarse_count = coarse.shape[1]
    pl.semaphore_wait(barrier, len(partners))
    target_copies, record_copies = {}, {}
    for index in (3, 2, 1):
        target_copies[index] = pltpu.make_async_remote_copy(
            src_ref=target_tile,
            dst_ref=target_in.at[index - 1],
            send_sem=target_send.at[index - 1],
            recv_sem=target_recv.at[index - 1],
            device_id=at(*steps[index]),
            device_id_type=MESH,
        )
        target_copies[index].start()
    for index in (3, 2, 1):
        for k in range(CAPACITY):
            slots[index - 1, k, 0:coarse_count] = coarse[record_of(index * CAPACITY + k)]
        record_copies[index] = pltpu.make_async_remote_copy(
            src_ref=slots.at[index - 1],
            dst_ref=arrived.at[pl.ds(index * CAPACITY, CAPACITY)],
            send_sem=record_send.at[index - 1],
            recv_sem=record_recv.at[index - 1],
            device_id=at(*steps[index]),
            device_id_type=MESH,
        )
        record_copies[index].start()
    for k in range(CAPACITY):
        arrived[k, 0:coarse_count] = coarse[record_of(k)]

    place_nodes(node_values, mass, pot)
    spread_matrix(cell_matrix, matrix, from_x, from_y, from_xy)
    block[1] = jnp.zeros(block.shape[1:], F32)

    for index in (3, 2, 1):
        target_copies[index].wait()
    lists = [
        pltpu.make_async_copy(target_in.at[i], target_list.at[i], list_sems.at[i]) for i in range(3)
    ]
    for copy in lists:
        copy.start()
    for copy in lists:
        copy.wait()
    own = me_x * size_y + me_y
    places = [0] * CELLS
    for index in range(4):
        seen = 0
        for r in range(CELLS):
            target = targets[r] if index == 0 else target_list[index - 1, 0, r]
            hit = target // CELLS == own
            cell = jnp.where(hit, lax.rem(target, CELLS), -1)
            slot = index * CAPACITY + seen
            for g in range(CELLS):
                places[g] = places[g] + jnp.where(cell == g, slot, 0)
            seen = seen + jnp.where(hit, 1, 0)
    places = [jnp.minimum(jnp.maximum(p, 0), 4 * CAPACITY - 1) for p in places]
    for index in (3, 2, 1):
        record_copies[index].wait()
    slot_row = row_in_slot((COLUMN, STATES), 0)
    for e in range(2):
        for f in range(2):
            for h in range(COUNT_Z):
                rhs[0:COARSE_ROWS, h * STATES : (h + 1) * STATES] = arrived[
                    places[(2 * e + f) * COUNT_Z + h]
                ]
            fine = dot_nn(table[...], rhs[0:COARSE_ROWS, :]).astype(BF16).astype(F32)
            for a in range(ORDER):
                for b in range(ORDER):
                    first = (a * ORDER + b) * SLOT
                    lines = [
                        fine[first : first + SLOT, h * STATES : (h + 1) * STATES]
                        for h in range(COUNT_Z)
                    ]
                    lines = jnp.concatenate(lines, axis=0)
                    again = pltpu.roll(lines, COLUMN - SLOT + ORDER, 0)
                    block[0, e * ORDER + a, f * ORDER + b] = jnp.where(
                        slot_row == ORDER, again, lines
                    )

    low = window[0]
    high = window[1]
    center = (low + high) / 2.0
    radius = (high - low) / 2.0

    def remote(turn, index, src, dst, step_x, step_y):
        return pltpu.make_async_remote_copy(
            src_ref=src,
            dst_ref=dst,
            send_sem=send_sems.at[turn, index],
            recv_sem=recv_sems.at[turn, index],
            device_id=at(step_x, step_y),
            device_id_type=MESH,
        )

    zeros = jnp.zeros((SLOT, STATES), F32)

    def pack(first, second):
        return jnp.concatenate([first, second], axis=0).astype(BF16)

    def add_product(product, e, f, points_x, points_y, written):
        for a in range(points_x):
            for b in range(points_y):
                first = (a * SLOT + b) * SLOT
                x, y = e * ORDER + a, f * ORDER + b
                for h in range(COUNT_Z):
                    rows = slice(h * SLOT, (h + 1) * SLOT)
                    part = product[first : first + SLOT, h * STATES : (h + 1) * STATES]
                    if (x, y) in written:
                        part = part + total[x, y, rows]
                    total[x, y, rows] = part
                written.add((x, y))

    def column(q, e, f, written):
        points_x = POINTS if e == 0 else ORDER
        for a in range(points_x):
            x = e * ORDER + a
            for h in range(COUNT_Z):
                rows = slice(h * SLOT, (h + 1) * SLOT)
                chunks = []
                for b in range(POINTS):
                    y = f * ORDER + b
                    own = y < ROWS
                    chunks.append(mass[x, y, rows] * block[q, x, y, rows] if own else zeros)
                chunks.append(chunks[0] if f == 0 else zeros)
                for i in range(PAIRS):
                    tile = pack(chunks[2 * i], chunks[2 * i + 1])
                    copies = [a, POINTS] if (a == 0 and e == 0) else [a]
                    for place in copies:
                        first = (place * PAIRS + i) * 2 * SLOT
                        rhs[first : first + 2 * SLOT, h * STATES : (h + 1) * STATES] = tile
        depth = FACE * (SLOT if e == 0 else ORDER)
        product = dot_nn(matrix[:, 0:depth], rhs[0:depth, :])
        add_product(product, e, f, POINTS, POINTS, written)

    def taken_column(e, f, factor, upper, lower, points_x, points_y, written):
        for base, lines in ((0, upper), (FACE, lower)):
            values = [line.astype(F32) for line in lines]
            for h in range(COUNT_Z):
                rows = slice(h * SLOT, (h + 1) * SLOT)
                chunks = [value[rows] for value in values]
                chunks += [zeros] * (SLOT - len(chunks))
                for i in range(PAIRS):
                    first = base + i * 2 * SLOT
                    rhs_taken[first : first + 2 * SLOT, h * STATES : (h + 1) * STATES] = pack(
                        chunks[2 * i], chunks[2 * i + 1]
                    )
        add_product(dot_nn(factor[...], rhs_taken[...]), e, f, points_x, points_y, written)

    def finish(q, x, y, count, alpha, beta):
        shape = (count, COLUMN, STATES)
        slot_row = row_in_slot(shape, 1)
        ys = pl.ds(y, count)
        raw = total[x, ys]
        summed = raw + jnp.where(slot_row == 0, pltpu.roll(raw, SLOT - ORDER, 1), 0.0)
        again = pltpu.roll(summed, COLUMN - SLOT + ORDER, 1)
        full = jnp.where(slot_row < ORDER, summed, jnp.where(slot_row == ORDER, again, 0.0))
        value = block[q, x, ys]
        result = mass[x, ys] * full + (pot[x, ys] - center) * value
        block[1 - q, x, ys] = alpha * result - beta * block[1 - q, x, ys]

    def one_apply(k, p):
        q = lax.rem(p * CHEB_DEGREE + k, 2)
        first = k == 0
        alpha = jnp.where(first, 1.0, 2.0) / radius
        beta = jnp.where(first, 0.0, 1.0)
        send_x[...] = (mass[0, 0:ROWS] * block[q, 0, 0:ROWS]).astype(BF16)
        send_y[...] = (mass[0:ROWS, 0] * block[q, 0:ROWS, 0]).astype(BF16)
        half = pl.ds(ORDER, ORDER)
        values = [
            remote(q, 0, send_x, take_x.at[q, pl.ds(ORDER, ROWS)], -1, 0),
            remote(q, 1, send_y, take_y.at[q, pl.ds(ORDER, ROWS)], 0, -1),
            remote(q, 2, send_x.at[half], take_x.at[q, pl.ds(0, ORDER)], -1, 1),
            remote(q, 3, send_y.at[half], take_y.at[q, pl.ds(0, ORDER)], 1, -1),
            remote(q, 4, send_x.at[pl.ds(0, 1)], take_x.at[q, pl.ds(ORDER + ROWS, 1)], -1, -1),
        ]
        for copy in values:
            copy.start()
        written = set()
        column(q, 1, 1, written)
        column(q, 0, 1, written)
        column(q, 1, 0, written)
        back_x[...] = total[ROWS, 0:ROWS].astype(BF16)
        back_y[...] = total[0:ROWS, ROWS].astype(BF16)
        back_c[...] = total[ROWS, ROWS].astype(BF16)
        sums = [
            remote(q, 5, back_x, got_x.at[q], 1, 0),
            remote(q, 6, back_y, got_y.at[q], 0, 1),
            remote(q, 7, back_c, got_c.at[q], 1, 1),
        ]
        for copy in sums:
            copy.start()
        column(q, 0, 0, written)
        for copy in values:
            copy.wait()
        along_x = [take_x[q, line] for line in range(2 * ORDER + POINTS)]
        along_y = [take_y[q, line] for line in range(3 * ORDER)]
        last = 2 * ORDER
        taken_column(
            1, 1, from_xy, along_x[last:], along_y[last:], ORDER, ORDER, written
        )
        taken_column(
            1, 0, from_x, along_x[ORDER : last + 1], along_x[0:POINTS], ORDER, POINTS, written
        )
        taken_column(
            0, 1, from_y, along_y[ORDER : last + 1], along_y[0:POINTS], POINTS, ORDER, written
        )

        def interior(x, carry):
            finish(q, x, 1, ROWS - 1, alpha, beta)
            return carry

        lax.fori_loop(1, ROWS, interior, 0)
        for copy in sums:
            copy.wait()
        total[0, 0:ROWS] += got_x[q].astype(F32)
        total[0:ROWS, 0] += got_y[q].astype(F32)
        total[0, 0] += got_c[q].astype(F32)
        finish(q, 0, 0, ROWS, alpha, beta)

        def edge(x, carry):
            finish(q, x, 0, 1, alpha, beta)
            return carry

        lax.fori_loop(1, ROWS, edge, 0)

    def sum_everywhere(p):
        share = STATES // size_y

        def move(index, src, dst, device):
            return pltpu.make_async_remote_copy(
                src_ref=src,
                dst_ref=dst,
                send_sem=sum_send.at[p, index],
                recv_sem=sum_recv.at[p, index],
                device_id=device,
                device_id_type=MESH,
            )

        def rows_of(owner):
            return pl.ds(pl.multiple_of(owner * share, SLOT), share)

        mine = rows_of(me_y)
        copies = []
        for d in range(1, size_y):
            device = at(0, d)
            copies.append(
                move(d - 1, partial.at[rows_of(device[1])], piece_in.at[p, d - 1], device)
            )
        for copy in copies:
            copy.start()
        for copy in copies:
            copy.wait()
        piece = partial[mine, :]
        for d in range(1, size_y):
            piece = piece + piece_in[p, d - 1]
        ring_in[p, me_x] = piece
        copies = []
        for d in range(1, size_x):
            copies.append(
                move(size_y + d - 2, ring_in.at[p, me_x], ring_in.at[p, me_x], at(d, 0))
            )
        for copy in copies:
            copy.start()
        for copy in copies:
            copy.wait()
        piece = ring_in[p, 0]
        for d in range(1, size_x):
            piece = piece + ring_in[p, d]
        gram_sum[p, mine] = piece / node_total
        copies = []
        for d in range(1, size_y):
            copies.append(
                move(
                    size_y + size_x + d - 3, gram_sum.at[p, mine], gram_sum.at[p, mine], at(0, d)
                )
            )
        for copy in copies:
            copy.start()
        for copy in copies:
            copy.wait()

    def one_pass(p, carry):
        def step(k, inner):
            one_apply(k, p)
            return inner

        lax.fori_loop(0, CHEB_DEGREE, step, 0)
        q = lax.rem((p + 1) * CHEB_DEGREE, 2)

        def divide(x, inner):
            shape = (ROWS, COLUMN, STATES)
            value = jnp.where(row_in_slot(shape, 1) < ORDER, block[q, x, 0:ROWS], 0.0)
            high_part, low_part = split_two(value.reshape(ROWS * COLUMN, STATES))
            rows = pl.ds(pl.multiple_of(x * ROWS * COLUMN, ROWS * COLUMN), ROWS * COLUMN)
            split[rows, 0:STATES] = high_part
            split[rows, STATES : 2 * STATES] = low_part
            return inner

        lax.fori_loop(0, ROWS, divide, 0)
        products = dot_tn(split[:, 0:STATES], split[...])
        cross = products[:, STATES : 2 * STATES]
        partial[...] = products[:, 0:STATES] + cross + cross.T
        sum_everywhere(p)
        whole = gram_sum[p]
        work[:, 0:STATES] = whole
        diagonal = lax.broadcasted_iota(jnp.int32, (STATES, STATES), 0) == lax.broadcasted_iota(
            jnp.int32, (STATES, STATES), 1
        )
        work[:, STATES : 2 * STATES] = jnp.where(diagonal, 1.0, 0.0)
        factor_rows(work)
        inverse = work[:, STATES : 2 * STATES]
        gram_out[...] = whole
        pair = stacked_inverse(inverse)

        def turned(x):
            value = block[q, x, 0:ROWS].reshape(ROWS * COLUMN, STATES)
            return times_inverse(value, pair).reshape(ROWS, COLUMN, STATES)

        @pl.when(p == 0)
        def _():
            def turn(x, inner):
                block[q, x, 0:ROWS] = turned(x)
                return inner

            lax.fori_loop(0, ROWS, turn, 0)

        @pl.when(p == 1)
        def _():
            def turn(x, inner):
                result = turned(x)
                for h in range(COUNT_Z):
                    states_out[x, :, h * ORDER : (h + 1) * ORDER, :] = result[
                        :, h * SLOT : h * SLOT + ORDER, :
                    ]
                return inner

            lax.fori_loop(0, ROWS, turn, 0)

        return carry

    lax.fori_loop(0, 2, one_pass, 0)


def stacked_inverse(inverse):
    high, low = split_two(inverse)
    return jnp.concatenate(
        [jnp.concatenate([high, high], axis=1), jnp.concatenate([low, low], axis=1)], axis=0
    )


def times_inverse(value, pair):
    high, low = split_two(value)
    both = dot_nt(jnp.concatenate([high, low], axis=1), pair)
    return both[:, 0:STATES] + both[:, STATES : 2 * STATES]


def place_nodes(node_values, mass, pot):
    count_z = COUNT_Z * ORDER
    width = 3 * count_z
    row = lax.broadcasted_iota(jnp.int32, (COLUMN, width), 0)
    lane = lax.broadcasted_iota(jnp.int32, (COLUMN, width), 1)
    within = row % SLOT
    source = lax.rem((row // SLOT) * ORDER + within, count_z)
    pick = jnp.where((lax.rem(lane, count_z) == source) & (within < POINTS), 1.0, 0.0)
    ones = jnp.ones((width, STATES), BF16)
    third = lax.broadcasted_iota(jnp.int32, (2 * ROWS, width), 1) // count_z

    def one(x, carry):
        for base, out in ((0, mass), (ROWS * ROWS, pot)):
            start = pl.multiple_of(base + 2 * ROWS * x, SLOT)
            values = node_values[pl.ds(start, 2 * ROWS), :]
            high, middle, low = [v.astype(F32) for v in split_three(values)]
            parts = jnp.where(third == 0, high, jnp.where(third == 1, middle, low))
            spread = [
                jnp.broadcast_to(parts[y : y + 1, :], (COLUMN, width)) * pick
                for y in range(2 * ROWS)
            ]
            lines = dot_nn(jnp.concatenate(spread, axis=0).astype(BF16), ones)
            lines = lines.reshape(2, ROWS, COLUMN, STATES)
            out[2 * x, 0:ROWS] = lines[0]
            out[2 * x + 1, 0:ROWS] = lines[1]
        return carry

    lax.fori_loop(0, ROWS // 2, one, 0)
    mass[ROWS] = jnp.ones(mass.shape[1:], F32)
    mass[0:ROWS, ROWS] = jnp.ones((ROWS, COLUMN, STATES), F32)


def spread_matrix(cell_matrix, matrix, from_x, from_y, from_xy):
    nodes = POINTS**3
    row = lax.broadcasted_iota(jnp.int32, (KDIM, nodes), 0)
    col = lax.broadcasted_iota(jnp.int32, (KDIM, nodes), 1)
    b = (row // SLOT) % SLOT
    c = row % SLOT
    source = (row // FACE) * POINTS * POINTS + b * POINTS + c
    pick = jnp.where((col == source) & (b < POINTS) & (c < POINTS), 1.0, 0.0).astype(BF16)
    half = dot_nn(pick, cell_matrix[...]).astype(BF16)
    full = dot_nt(half, pick)
    width = SLOT * FACE
    full = jnp.concatenate([full, jnp.zeros((KDIM, FACE), F32)], axis=1)
    lane = lax.broadcasted_iota(jnp.int32, (FACE, width), 1)
    at_x = lane // FACE == POINTS
    at_y = (lane // SLOT) % SLOT == POINTS

    def seen(rows, shift, mask):
        return jnp.where(mask[0 : rows.shape[0]], pltpu.roll(rows, shift, 1), 0.0)

    last_y = [full[a * FACE + ORDER * SLOT : a * FACE + POINTS * SLOT] for a in range(POINTS)]
    last_x = full[ORDER * FACE : POINTS * FACE]
    groups = []
    for a in range(POINTS):
        group = full[a * FACE : (a + 1) * FACE]
        first = group[0:SLOT] + seen(last_y[a], SLOT, at_y & (~at_x))
        if a == 0:
            first = first + seen(last_y[ORDER], FACE + SLOT, at_y & at_x)
        group = jnp.concatenate([first, group[SLOT:]], axis=0)
        if a == 0:
            group = group + seen(last_x, FACE, at_x & (~at_y))
        groups.append(group)
    matrix[...] = jnp.concatenate(groups, axis=0).astype(BF16)

    row = lax.broadcasted_iota(jnp.int32, (KDIM, FACE), 0)
    col = lax.broadcasted_iota(jnp.int32, (KDIM, FACE), 1)
    face_x = jnp.where(row == ORDER * FACE + col, 1.0, 0.0)
    face_y = jnp.where(row == (col // SLOT) * FACE + ORDER * SLOT + col % SLOT, 1.0, 0.0)
    faces = jnp.concatenate([face_x, face_y], axis=1).astype(BF16)
    both = dot_nn(full[:, 0:KDIM].astype(BF16), faces)
    from_xy[...] = both.astype(BF16)
    low = lax.broadcasted_iota(jnp.int32, (FACE, 2 * FACE), 1) < FACE
    groups = []
    for a in range(POINTS):
        group = both[a * FACE : (a + 1) * FACE]
        moved = jnp.concatenate(
            [group[ORDER * SLOT : POINTS * SLOT], jnp.zeros((FACE - SLOT, 2 * FACE), F32)], axis=0
        )
        groups.append(jnp.where(low, group, pltpu.roll(moved, FACE, 1)))
    from_x[...] = jnp.concatenate(groups, axis=0).astype(BF16)
    groups = []
    for a in range(POINTS):
        group = pltpu.roll(both[a * FACE : (a + 1) * FACE], FACE, 1)
        moved = both[ORDER * FACE : POINTS * FACE] if a == 0 else jnp.zeros_like(group)
        groups.append(jnp.where(low, group, moved))
    from_y[...] = jnp.concatenate(groups, axis=0).astype(BF16)


def padded_table():
    table = lagrange_table(ORDER, COARSE_ORDER).astype(np.float32)
    table = table.reshape(ORDER * ORDER, ORDER, -1)
    table = np.pad(table, ((0, 0), (0, SLOT - ORDER), (0, COARSE_ROWS - table.shape[-1])))
    return jnp.asarray(table.reshape(-1, COARSE_ROWS), F32).astype(BF16)


def local(coarse_states, record_target, cell_matrix, mass_scale, potential, filter_window):
    rows_x, rows_y, rows_z = mass_scale.shape
    size_x = lax.axis_size("dx")
    size_y = lax.axis_size("dy")
    node_total = float(rows_x * rows_y * rows_z * size_x * size_y)
    lines = [v.reshape(rows_x * rows_y, rows_z) for v in (mass_scale, potential)]
    node_values = jnp.concatenate(lines, axis=0)
    node_values = jnp.concatenate([node_values] * 3, axis=1)
    target_tile = jnp.pad(record_target[None, :], ((0, SLOT - 1), (0, STATES - CELLS)))
    padded = (ROWS + 1, ROWS + 1, COLUMN, STATES)
    inside = (ROWS, ROWS, COLUMN, STATES)
    face = (ROWS, COLUMN, STATES)
    line = (COLUMN, STATES)
    share = STATES // size_y
    messages = 2 * size_y + size_x - 3
    vmem = pl.BlockSpec(memory_space=pltpu.VMEM)
    return pl.pallas_call(
        functools.partial(filter_kernel, size_x, size_y, node_total),
        out_shape=(
            jax.ShapeDtypeStruct((rows_x, rows_y, rows_z, STATES), F32),
            jax.ShapeDtypeStruct((STATES, STATES), F32),
        ),
        in_specs=[pl.BlockSpec(memory_space=pltpu.SMEM)] * 2 + [vmem] * 5,
        out_specs=(vmem, vmem),
        scratch_shapes=[
            pltpu.VMEM(padded, F32),
            pltpu.VMEM(inside, F32),
            pltpu.VMEM((KDIM, SLOT * FACE), BF16),
            pltpu.VMEM((KDIM, 2 * FACE), BF16),
            pltpu.VMEM((KDIM, 2 * FACE), BF16),
            pltpu.VMEM((KDIM, 2 * FACE), BF16),
            pltpu.VMEM((3, CAPACITY, COARSE_ROWS, STATES), BF16),
            pltpu.VMEM((4 * CAPACITY, COARSE_ROWS, STATES), BF16),
            pltpu.VMEM((3, SLOT, STATES), jnp.int32),
            pltpu.SMEM((3, SLOT, STATES), jnp.int32),
            pltpu.VMEM((2,) + padded, F32),
            pltpu.VMEM(padded, F32),
            pltpu.VMEM((SLOT * FACE, COUNT_Z * STATES), BF16),
            pltpu.VMEM((2 * FACE, COUNT_Z * STATES), BF16),
            pltpu.VMEM(face, BF16),
            pltpu.VMEM(face, BF16),
            pltpu.VMEM((2, 2 * ORDER + POINTS) + line, BF16),
            pltpu.VMEM((2, 3 * ORDER) + line, BF16),
            pltpu.VMEM(face, BF16),
            pltpu.VMEM(face, BF16),
            pltpu.VMEM(line, BF16),
            pltpu.VMEM((2,) + face, BF16),
            pltpu.VMEM((2,) + face, BF16),
            pltpu.VMEM((2,) + line, BF16),
            pltpu.VMEM((ROWS * ROWS * COLUMN, 2 * STATES), BF16),
            pltpu.VMEM((STATES, STATES), F32),
            pltpu.VMEM((2, size_y - 1, share, STATES), F32),
            pltpu.VMEM((2, size_x, share, STATES), F32),
            pltpu.VMEM((2, STATES, STATES), F32),
            pltpu.VMEM((STATES, 2 * STATES), F32),
            pltpu.SemaphoreType.DMA((3,)),
            pltpu.SemaphoreType.DMA((3,)),
            pltpu.SemaphoreType.DMA((3,)),
            pltpu.SemaphoreType.DMA((3,)),
            pltpu.SemaphoreType.DMA((3,)),
            pltpu.SemaphoreType.DMA((2, 8)),
            pltpu.SemaphoreType.DMA((2, 8)),
            pltpu.SemaphoreType.DMA((2, messages)),
            pltpu.SemaphoreType.DMA((2, messages)),
        ],
        compiler_params=pltpu.CompilerParams(
            collective_id=0, has_side_effects=True, vmem_limit_bytes=52 * 1024 * 1024
        ),
        cost_estimate=pl.CostEstimate(
            flops=6 * 4 * 2 * KDIM * KDIM * 512, bytes_accessed=10_000_000, transcendentals=0
        ),
        name="filter_twice",
    )(filter_window, record_target, target_tile, coarse_states, padded_table(), node_values, cell_matrix)


def solution(mesh):
    in_specs = (
        P(("dx", "dy"), None, None),
        P(("dx", "dy")),
        P(),
        P("dx", "dy", None),
        P("dx", "dy", None),
        P(),
    )
    out_specs = (P("dx", "dy", None, None), P())
    return jax.shard_map(local, mesh=mesh, in_specs=in_specs, out_specs=out_specs, check_vma=False)
```

```python
import functools

import jax
import jax.numpy as jnp
import numpy as np
from jax import lax
from jax.experimental import pallas as pl
from jax.experimental.pallas import tpu as pltpu
from jax.sharding import PartitionSpec as P

ORDER = 6
COARSE_ORDER = 4
CHEB_DEGREE = 3
POINTS = ORDER + 1
COUNT_Z = 4
SLOT = 8
COLUMN = COUNT_Z * SLOT
ROWS = 12
STATES = 128
PAIRS = 4
KDIM = POINTS * SLOT * SLOT
FACE = SLOT * SLOT
DEPTH = COUNT_Z * ORDER
PAIR = 2 * DEPTH
LINES = ROWS // 2
CELLS = 16
CAPACITY = CELLS // 2
COARSE_ROWS = 128
MESH = pl.DeviceIdType.MESH
F32 = jnp.float32
BF16 = jnp.bfloat16


def node_points(degree_value):
    return -np.cos(np.pi * np.arange(degree_value + 1) / degree_value)


def lagrange_table(fine_degree, coarse_degree):
    targets = node_points(fine_degree)
    sources = node_points(coarse_degree)
    matrix = np.ones((fine_degree + 1, coarse_degree + 1))
    for p in range(coarse_degree + 1):
        for m in range(coarse_degree + 1):
            if m != p:
                matrix[:, p] = matrix[:, p] * (targets - sources[m]) / (sources[p] - sources[m])
    owned_rows = matrix[:fine_degree]
    first = owned_rows[:, None, None, :, None, None]
    second = owned_rows[None, :, None, None, :, None]
    third = owned_rows[None, None, :, None, None, :]
    product = first * second * third
    return product.reshape(fine_degree**3, (coarse_degree + 1) ** 3)


def row_in_slot(shape, axis):
    return lax.broadcasted_iota(jnp.int32, shape, axis) % SLOT


def dot_nn(a, b):
    return lax.dot_general(a, b, (((1,), (0,)), ((), ())), preferred_element_type=F32)


def dot_tn(a, b):
    return lax.dot_general(a, b, (((0,), (0,)), ((), ())), preferred_element_type=F32)


def dot_nt(a, b):
    return lax.dot_general(a, b, (((1,), (1,)), ((), ())), preferred_element_type=F32)


def split_two(value):
    high = value.astype(BF16)
    return high, (value - high.astype(F32)).astype(BF16)


def split_three(value):
    high = value.astype(BF16)
    rest = value - high.astype(F32)
    middle = rest.astype(BF16)
    return high, middle, (rest - middle.astype(F32)).astype(BF16)


def factor_rows(work):
    size = STATES
    sub = lax.broadcasted_iota(jnp.int32, (SLOT, size), 0)
    lane = lax.broadcasted_iota(jnp.int32, (SLOT, size), 1)

    def panel(j, carry):
        base = pl.multiple_of(j * SLOT, SLOT)
        left = work[pl.ds(base, SLOT), 0:size]
        right = work[pl.ds(base, SLOT), size : 2 * size]
        turned = pltpu.roll(left, lax.rem(size - base, size), 1)
        columns = [jnp.broadcast_to(turned[:, m : m + 1], (SLOT, size)) for m in range(SLOT)]
        for m in range(SLOT):
            pivot = jnp.broadcast_to(columns[m][m : m + 1, :], (SLOT, size))
            scale = lax.rsqrt(pivot)
            scale = scale * (1.5 - 0.5 * pivot * scale * scale)
            below = sub > m
            at = sub == m
            coef = columns[m] * scale
            row_left = jnp.broadcast_to(left[m : m + 1, :], (SLOT, size)) * scale
            row_right = jnp.broadcast_to(right[m : m + 1, :], (SLOT, size)) * scale
            for n in range(m + 1, SLOT):
                entry = jnp.broadcast_to(columns[n][m : m + 1, :], (SLOT, size)) * scale
                columns[n] = jnp.where(below, columns[n] - coef * entry, columns[n])
            left = jnp.where(below, left - coef * row_left, jnp.where(at, row_left, left))
            right = jnp.where(below, right - coef * row_right, jnp.where(at, row_right, right))
        work[pl.ds(base, SLOT), 0:size] = left
        work[pl.ds(base, SLOT), size : 2 * size] = right
        later = jnp.where(lane >= base + SLOT, left, 0.0)
        l1, l2, l3 = [v.astype(F32) for v in split_three(later)]
        both = jnp.concatenate([left, right], axis=1)
        b1, b2, b3 = [v.astype(F32) for v in split_three(both)]
        lhs = jnp.concatenate([l1, l1, l2, l1, l3, l2], axis=0).astype(BF16)
        rhs = jnp.concatenate([b1, b2, b1, b3, b1, b2], axis=0).astype(BF16)
        work[...] = work[...] - dot_tn(lhs, rhs)
        return carry

    lax.fori_loop(0, size // SLOT, panel, 0)


def filter_kernel(
    size_x,
    size_y,
    node_total,
    window,
    targets,
    coarse,
    table,
    mass_in,
    pot_in,
    cell_matrix,
    filtered_out,
    inverse_out,
    gram_out,
    mass,
    pot,
    matrix,
    from_x,
    from_y,
    shrink,
    grow,
    grow_own,
    target_tile,
    filtered,
    slots,
    arrived,
    target_in,
    target_list,
    block,
    total,
    rhs,
    rhs_taken,
    send_x,
    send_y,
    take_x,
    take_y,
    back_x,
    back_y,
    back_c,
    got_x,
    got_y,
    got_c,
    split,
    partial,
    piece_in,
    ring_in,
    gram_sum,
    work,
    target_send,
    target_recv,
    list_sems,
    record_send,
    record_recv,
    store_sem,
    send_sems,
    recv_sems,
    sum_send,
    sum_recv,
):
    me_x = lax.axis_index("dx")
    me_y = lax.axis_index("dy")

    def at(step_x, step_y):
        return (lax.rem(me_x + step_x + size_x, size_x), lax.rem(me_y + step_y + size_y, size_y))

    partners = [at(0, d) for d in range(1, size_y)] + [at(d, 0) for d in range(1, size_x)]
    partners += [at(1, 1), at(-1, -1), at(1, -1), at(-1, 1)]
    barrier = pltpu.get_barrier_semaphore()
    for partner in partners:
        pl.semaphore_signal(barrier, inc=1, device_id=partner, device_id_type=MESH)
    steps = (None, (0, 1), (1, 0), (1, 1))
    buckets, ranks = [], []
    counts = [0, 0, 0, 0]
    for r in range(CELLS):
        device = targets[r] // CELLS
        step_x = lax.rem(device // size_y - me_x + size_x, size_x)
        step_y = lax.rem(lax.rem(device, size_y) - me_y + size_y, size_y)
        bucket = 2 * step_x + step_y
        rank = 0
        for index in range(4):
            rank = rank + jnp.where(bucket == index, counts[index], 0)
            counts[index] = counts[index] + jnp.where(bucket == index, 1, 0)
        buckets.append(bucket)
        ranks.append(bucket * CAPACITY + rank)

    def record_of(slot):
        found = 0
        for r in range(CELLS):
            found = found + jnp.where(ranks[r] == slot, r, 0)
        return jnp.minimum(jnp.maximum(found, 0), CELLS - 1)

    last = COARSE_ROWS - 16
    for index in range(3):
        slots[index, :, last:COARSE_ROWS] = jnp.zeros((CAPACITY, 16, STATES), BF16)
    arrived[0:CAPACITY, last:COARSE_ROWS] = jnp.zeros((CAPACITY, 16, STATES), BF16)
    coarse_count = coarse.shape[1]
    tile_lane = lax.broadcasted_iota(jnp.int32, (SLOT, STATES), 1)
    tile = jnp.zeros((SLOT, STATES), jnp.int32)
    for r in range(CELLS):
        tile = jnp.where(tile_lane == r, targets[r], tile)
    target_tile[...] = tile
    pl.semaphore_wait(barrier, len(partners))
    target_copies, record_copies = {}, {}
    for index in (3, 2, 1):
        target_copies[index] = pltpu.make_async_remote_copy(
            src_ref=target_tile,
            dst_ref=target_in.at[index - 1],
            send_sem=target_send.at[index - 1],
            recv_sem=target_recv.at[index - 1],
            device_id=at(*steps[index]),
            device_id_type=MESH,
        )
        target_copies[index].start()
    for index in (3, 2, 1):
        for k in range(CAPACITY):
            slots[index - 1, k, 0:coarse_count] = coarse[record_of(index * CAPACITY + k)]
        record_copies[index] = pltpu.make_async_remote_copy(
            src_ref=slots.at[index - 1],
            dst_ref=arrived.at[pl.ds(index * CAPACITY, CAPACITY)],
            send_sem=record_send.at[index - 1],
            recv_sem=record_recv.at[index - 1],
            device_id=at(*steps[index]),
            device_id_type=MESH,
        )
        record_copies[index].start()
    for k in range(CAPACITY):
        arrived[k, 0:coarse_count] = coarse[record_of(k)]

    place_nodes(mass_in, pot_in, mass, pot)
    spread_matrix(cell_matrix, matrix, from_x, from_y)
    line_tables(shrink, grow, grow_own)
    block[1] = jnp.zeros(block.shape[1:], F32)

    for index in (3, 2, 1):
        target_copies[index].wait()
    lists = [
        pltpu.make_async_copy(target_in.at[i], target_list.at[i], list_sems.at[i]) for i in range(3)
    ]
    for copy in lists:
        copy.start()
    for copy in lists:
        copy.wait()
    own = me_x * size_y + me_y
    places = [0] * CELLS
    for index in range(4):
        seen = 0
        for r in range(CELLS):
            target = targets[r] if index == 0 else target_list[index - 1, 0, r]
            hit = target // CELLS == own
            cell = jnp.where(hit, lax.rem(target, CELLS), -1)
            slot = index * CAPACITY + seen
            for g in range(CELLS):
                places[g] = places[g] + jnp.where(cell == g, slot, 0)
            seen = seen + jnp.where(hit, 1, 0)
    places = [jnp.minimum(jnp.maximum(p, 0), 4 * CAPACITY - 1) for p in places]
    for index in (3, 2, 1):
        record_copies[index].wait()
    slot_row = row_in_slot((COLUMN, STATES), 0)
    for e in range(2):
        for f in range(2):
            for h in range(COUNT_Z):
                rhs[0:COARSE_ROWS, h * STATES : (h + 1) * STATES] = arrived[
                    places[(2 * e + f) * COUNT_Z + h]
                ]
            fine = dot_nn(table[...], rhs[0:COARSE_ROWS, :]).astype(BF16).astype(F32)
            for a in range(ORDER):
                for b in range(ORDER):
                    first = (a * ORDER + b) * SLOT
                    lines = [
                        fine[first : first + SLOT, h * STATES : (h + 1) * STATES]
                        for h in range(COUNT_Z)
                    ]
                    lines = jnp.concatenate(lines, axis=0)
                    again = pltpu.roll(lines, COLUMN - SLOT + ORDER, 0)
                    block[0, e * ORDER + a, f * ORDER + b] = jnp.where(
                        slot_row == ORDER, again, lines
                    )

    low = window[0]
    high = window[1]
    center = (low + high) / 2.0
    radius = (high - low) / 2.0

    def remote(turn, index, src, dst, step_x, step_y):
        return pltpu.make_async_remote_copy(
            src_ref=src,
            dst_ref=dst,
            send_sem=send_sems.at[turn, index],
            recv_sem=recv_sems.at[turn, index],
            device_id=at(step_x, step_y),
            device_id_type=MESH,
        )

    zeros = jnp.zeros((SLOT, STATES), F32)

    def pack(first, second):
        return jnp.concatenate([first, second], axis=0).astype(BF16)

    def add_product(product, e, f, points_x, points_y, written):
        for a in range(points_x):
            for b in range(points_y):
                first = (a * SLOT + b) * SLOT
                x, y = e * ORDER + a, f * ORDER + b
                for h in range(COUNT_Z):
                    rows = slice(h * SLOT, (h + 1) * SLOT)
                    part = product[first : first + SLOT, h * STATES : (h + 1) * STATES]
                    if (x, y) in written:
                        part = part + total[x, y, rows]
                    total[x, y, rows] = part
                written.add((x, y))

    def column(q, e, f, written):
        points_x = POINTS if e == 0 else ORDER
        for a in range(points_x):
            x = e * ORDER + a
            for h in range(COUNT_Z):
                rows = slice(h * SLOT, (h + 1) * SLOT)
                chunks = []
                for b in range(POINTS):
                    y = f * ORDER + b
                    own = y < ROWS
                    chunks.append(mass[x, y, rows] * block[q, x, y, rows] if own else zeros)
                chunks.append(chunks[0] if f == 0 else zeros)
                for i in range(PAIRS):
                    tile = pack(chunks[2 * i], chunks[2 * i + 1])
                    copies = [a, POINTS] if (a == 0 and e == 0) else [a]
                    for place in copies:
                        first = (place * PAIRS + i) * 2 * SLOT
                        rhs[first : first + 2 * SLOT, h * STATES : (h + 1) * STATES] = tile
        depth = FACE * (SLOT if e == 0 else ORDER)
        product = dot_nn(matrix[:, 0:depth], rhs[0:depth, :])
        add_product(product, e, f, POINTS, POINTS, written)

    def taken_rows(base, lines, h):
        chunks = [line[h * SLOT : (h + 1) * SLOT] if line is not None else zeros for line in lines]
        for i in range(PAIRS):
            first = base + i * 2 * SLOT
            rhs_taken[first : first + 2 * SLOT, h * STATES : (h + 1) * STATES] = pack(
                chunks[2 * i], chunks[2 * i + 1]
            )

    def taken_column(e, f, factor, runs, points_x, points_y, written):
        for index, lines in enumerate(runs):
            for h in range(COUNT_Z):
                taken_rows(index * FACE, lines, h)
        depth = FACE * len(runs)
        product = dot_nn(factor[:, 0:depth], rhs_taken[0:depth, :])
        add_product(product, e, f, points_x, points_y, written)

    def narrow(lines, out):
        wide = lines.astype(BF16).reshape(LINES, 2 * COLUMN, STATES)
        wide = jnp.concatenate([wide[i] for i in range(LINES)], axis=1)
        packed = dot_nn(shrink[...], wide).astype(BF16)
        for i in range(LINES):
            out[i] = packed[:, i * STATES : (i + 1) * STATES]

    def widen(pairs, rows_of_slot):
        wide = dot_nn(rows_of_slot[...], jnp.concatenate(pairs, axis=1))
        lines = []
        for i in range(len(pairs)):
            for half in range(2):
                lines.append(
                    wide[half * COLUMN : (half + 1) * COLUMN, i * STATES : (i + 1) * STATES]
                )
        return lines

    def folded(raw):
        axis = raw.ndim - 2
        first = row_in_slot(raw.shape, axis) == 0
        return raw + jnp.where(first, pltpu.roll(raw, SLOT - ORDER, axis), 0.0)

    def finish(q, x, y, count, alpha, beta):
        shape = (count, COLUMN, STATES)
        slot_row = row_in_slot(shape, 1)
        ys = pl.ds(y, count)
        raw = total[x, ys]
        summed = folded(raw)
        again = pltpu.roll(summed, COLUMN - SLOT + ORDER, 1)
        full = jnp.where(slot_row < ORDER, summed, jnp.where(slot_row == ORDER, again, 0.0))
        value = block[q, x, ys]
        result = mass[x, ys] * full + (pot[x, ys] - center) * value
        block[1 - q, x, ys] = alpha * result - beta * block[1 - q, x, ys]

    def one_apply(k, p):
        q = lax.rem(p * CHEB_DEGREE + k, 2)
        first = k == 0
        alpha = jnp.where(first, 1.0, 2.0) / radius
        beta = jnp.where(first, 0.0, 1.0)
        half = pl.ds(LINES // 2, LINES // 2)
        quarter = LINES // 2
        values_x = [
            remote(q, 0, send_x, take_x.at[q, pl.ds(quarter, LINES)], -1, 0),
            remote(q, 2, send_x.at[half], take_x.at[q, pl.ds(0, quarter)], -1, 1),
            remote(
                q, 3, send_x.at[pl.ds(0, 1)], take_x.at[q, pl.ds(quarter + LINES, 1)], -1, -1
            ),
        ]
        value_y = remote(q, 1, send_y, take_y.at[q], 0, -1)
        sum_x = remote(q, 4, back_x, got_x.at[q], 1, 0)
        sum_y = remote(q, 5, back_y, got_y.at[q], 0, 1)
        sum_c = remote(q, 6, back_c, got_c.at[q], 1, 1)
        narrow(mass[0, 0:ROWS] * block[q, 0, 0:ROWS], send_x)
        for copy in values_x:
            copy.start()
        narrow(mass[0:ROWS, 0] * block[q, 0:ROWS, 0], send_y)
        value_y.start()
        written = set()
        column(q, 1, 1, written)
        column(q, 1, 0, written)
        column(q, 0, 1, written)
        narrow(folded(total[0:ROWS, ROWS]), back_y)
        sum_y.start()
        back_c[...] = total[ROWS, ROWS].astype(BF16)
        sum_c.start()
        value_y.wait()
        along_y = widen([take_y[q, i] for i in range(LINES)], grow)
        taken_column(1, 1, from_y, [along_y[ORDER:] + [None] * 2], POINTS, ORDER, written)
        narrow(folded(total[ROWS, 0:ROWS]), back_x)
        sum_x.start()
        taken_column(
            0, 1, from_y, [along_y[0:POINTS] + [along_y[0]]], POINTS, ORDER, written
        )
        column(q, 0, 0, written)
        for copy in values_x:
            copy.wait()
        along_x = widen([take_x[q, i] for i in range(quarter + LINES + 1)], grow)
        last = 2 * ORDER
        taken_column(
            1, 1, from_x, [along_x[last : last + POINTS] + [None]], ORDER, ORDER, written
        )
        taken_column(
            1,
            0,
            from_x,
            [along_x[ORDER : last + 1] + [None], along_x[0:POINTS] + [None]],
            ORDER,
            POINTS,
            written,
        )

        def interior(x, carry):
            finish(q, x, 1, ROWS - 1, alpha, beta)
            return carry

        lax.fori_loop(1, ROWS, interior, 0)
        for copy in (sum_c, sum_y, sum_x):
            copy.wait()
        total[0, 0] += got_c[q].astype(F32)
        for x, line in enumerate(widen([got_y[q, i] for i in range(LINES)], grow_own)):
            total[x, 0] += line
        for y, line in enumerate(widen([got_x[q, i] for i in range(LINES)], grow_own)):
            total[0, y] += line
        finish(q, 0, 0, ROWS, alpha, beta)

        def edge(x, carry):
            finish(q, x, 0, 1, alpha, beta)
            return carry

        lax.fori_loop(1, ROWS, edge, 0)

    def sum_everywhere(p):
        share = STATES // size_y

        def move(index, src, dst, device):
            return pltpu.make_async_remote_copy(
                src_ref=src,
                dst_ref=dst,
                send_sem=sum_send.at[p, index],
                recv_sem=sum_recv.at[p, index],
                device_id=device,
                device_id_type=MESH,
            )

        def rows_of(owner):
            return pl.ds(pl.multiple_of(owner * share, SLOT), share)

        mine = rows_of(me_y)
        copies = []
        for d in range(1, size_y):
            device = at(0, d)
            copies.append(
                move(d - 1, partial.at[rows_of(device[1])], piece_in.at[p, d - 1], device)
            )
        for copy in copies:
            copy.start()
        for copy in copies:
            copy.wait()
        piece = partial[mine, :]
        for d in range(1, size_y):
            piece = piece + piece_in[p, d - 1]
        ring_in[p, me_x] = piece
        copies = []
        for d in range(1, size_x):
            copies.append(
                move(size_y + d - 2, ring_in.at[p, me_x], ring_in.at[p, me_x], at(d, 0))
            )
        for copy in copies:
            copy.start()
        for copy in copies:
            copy.wait()
        piece = ring_in[p, 0]
        for d in range(1, size_x):
            piece = piece + ring_in[p, d]
        gram_sum[p, mine] = piece / node_total
        copies = []
        for d in range(1, size_y):
            copies.append(
                move(
                    size_y + size_x + d - 3, gram_sum.at[p, mine], gram_sum.at[p, mine], at(0, d)
                )
            )
        for copy in copies:
            copy.start()
        for copy in copies:
            copy.wait()

    def one_pass(p, carry):
        def step(k, inner):
            one_apply(k, p)
            return inner

        lax.fori_loop(0, CHEB_DEGREE, step, 0)
        q = lax.rem((p + 1) * CHEB_DEGREE, 2)

        def divide(x, inner):
            value = block[q, x, 0:ROWS]
            value = jnp.concatenate(
                [value[:, h * SLOT : h * SLOT + ORDER] for h in range(COUNT_Z)], axis=1
            )

            @pl.when(p == 1)
            def _():
                filtered[x] = value

            high_part, low_part = split_two(value.reshape(ROWS * DEPTH, STATES))
            rows = pl.ds(pl.multiple_of(x * ROWS * DEPTH, ROWS * DEPTH), ROWS * DEPTH)
            split[rows, 0:STATES] = high_part
            split[rows, STATES : 2 * STATES] = low_part
            return inner

        lax.fori_loop(0, ROWS, divide, 0)

        @pl.when(p == 1)
        def _():
            pltpu.make_async_copy(filtered, filtered_out, store_sem).start()

        products = dot_tn(split[:, 0:STATES], split[...])
        cross = products[:, STATES : 2 * STATES]
        partial[...] = products[:, 0:STATES] + cross + cross.T
        sum_everywhere(p)
        whole = gram_sum[p]
        work[:, 0:STATES] = whole
        diagonal = lax.broadcasted_iota(jnp.int32, (STATES, STATES), 0) == lax.broadcasted_iota(
            jnp.int32, (STATES, STATES), 1
        )
        work[:, STATES : 2 * STATES] = jnp.where(diagonal, 1.0, 0.0)
        factor_rows(work)
        inverse = work[:, STATES : 2 * STATES]
        gram_out[...] = whole
        inverse_out[...] = inverse

        @pl.when(p == 0)
        def _():
            pair = stacked_inverse(inverse)

            def turn(x, inner):
                value = block[q, x, 0:ROWS].reshape(ROWS * COLUMN, STATES)
                block[q, x, 0:ROWS] = times_inverse(value, pair).reshape(ROWS, COLUMN, STATES)
                return inner

            lax.fori_loop(0, ROWS, turn, 0)

        return carry

    lax.fori_loop(0, 2, one_pass, 0)
    pltpu.make_async_copy(filtered, filtered_out, store_sem).wait()


def stacked_inverse(inverse):
    high, low = split_two(inverse)
    return jnp.concatenate(
        [jnp.concatenate([high, high], axis=1), jnp.concatenate([low, low], axis=1)], axis=0
    )


def times_inverse(value, pair):
    high, low = split_two(value)
    both = dot_nt(jnp.concatenate([high, low], axis=1), pair)
    return both[:, 0:STATES] + both[:, STATES : 2 * STATES]


def place_nodes(mass_in, pot_in, mass, pot):
    width = 3 * DEPTH
    row = lax.broadcasted_iota(jnp.int32, (COLUMN, width), 0)
    lane = lax.broadcasted_iota(jnp.int32, (COLUMN, width), 1)
    within = row % SLOT
    source = lax.rem((row // SLOT) * ORDER + within, DEPTH)
    pick = jnp.where((lax.rem(lane, DEPTH) == source) & (within < POINTS), 1.0, 0.0)
    ones = jnp.ones((width, STATES), BF16)

    def one(x, carry):
        for values, out in ((mass_in, mass), (pot_in, pot)):
            parts = [v.astype(F32) for v in split_three(values[x])]
            parts = jnp.concatenate(parts, axis=1)
            spread = [
                jnp.broadcast_to(parts[y : y + 1, :], (COLUMN, width)) * pick for y in range(ROWS)
            ]
            lines = dot_nn(jnp.concatenate(spread, axis=0).astype(BF16), ones)
            out[x, 0:ROWS] = lines.reshape(ROWS, COLUMN, STATES)
        return carry

    lax.fori_loop(0, ROWS, one, 0)
    mass[ROWS] = jnp.ones(mass.shape[1:], F32)
    mass[0:ROWS, ROWS] = jnp.ones((ROWS, COLUMN, STATES), F32)


def line_tables(shrink, grow, grow_own):
    row = lax.broadcasted_iota(jnp.int32, (PAIR, 2 * COLUMN), 0)
    col = lax.broadcasted_iota(jnp.int32, (PAIR, 2 * COLUMN), 1)
    z = row % DEPTH
    chosen = (row // DEPTH) * COLUMN + (z // ORDER) * SLOT + z % ORDER
    shrink[...] = jnp.where(col == chosen, 1.0, 0.0).astype(BF16)
    row = lax.broadcasted_iota(jnp.int32, (2 * COLUMN, PAIR), 0)
    col = lax.broadcasted_iota(jnp.int32, (2 * COLUMN, PAIR), 1)
    c = row % SLOT
    z = (((row // SLOT) % COUNT_Z) * ORDER + c) % DEPTH
    same = col == (row // COLUMN) * DEPTH + z
    grow[...] = jnp.where(same & (c < POINTS), 1.0, 0.0).astype(BF16)
    grow_own[...] = jnp.where(same & (c < ORDER), 1.0, 0.0).astype(BF16)


def spread_matrix(cell_matrix, matrix, from_x, from_y):
    nodes = POINTS**3
    row = lax.broadcasted_iota(jnp.int32, (KDIM, nodes), 0)
    col = lax.broadcasted_iota(jnp.int32, (KDIM, nodes), 1)
    b = (row // SLOT) % SLOT
    c = row % SLOT
    source = (row // FACE) * POINTS * POINTS + b * POINTS + c
    pick = jnp.where((col == source) & (b < POINTS) & (c < POINTS), 1.0, 0.0).astype(BF16)
    half = dot_nn(pick, cell_matrix[...]).astype(BF16)
    full = dot_nt(half, pick)
    width = SLOT * FACE
    full = jnp.concatenate([full, jnp.zeros((KDIM, FACE), F32)], axis=1)
    lane = lax.broadcasted_iota(jnp.int32, (FACE, width), 1)
    at_x = lane // FACE == POINTS
    at_y = (lane // SLOT) % SLOT == POINTS

    def seen(rows, shift, mask):
        return jnp.where(mask[0 : rows.shape[0]], pltpu.roll(rows, shift, 1), 0.0)

    last_y = [full[a * FACE + ORDER * SLOT : a * FACE + POINTS * SLOT] for a in range(POINTS)]
    last_x = full[ORDER * FACE : POINTS * FACE]
    groups = []
    for a in range(POINTS):
        group = full[a * FACE : (a + 1) * FACE]
        first = group[0:SLOT] + seen(last_y[a], SLOT, at_y & (~at_x))
        if a == 0:
            first = first + seen(last_y[ORDER], FACE + SLOT, at_y & at_x)
        group = jnp.concatenate([first, group[SLOT:]], axis=0)
        if a == 0:
            group = group + seen(last_x, FACE, at_x & (~at_y))
        groups.append(group)
    matrix[...] = jnp.concatenate(groups, axis=0).astype(BF16)

    row = lax.broadcasted_iota(jnp.int32, (KDIM, FACE), 0)
    col = lax.broadcasted_iota(jnp.int32, (KDIM, FACE), 1)
    face_x = jnp.where(row == ORDER * FACE + col, 1.0, 0.0)
    face_y = jnp.where(row == (col // SLOT) * FACE + ORDER * SLOT + col % SLOT, 1.0, 0.0)
    faces = jnp.concatenate([face_x, face_y], axis=1).astype(BF16)
    both = dot_nn(full[:, 0:KDIM].astype(BF16), faces)
    low = lax.broadcasted_iota(jnp.int32, (FACE, 2 * FACE), 1) < FACE
    groups = []
    for a in range(POINTS):
        group = both[a * FACE : (a + 1) * FACE]
        moved = jnp.concatenate(
            [group[ORDER * SLOT : POINTS * SLOT], jnp.zeros((FACE - SLOT, 2 * FACE), F32)], axis=0
        )
        groups.append(jnp.where(low, group, pltpu.roll(moved, FACE, 1)))
    from_x[...] = jnp.concatenate(groups, axis=0).astype(BF16)
    faces_y = pltpu.roll(both, FACE, 1)[:, 0:FACE]
    seen_y = pltpu.roll(both[ORDER * FACE : POINTS * FACE], FACE + SLOT, 1)[:, 0:FACE]
    at_end = lax.broadcasted_iota(jnp.int32, (FACE, FACE), 1) >= POINTS * SLOT
    first = jnp.where(at_end, seen_y, faces_y[0:FACE])
    from_y[...] = jnp.concatenate([first, faces_y[FACE:]], axis=0).astype(BF16)


def padded_table():
    table = lagrange_table(ORDER, COARSE_ORDER).astype(np.float32)
    table = table.reshape(ORDER * ORDER, ORDER, -1)
    table = np.pad(table, ((0, 0), (0, SLOT - ORDER), (0, COARSE_ROWS - table.shape[-1])))
    return jnp.asarray(table.reshape(-1, COARSE_ROWS), F32).astype(BF16)


def local(coarse_states, record_target, cell_matrix, mass_scale, potential, filter_window):
    rows_x, rows_y, rows_z = mass_scale.shape
    size_x = lax.axis_size("dx")
    size_y = lax.axis_size("dy")
    node_total = float(rows_x * rows_y * rows_z * size_x * size_y)
    padded = (ROWS + 1, ROWS + 1, COLUMN, STATES)
    inside = (ROWS, ROWS, COLUMN, STATES)
    pair = (PAIR, STATES)
    face = (LINES,) + pair
    line = (COLUMN, STATES)
    share = STATES // size_y
    messages = 2 * size_y + size_x - 3
    vmem = pl.BlockSpec(memory_space=pltpu.VMEM)
    filtered, inverse, gram_matrix = pl.pallas_call(
        functools.partial(filter_kernel, size_x, size_y, node_total),
        out_shape=(
            jax.ShapeDtypeStruct((rows_x, rows_y, rows_z, STATES), F32),
            jax.ShapeDtypeStruct((STATES, STATES), F32),
            jax.ShapeDtypeStruct((STATES, STATES), F32),
        ),
        in_specs=[pl.BlockSpec(memory_space=pltpu.SMEM)] * 2 + [vmem] * 5,
        out_specs=(pl.BlockSpec(memory_space=pl.ANY), vmem, vmem),
        scratch_shapes=[
            pltpu.VMEM(padded, F32),
            pltpu.VMEM(inside, F32),
            pltpu.VMEM((KDIM, SLOT * FACE), BF16),
            pltpu.VMEM((KDIM, 2 * FACE), BF16),
            pltpu.VMEM((KDIM, FACE), BF16),
            pltpu.VMEM((PAIR, 2 * COLUMN), BF16),
            pltpu.VMEM((2 * COLUMN, PAIR), BF16),
            pltpu.VMEM((2 * COLUMN, PAIR), BF16),
            pltpu.VMEM((SLOT, STATES), jnp.int32),
            pltpu.VMEM((rows_x, rows_y, rows_z, STATES), F32),
            pltpu.VMEM((3, CAPACITY, COARSE_ROWS, STATES), BF16),
            pltpu.VMEM((4 * CAPACITY, COARSE_ROWS, STATES), BF16),
            pltpu.VMEM((3, SLOT, STATES), jnp.int32),
            pltpu.SMEM((3, SLOT, STATES), jnp.int32),
            pltpu.VMEM((2,) + padded, F32),
            pltpu.VMEM(padded, F32),
            pltpu.VMEM((SLOT * FACE, COUNT_Z * STATES), BF16),
            pltpu.VMEM((2 * FACE, COUNT_Z * STATES), BF16),
            pltpu.VMEM(face, BF16),
            pltpu.VMEM(face, BF16),
            pltpu.VMEM((2, LINES // 2 + LINES + 1) + pair, BF16),
            pltpu.VMEM((2,) + face, BF16),
            pltpu.VMEM(face, BF16),
            pltpu.VMEM(face, BF16),
            pltpu.VMEM(line, BF16),
            pltpu.VMEM((2,) + face, BF16),
            pltpu.VMEM((2,) + face, BF16),
            pltpu.VMEM((2,) + line, BF16),
            pltpu.VMEM((ROWS * ROWS * DEPTH, 2 * STATES), BF16),
            pltpu.VMEM((STATES, STATES), F32),
            pltpu.VMEM((2, size_y - 1, share, STATES), F32),
            pltpu.VMEM((2, size_x, share, STATES), F32),
            pltpu.VMEM((2, STATES, STATES), F32),
            pltpu.VMEM((STATES, 2 * STATES), F32),
            pltpu.SemaphoreType.DMA((3,)),
            pltpu.SemaphoreType.DMA((3,)),
            pltpu.SemaphoreType.DMA((3,)),
            pltpu.SemaphoreType.DMA((3,)),
            pltpu.SemaphoreType.DMA((3,)),
            pltpu.SemaphoreType.DMA,
            pltpu.SemaphoreType.DMA((2, 7)),
            pltpu.SemaphoreType.DMA((2, 7)),
            pltpu.SemaphoreType.DMA((2, messages)),
            pltpu.SemaphoreType.DMA((2, messages)),
        ],
        compiler_params=pltpu.CompilerParams(
            collective_id=0, has_side_effects=True, vmem_limit_bytes=52 * 1024 * 1024
        ),
        cost_estimate=pl.CostEstimate(
            flops=6 * 4 * 2 * KDIM * KDIM * 512, bytes_accessed=10_000_000, transcendentals=0
        ),
        name="filter_twice",
    )(
        filter_window,
        record_target,
        coarse_states,
        padded_table(),
        mass_scale,
        potential,
        cell_matrix,
    )
    states = jnp.dot(
        filtered.reshape(-1, STATES),
        inverse.T,
        precision=lax.Precision.HIGH,
        preferred_element_type=F32,
    )
    return (states.reshape(filtered.shape), gram_matrix)


def solution(mesh):
    in_specs = (
        P(("dx", "dy"), None, None),
        P(("dx", "dy")),
        P(),
        P("dx", "dy", None),
        P("dx", "dy", None),
        P(),
    )
    out_specs = (P("dx", "dy", None, None), P())
    return jax.shard_map(local, mesh=mesh, in_specs=in_specs, out_specs=out_specs, check_vma=False)
```

```python
import functools

import jax
import jax.numpy as jnp
import numpy as np
from jax import lax
from jax.experimental import pallas as pl
from jax.experimental.pallas import tpu as pltpu
from jax.sharding import PartitionSpec as P

ORDER = 6
COARSE_ORDER = 4
CHEB_DEGREE = 3
POINTS = ORDER + 1
COUNT_Z = 4
SLOT = 8
COLUMN = COUNT_Z * SLOT
ROWS = 12
STATES = 128
PAIRS = 4
KDIM = POINTS * SLOT * SLOT
FACE = SLOT * SLOT
DEPTH = COUNT_Z * ORDER
PAIR = 2 * DEPTH
LINES = ROWS // 2
CELLS = 16
CAPACITY = CELLS // 2
COARSE_ROWS = 128
MESH = pl.DeviceIdType.MESH
F32 = jnp.float32
BF16 = jnp.bfloat16


def node_points(degree_value):
    return -np.cos(np.pi * np.arange(degree_value + 1) / degree_value)


def lagrange_table(fine_degree, coarse_degree):
    targets = node_points(fine_degree)
    sources = node_points(coarse_degree)
    matrix = np.ones((fine_degree + 1, coarse_degree + 1))
    for p in range(coarse_degree + 1):
        for m in range(coarse_degree + 1):
            if m != p:
                matrix[:, p] = matrix[:, p] * (targets - sources[m]) / (sources[p] - sources[m])
    owned_rows = matrix[:fine_degree]
    first = owned_rows[:, None, None, :, None, None]
    second = owned_rows[None, :, None, None, :, None]
    third = owned_rows[None, None, :, None, None, :]
    product = first * second * third
    return product.reshape(fine_degree**3, (coarse_degree + 1) ** 3)


def cut_index(value, size):
    assert size & (size - 1) == 0
    return lax.shift_right_logical(value, size.bit_length() - 1), value & (size - 1)


def row_in_slot(shape, axis):
    return lax.broadcasted_iota(jnp.int32, shape, axis) % SLOT


def dot_nn(a, b):
    return lax.dot_general(a, b, (((1,), (0,)), ((), ())), preferred_element_type=F32)


def dot_tn(a, b):
    return lax.dot_general(a, b, (((0,), (0,)), ((), ())), preferred_element_type=F32)


def dot_nt(a, b):
    return lax.dot_general(a, b, (((1,), (1,)), ((), ())), preferred_element_type=F32)


def split_two(value):
    high = value.astype(BF16)
    return high, (value - high.astype(F32)).astype(BF16)


def split_three(value):
    high = value.astype(BF16)
    rest = value - high.astype(F32)
    middle = rest.astype(BF16)
    return high, middle, (rest - middle.astype(F32)).astype(BF16)


def factor_rows(work):
    size = STATES
    sub = lax.broadcasted_iota(jnp.int32, (SLOT, size), 0)
    lane = lax.broadcasted_iota(jnp.int32, (SLOT, size), 1)

    def panel(j, carry):
        base = pl.multiple_of(j * SLOT, SLOT)
        left = work[pl.ds(base, SLOT), 0:size]
        right = work[pl.ds(base, SLOT), size : 2 * size]
        turned = pltpu.roll(left, lax.rem(size - base, size), 1)
        columns = [jnp.broadcast_to(turned[:, m : m + 1], (SLOT, size)) for m in range(SLOT)]
        for m in range(SLOT):
            pivot = jnp.broadcast_to(columns[m][m : m + 1, :], (SLOT, size))
            scale = lax.rsqrt(pivot)
            scale = scale * (1.5 - 0.5 * pivot * scale * scale)
            below = sub > m
            at = sub == m
            coef = columns[m] * scale
            row_left = jnp.broadcast_to(left[m : m + 1, :], (SLOT, size)) * scale
            row_right = jnp.broadcast_to(right[m : m + 1, :], (SLOT, size)) * scale
            for n in range(m + 1, SLOT):
                entry = jnp.broadcast_to(columns[n][m : m + 1, :], (SLOT, size)) * scale
                columns[n] = jnp.where(below, columns[n] - coef * entry, columns[n])
            left = jnp.where(below, left - coef * row_left, jnp.where(at, row_left, left))
            right = jnp.where(below, right - coef * row_right, jnp.where(at, row_right, right))
        work[pl.ds(base, SLOT), 0:size] = left
        work[pl.ds(base, SLOT), size : 2 * size] = right
        later = jnp.where(lane >= base + SLOT, left, 0.0)
        l1, l2, l3 = [v.astype(F32) for v in split_three(later)]
        both = jnp.concatenate([left, right], axis=1)
        b1, b2, b3 = [v.astype(F32) for v in split_three(both)]
        lhs = jnp.concatenate([l1, l1, l2, l1, l3, l2], axis=0).astype(BF16)
        rhs = jnp.concatenate([b1, b2, b1, b3, b1, b2], axis=0).astype(BF16)
        work[...] = work[...] - dot_tn(lhs, rhs)
        return carry

    lax.fori_loop(0, size // SLOT, panel, 0)


def filter_kernel(
    size_x,
    size_y,
    node_total,
    window,
    targets,
    coarse,
    table_any,
    mass_any,
    pot_any,
    matrix_any,
    filtered_out,
    inverse_out,
    gram_out,
    mass,
    pot,
    matrix,
    from_x,
    from_y,
    from_xy,
    shrink,
    grow,
    grow_own,
    target_tile,
    table,
    mass_in,
    pot_in,
    cell_matrix,
    filtered,
    slots,
    arrived,
    target_in,
    target_list,
    block,
    total,
    rhs,
    rhs_two,
    rhs_taken,
    send_x,
    send_y,
    take_x,
    take_y,
    back_x,
    back_y,
    back_c,
    got_x,
    got_y,
    got_c,
    split,
    partial,
    piece_in,
    ring_in,
    gram_sum,
    work,
    target_send,
    target_recv,
    list_sems,
    record_send,
    record_recv,
    store_sem,
    fetch_sems,
    send_sems,
    recv_sems,
    sum_send,
    sum_recv,
):
    me_x = lax.axis_index("dx")
    me_y = lax.axis_index("dy")

    def at(step_x, step_y):
        return (lax.rem(me_x + step_x + size_x, size_x), lax.rem(me_y + step_y + size_y, size_y))

    partners = [at(0, d) for d in range(1, size_y)] + [at(d, 0) for d in range(1, size_x)]
    partners += [at(1, 1), at(-1, -1), at(1, -1), at(-1, 1)]
    barrier = pltpu.get_barrier_semaphore()
    for partner in partners:
        pl.semaphore_signal(barrier, inc=1, device_id=partner, device_id_type=MESH)
    fetches = [
        pltpu.make_async_copy(src, dst, fetch_sems.at[i])
        for i, (src, dst) in enumerate(
            [
                (matrix_any, cell_matrix),
                (mass_any, mass_in),
                (pot_any, pot_in),
                (table_any, table),
            ]
        )
    ]
    for fetch in fetches:
        fetch.start()
    steps = (None, (0, 1), (1, 0), (1, 1))
    ranks = []
    counts = [0, 0, 0, 0]
    for r in range(CELLS):
        device = cut_index(targets[r], CELLS)[0]
        to_x, to_y = cut_index(device, size_y)
        step_x = (to_x - me_x + size_x) & (size_x - 1)
        step_y = (to_y - me_y + size_y) & (size_y - 1)
        bucket = 2 * step_x + step_y
        rank = 0
        for index in range(4):
            rank = jnp.where(bucket == index, counts[index], rank)
            counts[index] = jnp.where(bucket == index, counts[index] + 1, counts[index])
        ranks.append(bucket * CAPACITY + rank)

    def record_of(slot):
        found = 0
        for r in range(CELLS):
            found = jnp.where(ranks[r] == slot, r, found)
        return found & (CELLS - 1)

    last = COARSE_ROWS - 16
    for index in range(3):
        slots[index, :, last:COARSE_ROWS] = jnp.zeros((CAPACITY, 16, STATES), BF16)
    arrived[0:CAPACITY, last:COARSE_ROWS] = jnp.zeros((CAPACITY, 16, STATES), BF16)
    coarse_count = coarse.shape[1]
    tile_lane = lax.broadcasted_iota(jnp.int32, (SLOT, STATES), 1)
    tile = jnp.zeros((SLOT, STATES), jnp.int32)
    for r in range(CELLS):
        tile = jnp.where(tile_lane == r, targets[r], tile)
    target_tile[...] = tile
    pl.semaphore_wait(barrier, len(partners))
    target_copies, record_copies = {}, {}
    for index in (3, 2, 1):
        target_copies[index] = pltpu.make_async_remote_copy(
            src_ref=target_tile,
            dst_ref=target_in.at[index - 1],
            send_sem=target_send.at[index - 1],
            recv_sem=target_recv.at[index - 1],
            device_id=at(*steps[index]),
            device_id_type=MESH,
        )
        target_copies[index].start()
    for index in (3, 2, 1):
        for k in range(CAPACITY):
            slots[index - 1, k, 0:coarse_count] = coarse[record_of(index * CAPACITY + k)]
        record_copies[index] = pltpu.make_async_remote_copy(
            src_ref=slots.at[index - 1],
            dst_ref=arrived.at[pl.ds(index * CAPACITY, CAPACITY)],
            send_sem=record_send.at[index - 1],
            recv_sem=record_recv.at[index - 1],
            device_id=at(*steps[index]),
            device_id_type=MESH,
        )
        record_copies[index].start()
    for k in range(CAPACITY):
        arrived[k, 0:coarse_count] = coarse[record_of(k)]

    for fetch in fetches:
        fetch.wait()
    place_nodes(mass_in, pot_in, mass, pot)
    spread_matrix(cell_matrix, matrix, from_x, from_y, from_xy)
    line_tables(shrink, grow, grow_own)
    block[1] = jnp.zeros(block.shape[1:], F32)

    for index in (3, 2, 1):
        target_copies[index].wait()
    lists = [
        pltpu.make_async_copy(target_in.at[i], target_list.at[i], list_sems.at[i]) for i in range(3)
    ]
    for copy in lists:
        copy.start()
    for copy in lists:
        copy.wait()
    own = me_x * size_y + me_y
    places = [0] * CELLS
    for index in range(4):
        seen = 0
        for r in range(CELLS):
            target = targets[r] if index == 0 else target_list[index - 1, 0, r]
            device, cell = cut_index(target, CELLS)
            hit = device == own
            cell = jnp.where(hit, cell, -1)
            slot = index * CAPACITY + seen
            for g in range(CELLS):
                places[g] = jnp.where(cell == g, slot, places[g])
            seen = jnp.where(hit, seen + 1, seen)
    places = [p & (4 * CAPACITY - 1) for p in places]
    for index in (3, 2, 1):
        record_copies[index].wait()
    slot_row = row_in_slot((COLUMN, STATES), 0)
    for e in range(2):
        for f in range(2):
            for h in range(COUNT_Z):
                rhs[0:COARSE_ROWS, h * STATES : (h + 1) * STATES] = arrived[
                    places[(2 * e + f) * COUNT_Z + h]
                ]
            fine = dot_nn(table[...], rhs[0:COARSE_ROWS, :]).astype(BF16).astype(F32)
            for a in range(ORDER):
                for b in range(ORDER):
                    first = (a * ORDER + b) * SLOT
                    lines = [
                        fine[first : first + SLOT, h * STATES : (h + 1) * STATES]
                        for h in range(COUNT_Z)
                    ]
                    lines = jnp.concatenate(lines, axis=0)
                    again = pltpu.roll(lines, COLUMN - SLOT + ORDER, 0)
                    block[0, e * ORDER + a, f * ORDER + b] = jnp.where(
                        slot_row == ORDER, again, lines
                    )

    low = window[0]
    high = window[1]
    center = (low + high) / 2.0
    radius = (high - low) / 2.0

    def remote(turn, index, src, dst, step_x, step_y):
        return pltpu.make_async_remote_copy(
            src_ref=src,
            dst_ref=dst,
            send_sem=send_sems.at[turn, index],
            recv_sem=recv_sems.at[turn, index],
            device_id=at(step_x, step_y),
            device_id_type=MESH,
        )

    zeros = jnp.zeros((SLOT, STATES), F32)

    def pack(first, second):
        return jnp.concatenate([first, second], axis=0).astype(BF16)

    def add_product(product, e, f, points_x, points_y, written):
        for a in range(points_x):
            for b in range(points_y):
                first = (a * SLOT + b) * SLOT
                x, y = e * ORDER + a, f * ORDER + b
                for h in range(COUNT_Z):
                    rows = slice(h * SLOT, (h + 1) * SLOT)
                    part = product[first : first + SLOT, h * STATES : (h + 1) * STATES]
                    if (x, y) in written:
                        part = part + total[x, y, rows]
                    total[x, y, rows] = part
                written.add((x, y))

    def gather(q, e, f, out, lane):
        points_x = POINTS if e == 0 else ORDER
        for a in range(points_x):
            x = e * ORDER + a
            for h in range(COUNT_Z):
                rows = slice(h * SLOT, (h + 1) * SLOT)
                chunks = []
                for b in range(POINTS):
                    y = f * ORDER + b
                    own = y < ROWS
                    chunks.append(mass[x, y, rows] * block[q, x, y, rows] if own else zeros)
                chunks.append(chunks[0] if f == 0 else zeros)
                for i in range(PAIRS):
                    tile = pack(chunks[2 * i], chunks[2 * i + 1])
                    copies = [a, POINTS] if (a == 0 and e == 0) else [a]
                    for place in copies:
                        first = (place * PAIRS + i) * 2 * SLOT
                        lanes = slice(lane + h * STATES, lane + (h + 1) * STATES)
                        out[first : first + 2 * SLOT, lanes] = tile

    def taken_rows(base, lines, h):
        chunks = [line[h * SLOT : (h + 1) * SLOT] if line is not None else zeros for line in lines]
        for i in range(PAIRS):
            first = base + i * 2 * SLOT
            rhs_taken[first : first + 2 * SLOT, h * STATES : (h + 1) * STATES] = pack(
                chunks[2 * i], chunks[2 * i + 1]
            )

    def taken_column(e, f, factor, runs, points_x, points_y, written):
        for index, lines in enumerate(runs):
            for h in range(COUNT_Z):
                taken_rows(index * FACE, lines, h)
        depth = FACE * len(runs)
        product = dot_nn(factor[:, 0:depth], rhs_taken[0:depth, :])
        add_product(product, e, f, points_x, points_y, written)

    def narrow(lines, out):
        wide = lines.astype(BF16).reshape(LINES, 2 * COLUMN, STATES)
        wide = jnp.concatenate([wide[i] for i in range(LINES)], axis=1)
        packed = dot_nn(shrink[...], wide).astype(BF16)
        for i in range(LINES):
            out[i] = packed[:, i * STATES : (i + 1) * STATES]

    def widen(pairs, rows_of_slot):
        wide = dot_nn(rows_of_slot[...], jnp.concatenate(pairs, axis=1))
        lines = []
        for i in range(len(pairs)):
            for half in range(2):
                lines.append(
                    wide[half * COLUMN : (half + 1) * COLUMN, i * STATES : (i + 1) * STATES]
                )
        return lines

    def folded(raw):
        axis = raw.ndim - 2
        first = row_in_slot(raw.shape, axis) == 0
        return raw + jnp.where(first, pltpu.roll(raw, SLOT - ORDER, axis), 0.0)

    def finish(q, index, alpha, beta):
        raw = total[index]
        slot_row = row_in_slot(raw.shape, 1)
        summed = folded(raw)
        again = pltpu.roll(summed, COLUMN - SLOT + ORDER, 1)
        full = jnp.where(slot_row < ORDER, summed, jnp.where(slot_row == ORDER, again, 0.0))
        value = block[(q,) + index]
        result = mass[index] * full + (pot[index] - center) * value
        block[(1 - q,) + index] = alpha * result - beta * block[(1 - q,) + index]

    def one_apply(k, p):
        q = lax.rem(p * CHEB_DEGREE + k, 2)
        first = k == 0
        alpha = jnp.where(first, 1.0, 2.0) / radius
        beta = jnp.where(first, 0.0, 1.0)
        quarter = LINES // 2
        half = pl.ds(quarter, quarter)
        values = [
            remote(q, 0, send_x, take_x.at[q, pl.ds(quarter, LINES)], -1, 0),
            remote(q, 1, send_x.at[half], take_x.at[q, pl.ds(0, quarter)], -1, 1),
            remote(
                q, 2, send_x.at[pl.ds(0, 1)], take_x.at[q, pl.ds(quarter + LINES, 1)], -1, -1
            ),
            remote(q, 3, send_y.at[half], take_y.at[q, pl.ds(0, quarter)], 1, -1),
            remote(q, 4, send_y, take_y.at[q, pl.ds(quarter, LINES)], 0, -1),
        ]
        sum_x = remote(q, 5, back_x, got_x.at[q], 1, 0)
        sum_y = remote(q, 6, back_y, got_y.at[q], 0, 1)
        sum_c = remote(q, 7, back_c, got_c.at[q], 1, 1)
        narrow(mass[0, 0:ROWS] * block[q, 0, 0:ROWS], send_x)
        for copy in values[0:3]:
            copy.start()
        narrow(mass[0:ROWS, 0] * block[q, 0:ROWS, 0], send_y)
        for copy in values[3:5]:
            copy.start()
        written = set()
        width = COUNT_Z * STATES
        inner = FACE * ORDER
        gather(q, 1, 0, rhs_two, 0)
        gather(q, 1, 1, rhs_two, width)
        face = dot_nn(matrix[inner : inner + FACE, 0:inner], rhs_two[...])

        def face_line(f, b):
            parts = [
                face[b * SLOT : (b + 1) * SLOT, f * width + h * STATES : f * width + (h + 1) * STATES]
                for h in range(COUNT_Z)
            ]
            return jnp.concatenate(parts, axis=0)

        lines = [face_line(0, b) for b in range(ORDER)]
        lines.append(face_line(0, ORDER) + face_line(1, 0))
        lines += [face_line(1, b) for b in range(1, ORDER)]
        narrow(folded(jnp.stack(lines)), back_x)
        sum_x.start()
        back_c[...] = face_line(1, ORDER).astype(BF16)
        sum_c.start()
        product = dot_nn(matrix[0:inner, 0:inner], rhs_two[:, width : 2 * width])
        add_product(product, 1, 1, ORDER, POINTS, written)
        gather(q, 0, 1, rhs, 0)
        add_product(dot_nn(matrix[...], rhs[...]), 0, 1, POINTS, POINTS, written)
        narrow(folded(total[0:ROWS, ROWS]), back_y)
        sum_y.start()
        product = dot_nn(matrix[0:inner, 0:inner], rhs_two[:, 0:width])
        add_product(product, 1, 0, ORDER, POINTS, written)
        gather(q, 0, 0, rhs, 0)
        add_product(dot_nn(matrix[...], rhs[...]), 0, 0, POINTS, POINTS, written)
        for copy in values:
            copy.wait()
        along_x = widen([take_x[q, i] for i in range(quarter + LINES + 1)], grow)
        along_y = widen([take_y[q, i] for i in range(quarter + LINES)], grow)
        last = 2 * ORDER
        none = [None]
        taken_column(
            1,
            1,
            from_xy,
            [along_x[last : last + POINTS] + none, along_y[last:] + none * 2],
            ORDER,
            ORDER,
            written,
        )
        taken_column(
            1,
            0,
            from_x,
            [along_x[ORDER : last + 1] + none, along_x[0:POINTS] + none],
            ORDER,
            POINTS,
            written,
        )
        taken_column(
            0,
            1,
            from_y,
            [along_y[ORDER : last + 1] + none, along_y[0:POINTS] + none],
            POINTS,
            ORDER,
            written,
        )

        def interior(x, carry):
            finish(q, (x, pl.ds(1, ROWS - 1)), alpha, beta)
            return carry

        lax.fori_loop(1, ROWS, interior, 0)
        for copy in (sum_c, sum_y, sum_x):
            copy.wait()
        total[0, 0] += got_c[q].astype(F32)
        for x, line in enumerate(widen([got_y[q, i] for i in range(LINES)], grow_own)):
            total[x, 0] += line
        for y, line in enumerate(widen([got_x[q, i] for i in range(LINES)], grow_own)):
            total[0, y] += line
        finish(q, (0, slice(0, ROWS)), alpha, beta)
        finish(q, (slice(1, ROWS), 0), alpha, beta)

    def sum_everywhere(p):
        share = STATES // size_y

        def move(index, src, dst, device):
            return pltpu.make_async_remote_copy(
                src_ref=src,
                dst_ref=dst,
                send_sem=sum_send.at[p, index],
                recv_sem=sum_recv.at[p, index],
                device_id=device,
                device_id_type=MESH,
            )

        def rows_of(owner):
            return pl.ds(pl.multiple_of(owner * share, SLOT), share)

        mine = rows_of(me_y)
        copies = []
        for d in range(1, size_y):
            device = at(0, d)
            copies.append(
                move(d - 1, partial.at[rows_of(device[1])], piece_in.at[p, d - 1], device)
            )
        for copy in copies:
            copy.start()
        for copy in copies:
            copy.wait()
        piece = partial[mine, :]
        for d in range(1, size_y):
            piece = piece + piece_in[p, d - 1]
        ring_in[p, me_x] = piece
        copies = []
        for d in range(1, size_x):
            copies.append(
                move(size_y + d - 2, ring_in.at[p, me_x], ring_in.at[p, me_x], at(d, 0))
            )
        for copy in copies:
            copy.start()
        for copy in copies:
            copy.wait()
        piece = ring_in[p, 0]
        for d in range(1, size_x):
            piece = piece + ring_in[p, d]
        gram_sum[p, mine] = piece / node_total
        copies = []
        for d in range(1, size_y):
            copies.append(
                move(
                    size_y + size_x + d - 3, gram_sum.at[p, mine], gram_sum.at[p, mine], at(0, d)
                )
            )
        for copy in copies:
            copy.start()
        for copy in copies:
            copy.wait()

    def one_pass(p, carry):
        def step(k, inner):
            one_apply(k, p)
            return inner

        lax.fori_loop(0, CHEB_DEGREE, step, 0)
        q = lax.rem((p + 1) * CHEB_DEGREE, 2)

        def divide(x, inner):
            value = block[q, x, 0:ROWS]
            value = jnp.concatenate(
                [value[:, h * SLOT : h * SLOT + ORDER] for h in range(COUNT_Z)], axis=1
            )

            @pl.when(p == 1)
            def _():
                filtered[x] = value

            high_part, low_part = split_two(value.reshape(ROWS * DEPTH, STATES))
            rows = pl.ds(pl.multiple_of(x * ROWS * DEPTH, ROWS * DEPTH), ROWS * DEPTH)
            split[rows, 0:STATES] = high_part
            split[rows, STATES : 2 * STATES] = low_part
            return inner

        lax.fori_loop(0, ROWS, divide, 0)

        @pl.when(p == 1)
        def _():
            pltpu.make_async_copy(filtered, filtered_out, store_sem).start()

        products = dot_tn(split[:, 0:STATES], split[...])
        cross = products[:, STATES : 2 * STATES]
        partial[...] = products[:, 0:STATES] + cross + cross.T
        sum_everywhere(p)
        whole = gram_sum[p]
        work[:, 0:STATES] = whole
        diagonal = lax.broadcasted_iota(jnp.int32, (STATES, STATES), 0) == lax.broadcasted_iota(
            jnp.int32, (STATES, STATES), 1
        )
        work[:, STATES : 2 * STATES] = jnp.where(diagonal, 1.0, 0.0)
        factor_rows(work)
        inverse = work[:, STATES : 2 * STATES]
        gram_out[...] = whole
        inverse_out[...] = inverse

        @pl.when(p == 0)
        def _():
            pair = stacked_inverse(inverse)

            def turn(x, inner):
                value = block[q, x, 0:ROWS].reshape(ROWS * COLUMN, STATES)
                block[q, x, 0:ROWS] = times_inverse(value, pair).reshape(ROWS, COLUMN, STATES)
                return inner

            lax.fori_loop(0, ROWS, turn, 0)

        return carry

    lax.fori_loop(0, 2, one_pass, 0)
    pltpu.make_async_copy(filtered, filtered_out, store_sem).wait()


def stacked_inverse(inverse):
    high, low = split_two(inverse)
    return jnp.concatenate(
        [jnp.concatenate([high, high], axis=1), jnp.concatenate([low, low], axis=1)], axis=0
    )


def times_inverse(value, pair):
    high, low = split_two(value)
    both = dot_nt(jnp.concatenate([high, low], axis=1), pair)
    return both[:, 0:STATES] + both[:, STATES : 2 * STATES]


def place_nodes(mass_in, pot_in, mass, pot):
    width = 3 * DEPTH
    row = lax.broadcasted_iota(jnp.int32, (COLUMN, width), 0)
    lane = lax.broadcasted_iota(jnp.int32, (COLUMN, width), 1)
    within = row % SLOT
    source = lax.rem((row // SLOT) * ORDER + within, DEPTH)
    pick = jnp.where((lax.rem(lane, DEPTH) == source) & (within < POINTS), 1.0, 0.0)
    ones = jnp.ones((width, STATES), BF16)

    def one(x, carry):
        for values, out in ((mass_in, mass), (pot_in, pot)):
            parts = [v.astype(F32) for v in split_three(values[x])]
            parts = jnp.concatenate(parts, axis=1)
            spread = [
                jnp.broadcast_to(parts[y : y + 1, :], (COLUMN, width)) * pick for y in range(ROWS)
            ]
            lines = dot_nn(jnp.concatenate(spread, axis=0).astype(BF16), ones)
            out[x, 0:ROWS] = lines.reshape(ROWS, COLUMN, STATES)
        return carry

    lax.fori_loop(0, ROWS, one, 0, unroll=2)
    mass[ROWS] = jnp.ones(mass.shape[1:], F32)
    mass[0:ROWS, ROWS] = jnp.ones((ROWS, COLUMN, STATES), F32)


def line_tables(shrink, grow, grow_own):
    row = lax.broadcasted_iota(jnp.int32, (PAIR, 2 * COLUMN), 0)
    col = lax.broadcasted_iota(jnp.int32, (PAIR, 2 * COLUMN), 1)
    z = row % DEPTH
    chosen = (row // DEPTH) * COLUMN + (z // ORDER) * SLOT + z % ORDER
    shrink[...] = jnp.where(col == chosen, 1.0, 0.0).astype(BF16)
    row = lax.broadcasted_iota(jnp.int32, (2 * COLUMN, PAIR), 0)
    col = lax.broadcasted_iota(jnp.int32, (2 * COLUMN, PAIR), 1)
    c = row % SLOT
    z = (((row // SLOT) % COUNT_Z) * ORDER + c) % DEPTH
    same = col == (row // COLUMN) * DEPTH + z
    grow[...] = jnp.where(same & (c < POINTS), 1.0, 0.0).astype(BF16)
    grow_own[...] = jnp.where(same & (c < ORDER), 1.0, 0.0).astype(BF16)


def spread_matrix(cell_matrix, matrix, from_x, from_y, from_xy):
    nodes = POINTS**3
    row = lax.broadcasted_iota(jnp.int32, (KDIM, nodes), 0)
    col = lax.broadcasted_iota(jnp.int32, (KDIM, nodes), 1)
    b = (row // SLOT) % SLOT
    c = row % SLOT
    source = (row // FACE) * POINTS * POINTS + b * POINTS + c
    pick = jnp.where((col == source) & (b < POINTS) & (c < POINTS), 1.0, 0.0).astype(BF16)
    half = dot_nn(pick, cell_matrix[...]).astype(BF16)
    full = dot_nt(half, pick)
    width = SLOT * FACE
    full = jnp.concatenate([full, jnp.zeros((KDIM, FACE), F32)], axis=1)
    lane = lax.broadcasted_iota(jnp.int32, (FACE, width), 1)
    at_x = lane // FACE == POINTS
    at_y = (lane // SLOT) % SLOT == POINTS

    def seen(rows, shift, mask):
        return jnp.where(mask[0 : rows.shape[0]], pltpu.roll(rows, shift, 1), 0.0)

    last_y = [full[a * FACE + ORDER * SLOT : a * FACE + POINTS * SLOT] for a in range(POINTS)]
    last_x = full[ORDER * FACE : POINTS * FACE]
    groups = []
    for a in range(POINTS):
        group = full[a * FACE : (a + 1) * FACE]
        first = group[0:SLOT] + seen(last_y[a], SLOT, at_y & (~at_x))
        if a == 0:
            first = first + seen(last_y[ORDER], FACE + SLOT, at_y & at_x)
        group = jnp.concatenate([first, group[SLOT:]], axis=0)
        if a == 0:
            group = group + seen(last_x, FACE, at_x & (~at_y))
        groups.append(group)
    matrix[...] = jnp.concatenate(groups, axis=0).astype(BF16)

    row = lax.broadcasted_iota(jnp.int32, (KDIM, FACE), 0)
    col = lax.broadcasted_iota(jnp.int32, (KDIM, FACE), 1)
    face_x = jnp.where(row == ORDER * FACE + col, 1.0, 0.0)
    face_y = jnp.where(row == (col // SLOT) * FACE + ORDER * SLOT + col % SLOT, 1.0, 0.0)
    faces = jnp.concatenate([face_x, face_y], axis=1).astype(BF16)
    both = dot_nn(full[:, 0:KDIM].astype(BF16), faces)
    from_xy[...] = both.astype(BF16)
    low = lax.broadcasted_iota(jnp.int32, (FACE, 2 * FACE), 1) < FACE
    groups = []
    for a in range(POINTS):
        group = both[a * FACE : (a + 1) * FACE]
        moved = jnp.concatenate(
            [group[ORDER * SLOT : POINTS * SLOT], jnp.zeros((FACE - SLOT, 2 * FACE), F32)], axis=0
        )
        groups.append(jnp.where(low, group, pltpu.roll(moved, FACE, 1)))
    from_x[...] = jnp.concatenate(groups, axis=0).astype(BF16)
    groups = []
    for a in range(POINTS):
        group = pltpu.roll(both[a * FACE : (a + 1) * FACE], FACE, 1)
        moved = both[ORDER * FACE : POINTS * FACE] if a == 0 else jnp.zeros_like(group)
        groups.append(jnp.where(low, group, moved))
    from_y[...] = jnp.concatenate(groups, axis=0).astype(BF16)


def padded_table():
    table = lagrange_table(ORDER, COARSE_ORDER).astype(np.float32)
    table = table.reshape(ORDER * ORDER, ORDER, -1)
    table = np.pad(table, ((0, 0), (0, SLOT - ORDER), (0, COARSE_ROWS - table.shape[-1])))
    return jnp.asarray(table.reshape(-1, COARSE_ROWS), F32).astype(BF16)


def local(coarse_states, record_target, cell_matrix, mass_scale, potential, filter_window):
    rows_x, rows_y, rows_z = mass_scale.shape
    size_x = lax.axis_size("dx")
    size_y = lax.axis_size("dy")
    node_total = float(rows_x * rows_y * rows_z * size_x * size_y)
    padded = (ROWS + 1, ROWS + 1, COLUMN, STATES)
    inside = (ROWS, ROWS, COLUMN, STATES)
    pair = (PAIR, STATES)
    face = (LINES,) + pair
    line = (COLUMN, STATES)
    share = STATES // size_y
    messages = 2 * size_y + size_x - 3
    vmem = pl.BlockSpec(memory_space=pltpu.VMEM)
    filtered, inverse, gram_matrix = pl.pallas_call(
        functools.partial(filter_kernel, size_x, size_y, node_total),
        out_shape=(
            jax.ShapeDtypeStruct((rows_x, rows_y, rows_z, STATES), F32),
            jax.ShapeDtypeStruct((STATES, STATES), F32),
            jax.ShapeDtypeStruct((STATES, STATES), F32),
        ),
        in_specs=[pl.BlockSpec(memory_space=pltpu.SMEM)] * 2
        + [vmem]
        + [pl.BlockSpec(memory_space=pl.ANY)] * 4,
        out_specs=(pl.BlockSpec(memory_space=pl.ANY), vmem, vmem),
        scratch_shapes=[
            pltpu.VMEM(padded, F32),
            pltpu.VMEM(inside, F32),
            pltpu.VMEM((KDIM, SLOT * FACE), BF16),
            pltpu.VMEM((KDIM, 2 * FACE), BF16),
            pltpu.VMEM((KDIM, 2 * FACE), BF16),
            pltpu.VMEM((KDIM, 2 * FACE), BF16),
            pltpu.VMEM((PAIR, 2 * COLUMN), BF16),
            pltpu.VMEM((2 * COLUMN, PAIR), BF16),
            pltpu.VMEM((2 * COLUMN, PAIR), BF16),
            pltpu.VMEM((SLOT, STATES), jnp.int32),
            pltpu.VMEM((ORDER * ORDER * SLOT, COARSE_ROWS), BF16),
            pltpu.VMEM(mass_scale.shape, F32),
            pltpu.VMEM(potential.shape, F32),
            pltpu.VMEM(cell_matrix.shape, BF16),
            pltpu.VMEM((rows_x, rows_y, rows_z, STATES), F32),
            pltpu.VMEM((3, CAPACITY, COARSE_ROWS, STATES), BF16),
            pltpu.VMEM((4 * CAPACITY, COARSE_ROWS, STATES), BF16),
            pltpu.VMEM((3, SLOT, STATES), jnp.int32),
            pltpu.SMEM((3, SLOT, STATES), jnp.int32),
            pltpu.VMEM((2,) + padded, F32),
            pltpu.VMEM(padded, F32),
            pltpu.VMEM((SLOT * FACE, COUNT_Z * STATES), BF16),
            pltpu.VMEM((ORDER * FACE, 2 * COUNT_Z * STATES), BF16),
            pltpu.VMEM((2 * FACE, COUNT_Z * STATES), BF16),
            pltpu.VMEM(face, BF16),
            pltpu.VMEM(face, BF16),
            pltpu.VMEM((2, LINES // 2 + LINES + 1) + pair, BF16),
            pltpu.VMEM((2, LINES // 2 + LINES) + pair, BF16),
            pltpu.VMEM(face, BF16),
            pltpu.VMEM(face, BF16),
            pltpu.VMEM(line, BF16),
            pltpu.VMEM((2,) + face, BF16),
            pltpu.VMEM((2,) + face, BF16),
            pltpu.VMEM((2,) + line, BF16),
            pltpu.VMEM((ROWS * ROWS * DEPTH, 2 * STATES), BF16),
            pltpu.VMEM((STATES, STATES), F32),
            pltpu.VMEM((2, size_y - 1, share, STATES), F32),
            pltpu.VMEM((2, size_x, share, STATES), F32),
            pltpu.VMEM((2, STATES, STATES), F32),
            pltpu.VMEM((STATES, 2 * STATES), F32),
            pltpu.SemaphoreType.DMA((3,)),
            pltpu.SemaphoreType.DMA((3,)),
            pltpu.SemaphoreType.DMA((3,)),
            pltpu.SemaphoreType.DMA((3,)),
            pltpu.SemaphoreType.DMA((3,)),
            pltpu.SemaphoreType.DMA,
            pltpu.SemaphoreType.DMA((4,)),
            pltpu.SemaphoreType.DMA((2, 8)),
            pltpu.SemaphoreType.DMA((2, 8)),
            pltpu.SemaphoreType.DMA((2, messages)),
            pltpu.SemaphoreType.DMA((2, messages)),
        ],
        compiler_params=pltpu.CompilerParams(
            collective_id=0, has_side_effects=True, vmem_limit_bytes=52 * 1024 * 1024
        ),
        cost_estimate=pl.CostEstimate(
            flops=6 * 4 * 2 * KDIM * KDIM * 512, bytes_accessed=10_000_000, transcendentals=0
        ),
        name="filter_twice",
    )(
        filter_window,
        record_target,
        coarse_states,
        padded_table(),
        mass_scale,
        potential,
        cell_matrix,
    )
    states = jnp.dot(
        filtered.reshape(-1, STATES),
        inverse.T,
        precision=lax.Precision.HIGH,
        preferred_element_type=F32,
    )
    return (states.reshape(filtered.shape), gram_matrix)


def solution(mesh):
    in_specs = (
        P(("dx", "dy"), None, None),
        P(("dx", "dy")),
        P(),
        P("dx", "dy", None),
        P("dx", "dy", None),
        P(),
    )
    out_specs = (P("dx", "dy", None, None), P())
    return jax.shard_map(local, mesh=mesh, in_specs=in_specs, out_specs=out_specs, check_vma=False)
```

```python
import functools

import jax
import jax.numpy as jnp
import numpy as np
from jax import lax
from jax.experimental import pallas as pl
from jax.experimental.pallas import tpu as pltpu
from jax.sharding import PartitionSpec as P

ORDER = 6
COARSE_ORDER = 4
CHEB_DEGREE = 3
POINTS = ORDER + 1
COUNT_Z = 4
SLOT = 8
COLUMN = COUNT_Z * SLOT
ROWS = 12
STATES = 128
PAIRS = 4
KDIM = POINTS * SLOT * SLOT
FACE = SLOT * SLOT
DEPTH = COUNT_Z * ORDER
PAIR = 2 * DEPTH
LINES = ROWS // 2
CELLS = 16
PANEL = 16
CAPACITY = CELLS // 2
COARSE_ROWS = 128
MESH = pl.DeviceIdType.MESH
F32 = jnp.float32
BF16 = jnp.bfloat16


def node_points(degree_value):
    return -np.cos(np.pi * np.arange(degree_value + 1) / degree_value)


def lagrange_table(fine_degree, coarse_degree):
    targets = node_points(fine_degree)
    sources = node_points(coarse_degree)
    matrix = np.ones((fine_degree + 1, coarse_degree + 1))
    for p in range(coarse_degree + 1):
        for m in range(coarse_degree + 1):
            if m != p:
                matrix[:, p] = matrix[:, p] * (targets - sources[m]) / (sources[p] - sources[m])
    owned_rows = matrix[:fine_degree]
    first = owned_rows[:, None, None, :, None, None]
    second = owned_rows[None, :, None, None, :, None]
    third = owned_rows[None, None, :, None, None, :]
    product = first * second * third
    return product.reshape(fine_degree**3, (coarse_degree + 1) ** 3)


def cut_index(value, size):
    assert size & (size - 1) == 0
    return lax.shift_right_logical(value, size.bit_length() - 1), value & (size - 1)


def row_in_slot(shape, axis):
    return lax.broadcasted_iota(jnp.int32, shape, axis) % SLOT


def dot_nn(a, b):
    return lax.dot_general(a, b, (((1,), (0,)), ((), ())), preferred_element_type=F32)


def dot_tn(a, b):
    return lax.dot_general(a, b, (((0,), (0,)), ((), ())), preferred_element_type=F32)


def dot_nt(a, b):
    return lax.dot_general(a, b, (((1,), (1,)), ((), ())), preferred_element_type=F32)


def split_two(value):
    high = value.astype(BF16)
    return high, (value - high.astype(F32)).astype(BF16)


def split_three(value):
    high = value.astype(BF16)
    rest = value - high.astype(F32)
    middle = rest.astype(BF16)
    return high, middle, (rest - middle.astype(F32)).astype(BF16)


def factor_rows(work):
    size = STATES
    sub = lax.broadcasted_iota(jnp.int32, (PANEL, size), 0)
    lane = lax.broadcasted_iota(jnp.int32, (PANEL, size), 1)

    def panel(j, carry):
        base = pl.multiple_of(j * PANEL, PANEL)
        left = work[pl.ds(base, PANEL), 0:size]
        right = work[pl.ds(base, PANEL), size : 2 * size]
        turned = pltpu.roll(left, lax.rem(size - base, size), 1)
        columns = [jnp.broadcast_to(turned[:, m : m + 1], (PANEL, size)) for m in range(PANEL)]
        for m in range(PANEL):
            pivot = jnp.broadcast_to(columns[m][m : m + 1, :], (PANEL, size))
            scale = lax.rsqrt(pivot)
            below = sub > m
            at = sub == m
            coef = columns[m] * scale
            row_left = jnp.broadcast_to(left[m : m + 1, :], (PANEL, size)) * scale
            row_right = jnp.broadcast_to(right[m : m + 1, :], (PANEL, size)) * scale
            for n in range(m + 1, PANEL):
                entry = jnp.broadcast_to(columns[n][m : m + 1, :], (PANEL, size)) * scale
                columns[n] = jnp.where(below, columns[n] - coef * entry, columns[n])
            left = jnp.where(below, left - coef * row_left, jnp.where(at, row_left, left))
            right = jnp.where(below, right - coef * row_right, jnp.where(at, row_right, right))
        work[pl.ds(base, PANEL), 0:size] = left
        work[pl.ds(base, PANEL), size : 2 * size] = right
        later = jnp.where(lane >= base + PANEL, left, 0.0)
        l1, l2, l3 = [v.astype(F32) for v in split_three(later)]
        both = jnp.concatenate([left, right], axis=1)
        b1, b2, b3 = [v.astype(F32) for v in split_three(both)]
        lhs = jnp.concatenate([l1, l1, l2, l1, l3, l2], axis=0).astype(BF16)
        rhs = jnp.concatenate([b1, b2, b1, b3, b1, b2], axis=0).astype(BF16)
        work[...] = work[...] - dot_tn(lhs, rhs)
        return carry

    lax.fori_loop(0, size // PANEL, panel, 0)


def filter_kernel(
    size_x,
    size_y,
    node_total,
    window,
    targets,
    coarse,
    table_any,
    mass_any,
    pot_any,
    matrix_any,
    filtered_out,
    inverse_out,
    gram_out,
    mass,
    pot,
    matrix,
    from_x,
    from_y,
    from_xy,
    shrink,
    grow,
    grow_own,
    target_tile,
    table,
    mass_in,
    pot_in,
    cell_matrix,
    slots,
    arrived,
    target_in,
    target_list,
    block,
    total,
    rhs,
    rhs_two,
    rhs_taken,
    send_x,
    send_y,
    take_x,
    take_y,
    back_x,
    back_y,
    back_c,
    got_x,
    got_y,
    got_c,
    split,
    partial,
    piece_in,
    ring_in,
    gram_sum,
    work,
    target_send,
    target_recv,
    list_sems,
    record_send,
    record_recv,
    store_sem,
    fetch_sems,
    send_sems,
    recv_sems,
    sum_send,
    sum_recv,
):
    me_x = lax.axis_index("dx")
    me_y = lax.axis_index("dy")

    def at(step_x, step_y):
        return (lax.rem(me_x + step_x + size_x, size_x), lax.rem(me_y + step_y + size_y, size_y))

    partners = [at(0, d) for d in range(1, size_y)] + [at(d, 0) for d in range(1, size_x)]
    partners += [at(1, 1), at(-1, -1), at(1, -1), at(-1, 1)]
    barrier = pltpu.get_barrier_semaphore()
    for partner in partners:
        pl.semaphore_signal(barrier, inc=1, device_id=partner, device_id_type=MESH)
    fetches = [
        pltpu.make_async_copy(src, dst, fetch_sems.at[i])
        for i, (src, dst) in enumerate(
            [
                (matrix_any, cell_matrix),
                (mass_any, mass_in),
                (pot_any, pot_in),
                (table_any, table),
            ]
        )
    ]
    for fetch in fetches:
        fetch.start()
    steps = (None, (0, 1), (1, 0), (1, 1))
    ranks = []
    counts = [0, 0, 0, 0]
    for r in range(CELLS):
        device = cut_index(targets[r], CELLS)[0]
        to_x, to_y = cut_index(device, size_y)
        step_x = (to_x - me_x + size_x) & (size_x - 1)
        step_y = (to_y - me_y + size_y) & (size_y - 1)
        bucket = 2 * step_x + step_y
        rank = 0
        for index in range(4):
            rank = jnp.where(bucket == index, counts[index], rank)
            counts[index] = jnp.where(bucket == index, counts[index] + 1, counts[index])
        ranks.append(bucket * CAPACITY + rank)

    def record_of(slot):
        found = 0
        for r in range(CELLS):
            found = jnp.where(ranks[r] == slot, r, found)
        return found & (CELLS - 1)

    last = COARSE_ROWS - 16
    for index in range(3):
        slots[index, :, last:COARSE_ROWS] = jnp.zeros((CAPACITY, 16, STATES), BF16)
    arrived[0:CAPACITY, last:COARSE_ROWS] = jnp.zeros((CAPACITY, 16, STATES), BF16)
    coarse_count = coarse.shape[1]
    tile_lane = lax.broadcasted_iota(jnp.int32, (SLOT, STATES), 1)
    tile = jnp.zeros((SLOT, STATES), jnp.int32)
    for r in range(CELLS):
        tile = jnp.where(tile_lane == r, targets[r], tile)
    target_tile[...] = tile
    pl.semaphore_wait(barrier, len(partners))
    target_copies, record_copies = {}, {}
    for index in (3, 2, 1):
        target_copies[index] = pltpu.make_async_remote_copy(
            src_ref=target_tile,
            dst_ref=target_in.at[index - 1],
            send_sem=target_send.at[index - 1],
            recv_sem=target_recv.at[index - 1],
            device_id=at(*steps[index]),
            device_id_type=MESH,
        )
        target_copies[index].start()
    for index in (3, 2, 1):
        for k in range(CAPACITY):
            slots[index - 1, k, 0:coarse_count] = coarse[record_of(index * CAPACITY + k)]
        record_copies[index] = pltpu.make_async_remote_copy(
            src_ref=slots.at[index - 1],
            dst_ref=arrived.at[pl.ds(index * CAPACITY, CAPACITY)],
            send_sem=record_send.at[index - 1],
            recv_sem=record_recv.at[index - 1],
            device_id=at(*steps[index]),
            device_id_type=MESH,
        )
        record_copies[index].start()
    for k in range(CAPACITY):
        arrived[k, 0:coarse_count] = coarse[record_of(k)]

    for fetch in fetches:
        fetch.wait()
    place_nodes(mass_in, pot_in, mass, pot)
    spread_matrix(cell_matrix, matrix, from_x, from_y, from_xy)
    line_tables(shrink, grow, grow_own)
    block[1] = jnp.zeros(block.shape[1:], F32)

    for index in (3, 2, 1):
        target_copies[index].wait()
    lists = [
        pltpu.make_async_copy(target_in.at[i], target_list.at[i], list_sems.at[i]) for i in range(3)
    ]
    for copy in lists:
        copy.start()
    for copy in lists:
        copy.wait()
    own = me_x * size_y + me_y
    places = [0] * CELLS
    for index in range(4):
        seen = 0
        for r in range(CELLS):
            target = targets[r] if index == 0 else target_list[index - 1, 0, r]
            device, cell = cut_index(target, CELLS)
            hit = device == own
            cell = jnp.where(hit, cell, -1)
            slot = index * CAPACITY + seen
            for g in range(CELLS):
                places[g] = jnp.where(cell == g, slot, places[g])
            seen = jnp.where(hit, seen + 1, seen)
    places = [p & (4 * CAPACITY - 1) for p in places]
    for index in (3, 2, 1):
        record_copies[index].wait()
    slot_row = row_in_slot((COLUMN, STATES), 0)
    for e in range(2):
        for f in range(2):
            for h in range(COUNT_Z):
                rhs[0:COARSE_ROWS, h * STATES : (h + 1) * STATES] = arrived[
                    places[(2 * e + f) * COUNT_Z + h]
                ]
            fine = dot_nn(table[...], rhs[0:COARSE_ROWS, :]).astype(BF16).astype(F32)
            for a in range(ORDER):
                for b in range(ORDER):
                    first = (a * ORDER + b) * SLOT
                    lines = [
                        fine[first : first + SLOT, h * STATES : (h + 1) * STATES]
                        for h in range(COUNT_Z)
                    ]
                    lines = jnp.concatenate(lines, axis=0)
                    again = pltpu.roll(lines, COLUMN - SLOT + ORDER, 0)
                    block[0, e * ORDER + a, f * ORDER + b] = jnp.where(
                        slot_row == ORDER, again, lines
                    )

    low = window[0]
    high = window[1]
    center = (low + high) / 2.0
    radius = (high - low) / 2.0

    def remote(turn, index, src, dst, step_x, step_y):
        return pltpu.make_async_remote_copy(
            src_ref=src,
            dst_ref=dst,
            send_sem=send_sems.at[turn, index],
            recv_sem=recv_sems.at[turn, index],
            device_id=at(step_x, step_y),
            device_id_type=MESH,
        )

    zeros = jnp.zeros((SLOT, STATES), F32)

    def pack(first, second):
        return jnp.concatenate([first, second], axis=0).astype(BF16)

    def add_product(product, e, f, points_x, points_y, written):
        for a in range(points_x):
            for b in range(points_y):
                first = (a * SLOT + b) * SLOT
                x, y = e * ORDER + a, f * ORDER + b
                for h in range(COUNT_Z):
                    rows = slice(h * SLOT, (h + 1) * SLOT)
                    part = product[first : first + SLOT, h * STATES : (h + 1) * STATES]
                    if (x, y) in written:
                        part = part + total[x, y, rows]
                    total[x, y, rows] = part
                written.add((x, y))

    def gather(q, e, f, out, lane):
        points_x = POINTS if e == 0 else ORDER
        for a in range(points_x):
            x = e * ORDER + a
            for h in range(COUNT_Z):
                rows = slice(h * SLOT, (h + 1) * SLOT)
                chunks = []
                for b in range(POINTS):
                    y = f * ORDER + b
                    own = y < ROWS
                    chunks.append(mass[x, y, rows] * block[q, x, y, rows] if own else zeros)
                chunks.append(chunks[0] if f == 0 else zeros)
                for i in range(PAIRS):
                    tile = pack(chunks[2 * i], chunks[2 * i + 1])
                    copies = [a, POINTS] if (a == 0 and e == 0) else [a]
                    for place in copies:
                        first = (place * PAIRS + i) * 2 * SLOT
                        lanes = slice(lane + h * STATES, lane + (h + 1) * STATES)
                        out[first : first + 2 * SLOT, lanes] = tile

    def taken_rows(base, lines, h):
        chunks = [line[h * SLOT : (h + 1) * SLOT] if line is not None else zeros for line in lines]
        for i in range(PAIRS):
            first = base + i * 2 * SLOT
            rhs_taken[first : first + 2 * SLOT, h * STATES : (h + 1) * STATES] = pack(
                chunks[2 * i], chunks[2 * i + 1]
            )

    def taken_column(e, f, factor, runs, points_x, points_y, written):
        for index, lines in enumerate(runs):
            for h in range(COUNT_Z):
                taken_rows(index * FACE, lines, h)
        depth = FACE * len(runs)
        product = dot_nn(factor[:, 0:depth], rhs_taken[0:depth, :])
        add_product(product, e, f, points_x, points_y, written)

    def narrow(lines, out):
        wide = lines.astype(BF16).reshape(LINES, 2 * COLUMN, STATES)
        wide = jnp.concatenate([wide[i] for i in range(LINES)], axis=1)
        packed = dot_nn(shrink[...], wide).astype(BF16)
        for i in range(LINES):
            out[i] = packed[:, i * STATES : (i + 1) * STATES]

    def widen(pairs, rows_of_slot):
        wide = dot_nn(rows_of_slot[...], jnp.concatenate(pairs, axis=1))
        lines = []
        for i in range(len(pairs)):
            for half in range(2):
                lines.append(
                    wide[half * COLUMN : (half + 1) * COLUMN, i * STATES : (i + 1) * STATES]
                )
        return lines

    def folded(raw):
        axis = raw.ndim - 2
        first = row_in_slot(raw.shape, axis) == 0
        return raw + jnp.where(first, pltpu.roll(raw, SLOT - ORDER, axis), 0.0)

    def finish(q, index, alpha, beta):
        raw = total[index]
        slot_row = row_in_slot(raw.shape, 1)
        summed = folded(raw)
        again = pltpu.roll(summed, COLUMN - SLOT + ORDER, 1)
        full = jnp.where(slot_row < ORDER, summed, jnp.where(slot_row == ORDER, again, 0.0))
        value = block[(q,) + index]
        result = mass[index] * full + (pot[index] - center) * value
        block[(1 - q,) + index] = alpha * result - beta * block[(1 - q,) + index]

    def one_apply(t):
        q = t % 2
        first = (t % CHEB_DEGREE) == 0
        alpha = jnp.where(first, 1.0, 2.0) / radius
        beta = jnp.where(first, 0.0, 1.0)
        quarter = LINES // 2
        half = pl.ds(quarter, quarter)
        values = [
            remote(q, 0, send_x, take_x.at[q, pl.ds(quarter, LINES)], -1, 0),
            remote(q, 1, send_x.at[half], take_x.at[q, pl.ds(0, quarter)], -1, 1),
            remote(
                q, 2, send_x.at[pl.ds(0, 1)], take_x.at[q, pl.ds(quarter + LINES, 1)], -1, -1
            ),
            remote(q, 3, send_y.at[half], take_y.at[q, pl.ds(0, quarter)], 1, -1),
            remote(q, 4, send_y, take_y.at[q, pl.ds(quarter, LINES)], 0, -1),
        ]
        sum_x = remote(q, 5, back_x, got_x.at[q], 1, 0)
        sum_y = remote(q, 6, back_y, got_y.at[q], 0, 1)
        sum_c = remote(q, 7, back_c, got_c.at[q], 1, 1)
        narrow(mass[0, 0:ROWS] * block[q, 0, 0:ROWS], send_x)
        for copy in values[0:3]:
            copy.start()
        narrow(mass[0:ROWS, 0] * block[q, 0:ROWS, 0], send_y)
        for copy in values[3:5]:
            copy.start()
        written = set()
        width = COUNT_Z * STATES
        inner = FACE * ORDER
        gather(q, 1, 0, rhs_two, 0)
        gather(q, 1, 1, rhs_two, width)
        face = dot_nn(matrix[inner : inner + FACE, 0:inner], rhs_two[...])

        def face_line(f, b):
            parts = [
                face[b * SLOT : (b + 1) * SLOT, f * width + h * STATES : f * width + (h + 1) * STATES]
                for h in range(COUNT_Z)
            ]
            return jnp.concatenate(parts, axis=0)

        lines = [face_line(0, b) for b in range(ORDER)]
        lines.append(face_line(0, ORDER) + face_line(1, 0))
        lines += [face_line(1, b) for b in range(1, ORDER)]
        narrow(folded(jnp.stack(lines)), back_x)
        sum_x.start()
        back_c[...] = face_line(1, ORDER).astype(BF16)
        sum_c.start()
        product = dot_nn(matrix[0:inner, 0:inner], rhs_two[:, width : 2 * width])
        add_product(product, 1, 1, ORDER, POINTS, written)
        gather(q, 0, 1, rhs, 0)
        add_product(dot_nn(matrix[...], rhs[...]), 0, 1, POINTS, POINTS, written)
        narrow(folded(total[0:ROWS, ROWS]), back_y)
        sum_y.start()
        product = dot_nn(matrix[0:inner, 0:inner], rhs_two[:, 0:width])
        add_product(product, 1, 0, ORDER, POINTS, written)
        gather(q, 0, 0, rhs, 0)
        add_product(dot_nn(matrix[...], rhs[...]), 0, 0, POINTS, POINTS, written)

        @pl.when(t == CHEB_DEGREE)
        def _():
            gather_pieces(0)

        @pl.when(t == CHEB_DEGREE + 1)
        def _():
            gather_rows(0)

        for copy in values:
            copy.wait()
        along_x = widen([take_x[q, i] for i in range(quarter + LINES + 1)], grow)
        along_y = widen([take_y[q, i] for i in range(quarter + LINES)], grow)
        last = 2 * ORDER
        none = [None]
        taken_column(
            1,
            1,
            from_xy,
            [along_x[last : last + POINTS] + none, along_y[last:] + none * 2],
            ORDER,
            ORDER,
            written,
        )
        taken_column(
            1,
            0,
            from_x,
            [along_x[ORDER : last + 1] + none, along_x[0:POINTS] + none],
            ORDER,
            POINTS,
            written,
        )
        taken_column(
            0,
            1,
            from_y,
            [along_y[ORDER : last + 1] + none, along_y[0:POINTS] + none],
            POINTS,
            ORDER,
            written,
        )

        def interior(x, carry):
            finish(q, (x, pl.ds(1, ROWS - 1)), alpha, beta)
            return carry

        lax.fori_loop(1, ROWS, interior, 0)
        for copy in (sum_c, sum_y, sum_x):
            copy.wait()
        total[0, 0] += got_c[q].astype(F32)
        for x, line in enumerate(widen([got_y[q, i] for i in range(LINES)], grow_own)):
            total[x, 0] += line
        for y, line in enumerate(widen([got_x[q, i] for i in range(LINES)], grow_own)):
            total[0, y] += line
        finish(q, (0, slice(0, ROWS)), alpha, beta)
        finish(q, (slice(1, ROWS), 0), alpha, beta)

    share = STATES // size_y

    def move(p, index, src, dst, device):
        return pltpu.make_async_remote_copy(
            src_ref=src,
            dst_ref=dst,
            send_sem=sum_send.at[p, index],
            recv_sem=sum_recv.at[p, index],
            device_id=device,
            device_id_type=MESH,
        )

    def rows_of(owner):
        return pl.ds(pl.multiple_of(owner * share, SLOT), share)

    mine = rows_of(me_y)

    def piece_copies(p):
        copies = []
        for d in range(1, size_y):
            device = at(0, d)
            src = partial.at[rows_of(device[1])]
            copies.append(move(p, d - 1, src, piece_in.at[p, d - 1], device))
        return copies

    def ring_copies(p):
        own = ring_in.at[p, me_x]
        return [move(p, size_y + d - 2, own, own, at(d, 0)) for d in range(1, size_x)]

    def row_copies(p):
        own = gram_sum.at[p, mine]
        first = size_y + size_x - 3
        return [move(p, first + d, own, own, at(0, d)) for d in range(1, size_y)]

    def gather_pieces(p):
        for copy in piece_copies(p):
            copy.wait()
        piece = partial[mine, :]
        for d in range(1, size_y):
            piece = piece + piece_in[p, d - 1]
        ring_in[p, me_x] = piece
        for copy in ring_copies(p):
            copy.start()

    def gather_rows(p):
        for copy in ring_copies(p):
            copy.wait()
        piece = ring_in[p, 0]
        for d in range(1, size_x):
            piece = piece + ring_in[p, d]
        gram_sum[p, mine] = piece / node_total
        for copy in row_copies(p):
            copy.start()

    def begin_sum(p, q):
        def divide(x, inner):
            value = block[q, x, 0:ROWS]
            value = jnp.concatenate(
                [value[:, h * SLOT : h * SLOT + ORDER] for h in range(COUNT_Z)], axis=1
            )
            high_part, low_part = split_two(value.reshape(ROWS * DEPTH, STATES))
            rows = pl.ds(pl.multiple_of(x * ROWS * DEPTH, ROWS * DEPTH), ROWS * DEPTH)
            split[rows, 0:STATES] = high_part
            split[rows, STATES : 2 * STATES] = low_part
            split[rows, 2 * STATES : 3 * STATES] = high_part
            return inner

        lax.fori_loop(0, ROWS, divide, 0)
        products = dot_tn(split[:, 0:STATES], split[:, 0 : 2 * STATES])
        cross = products[:, STATES : 2 * STATES]
        partial[...] = products[:, 0:STATES] + cross + cross.T
        for copy in piece_copies(p):
            copy.start()

    def end_sum(p):
        for copy in row_copies(p):
            copy.wait()
        work[:, 0:STATES] = gram_sum[p]
        shape = (STATES, STATES)
        diagonal = lax.broadcasted_iota(jnp.int32, shape, 0) == lax.broadcasted_iota(
            jnp.int32, shape, 1
        )
        work[:, STATES : 2 * STATES] = jnp.where(diagonal, 1.0, 0.0)
        factor_rows(work)
        return work[:, STATES : 2 * STATES]

    def step(t, carry):
        @pl.when(t == CHEB_DEGREE)
        def _():
            begin_sum(0, CHEB_DEGREE % 2)

        one_apply(t)

        @pl.when(t == CHEB_DEGREE + 1)
        def _():
            pair = stacked_inverse(end_sum(0))

            def turn(x, inner):
                for index in range(2):
                    value = block[index, x, 0:ROWS].reshape(ROWS * COLUMN, STATES)
                    block[index, x, 0:ROWS] = times_inverse(value, pair).reshape(
                        ROWS, COLUMN, STATES
                    )
                return inner

            lax.fori_loop(0, ROWS, turn, 0)

        return carry

    lax.fori_loop(0, 2 * CHEB_DEGREE, step, 0)
    begin_sum(1, 0)
    store = pltpu.make_async_copy(split, filtered_out, store_sem)
    store.start()
    gather_pieces(1)
    gather_rows(1)
    inverse = end_sum(1)
    high_part, low_part = split_two(inverse)
    inverse_out[...] = jnp.concatenate([high_part, high_part, low_part], axis=1)
    gram_out[...] = gram_sum[1]
    store.wait()


def stacked_inverse(inverse):
    high, low = split_two(inverse)
    return jnp.concatenate(
        [jnp.concatenate([high, high], axis=1), jnp.concatenate([low, low], axis=1)], axis=0
    )


def times_inverse(value, pair):
    high, low = split_two(value)
    both = dot_nt(jnp.concatenate([high, low], axis=1), pair)
    return both[:, 0:STATES] + both[:, STATES : 2 * STATES]


def place_nodes(mass_in, pot_in, mass, pot):
    width = 3 * DEPTH
    row = lax.broadcasted_iota(jnp.int32, (COLUMN, width), 0)
    lane = lax.broadcasted_iota(jnp.int32, (COLUMN, width), 1)
    within = row % SLOT
    source = lax.rem((row // SLOT) * ORDER + within, DEPTH)
    pick = jnp.where((lax.rem(lane, DEPTH) == source) & (within < POINTS), 1.0, 0.0)
    ones = jnp.ones((width, STATES), BF16)

    def one(x, carry):
        for values, out in ((mass_in, mass), (pot_in, pot)):
            parts = [v.astype(F32) for v in split_three(values[x])]
            parts = jnp.concatenate(parts, axis=1)
            spread = [
                jnp.broadcast_to(parts[y : y + 1, :], (COLUMN, width)) * pick for y in range(ROWS)
            ]
            lines = dot_nn(jnp.concatenate(spread, axis=0).astype(BF16), ones)
            out[x, 0:ROWS] = lines.reshape(ROWS, COLUMN, STATES)
        return carry

    lax.fori_loop(0, ROWS, one, 0, unroll=2)
    mass[ROWS] = jnp.ones(mass.shape[1:], F32)
    mass[0:ROWS, ROWS] = jnp.ones((ROWS, COLUMN, STATES), F32)


def line_tables(shrink, grow, grow_own):
    row = lax.broadcasted_iota(jnp.int32, (PAIR, 2 * COLUMN), 0)
    col = lax.broadcasted_iota(jnp.int32, (PAIR, 2 * COLUMN), 1)
    z = row % DEPTH
    chosen = (row // DEPTH) * COLUMN + (z // ORDER) * SLOT + z % ORDER
    shrink[...] = jnp.where(col == chosen, 1.0, 0.0).astype(BF16)
    row = lax.broadcasted_iota(jnp.int32, (2 * COLUMN, PAIR), 0)
    col = lax.broadcasted_iota(jnp.int32, (2 * COLUMN, PAIR), 1)
    c = row % SLOT
    z = (((row // SLOT) % COUNT_Z) * ORDER + c) % DEPTH
    same = col == (row // COLUMN) * DEPTH + z
    grow[...] = jnp.where(same & (c < POINTS), 1.0, 0.0).astype(BF16)
    grow_own[...] = jnp.where(same & (c < ORDER), 1.0, 0.0).astype(BF16)


def spread_matrix(cell_matrix, matrix, from_x, from_y, from_xy):
    nodes = POINTS**3
    row = lax.broadcasted_iota(jnp.int32, (KDIM, nodes), 0)
    col = lax.broadcasted_iota(jnp.int32, (KDIM, nodes), 1)
    b = (row // SLOT) % SLOT
    c = row % SLOT
    source = (row // FACE) * POINTS * POINTS + b * POINTS + c
    pick = jnp.where((col == source) & (b < POINTS) & (c < POINTS), 1.0, 0.0).astype(BF16)
    half = dot_nn(pick, cell_matrix[...]).astype(BF16)
    full = dot_nt(half, pick)
    width = SLOT * FACE
    full = jnp.concatenate([full, jnp.zeros((KDIM, FACE), F32)], axis=1)
    lane = lax.broadcasted_iota(jnp.int32, (FACE, width), 1)
    at_x = lane // FACE == POINTS
    at_y = (lane // SLOT) % SLOT == POINTS

    def seen(rows, shift, mask):
        return jnp.where(mask[0 : rows.shape[0]], pltpu.roll(rows, shift, 1), 0.0)

    last_y = [full[a * FACE + ORDER * SLOT : a * FACE + POINTS * SLOT] for a in range(POINTS)]
    last_x = full[ORDER * FACE : POINTS * FACE]
    groups = []
    for a in range(POINTS):
        group = full[a * FACE : (a + 1) * FACE]
        first = group[0:SLOT] + seen(last_y[a], SLOT, at_y & (~at_x))
        if a == 0:
            first = first + seen(last_y[ORDER], FACE + SLOT, at_y & at_x)
        group = jnp.concatenate([first, group[SLOT:]], axis=0)
        if a == 0:
            group = group + seen(last_x, FACE, at_x & (~at_y))
        groups.append(group)
    matrix[...] = jnp.concatenate(groups, axis=0).astype(BF16)

    row = lax.broadcasted_iota(jnp.int32, (KDIM, FACE), 0)
    col = lax.broadcasted_iota(jnp.int32, (KDIM, FACE), 1)
    face_x = jnp.where(row == ORDER * FACE + col, 1.0, 0.0)
    face_y = jnp.where(row == (col // SLOT) * FACE + ORDER * SLOT + col % SLOT, 1.0, 0.0)
    faces = jnp.concatenate([face_x, face_y], axis=1).astype(BF16)
    both = dot_nn(full[:, 0:KDIM].astype(BF16), faces)
    from_xy[...] = both.astype(BF16)
    low = lax.broadcasted_iota(jnp.int32, (FACE, 2 * FACE), 1) < FACE
    groups = []
    for a in range(POINTS):
        group = both[a * FACE : (a + 1) * FACE]
        moved = jnp.concatenate(
            [group[ORDER * SLOT : POINTS * SLOT], jnp.zeros((FACE - SLOT, 2 * FACE), F32)], axis=0
        )
        groups.append(jnp.where(low, group, pltpu.roll(moved, FACE, 1)))
    from_x[...] = jnp.concatenate(groups, axis=0).astype(BF16)
    groups = []
    for a in range(POINTS):
        group = pltpu.roll(both[a * FACE : (a + 1) * FACE], FACE, 1)
        moved = both[ORDER * FACE : POINTS * FACE] if a == 0 else jnp.zeros_like(group)
        groups.append(jnp.where(low, group, moved))
    from_y[...] = jnp.concatenate(groups, axis=0).astype(BF16)


def padded_table():
    table = lagrange_table(ORDER, COARSE_ORDER).astype(np.float32)
    table = table.reshape(ORDER * ORDER, ORDER, -1)
    table = np.pad(table, ((0, 0), (0, SLOT - ORDER), (0, COARSE_ROWS - table.shape[-1])))
    return jnp.asarray(table.reshape(-1, COARSE_ROWS), F32).astype(BF16)


def local(coarse_states, record_target, cell_matrix, mass_scale, potential, filter_window):
    rows_x, rows_y, rows_z = mass_scale.shape
    size_x = lax.axis_size("dx")
    size_y = lax.axis_size("dy")
    node_total = float(rows_x * rows_y * rows_z * size_x * size_y)
    padded = (ROWS + 1, ROWS + 1, COLUMN, STATES)
    inside = (ROWS, ROWS, COLUMN, STATES)
    pair = (PAIR, STATES)
    face = (LINES,) + pair
    line = (COLUMN, STATES)
    share = STATES // size_y
    messages = 2 * size_y + size_x - 3
    vmem = pl.BlockSpec(memory_space=pltpu.VMEM)
    filtered, inverse, gram_matrix = pl.pallas_call(
        functools.partial(filter_kernel, size_x, size_y, node_total),
        out_shape=(
            jax.ShapeDtypeStruct((rows_x * rows_y * rows_z, 3 * STATES), BF16),
            jax.ShapeDtypeStruct((STATES, 3 * STATES), BF16),
            jax.ShapeDtypeStruct((STATES, STATES), F32),
        ),
        in_specs=[pl.BlockSpec(memory_space=pltpu.SMEM)] * 2
        + [vmem]
        + [pl.BlockSpec(memory_space=pl.ANY)] * 4,
        out_specs=(pl.BlockSpec(memory_space=pl.ANY), vmem, vmem),
        scratch_shapes=[
            pltpu.VMEM(padded, F32),
            pltpu.VMEM(inside, F32),
            pltpu.VMEM((KDIM, SLOT * FACE), BF16),
            pltpu.VMEM((KDIM, 2 * FACE), BF16),
            pltpu.VMEM((KDIM, 2 * FACE), BF16),
            pltpu.VMEM((KDIM, 2 * FACE), BF16),
            pltpu.VMEM((PAIR, 2 * COLUMN), BF16),
            pltpu.VMEM((2 * COLUMN, PAIR), BF16),
            pltpu.VMEM((2 * COLUMN, PAIR), BF16),
            pltpu.VMEM((SLOT, STATES), jnp.int32),
            pltpu.VMEM((ORDER * ORDER * SLOT, COARSE_ROWS), BF16),
            pltpu.VMEM(mass_scale.shape, F32),
            pltpu.VMEM(potential.shape, F32),
            pltpu.VMEM(cell_matrix.shape, BF16),
            pltpu.VMEM((3, CAPACITY, COARSE_ROWS, STATES), BF16),
            pltpu.VMEM((4 * CAPACITY, COARSE_ROWS, STATES), BF16),
            pltpu.VMEM((3, SLOT, STATES), jnp.int32),
            pltpu.SMEM((3, SLOT, STATES), jnp.int32),
            pltpu.VMEM((2,) + padded, F32),
            pltpu.VMEM(padded, F32),
            pltpu.VMEM((SLOT * FACE, COUNT_Z * STATES), BF16),
            pltpu.VMEM((ORDER * FACE, 2 * COUNT_Z * STATES), BF16),
            pltpu.VMEM((2 * FACE, COUNT_Z * STATES), BF16),
            pltpu.VMEM(face, BF16),
            pltpu.VMEM(face, BF16),
            pltpu.VMEM((2, LINES // 2 + LINES + 1) + pair, BF16),
            pltpu.VMEM((2, LINES // 2 + LINES) + pair, BF16),
            pltpu.VMEM(face, BF16),
            pltpu.VMEM(face, BF16),
            pltpu.VMEM(line, BF16),
            pltpu.VMEM((2,) + face, BF16),
            pltpu.VMEM((2,) + face, BF16),
            pltpu.VMEM((2,) + line, BF16),
            pltpu.VMEM((ROWS * ROWS * DEPTH, 3 * STATES), BF16),
            pltpu.VMEM((STATES, STATES), F32),
            pltpu.VMEM((2, size_y - 1, share, STATES), F32),
            pltpu.VMEM((2, size_x, share, STATES), F32),
            pltpu.VMEM((2, STATES, STATES), F32),
            pltpu.VMEM((STATES, 2 * STATES), F32),
            pltpu.SemaphoreType.DMA((3,)),
            pltpu.SemaphoreType.DMA((3,)),
            pltpu.SemaphoreType.DMA((3,)),
            pltpu.SemaphoreType.DMA((3,)),
            pltpu.SemaphoreType.DMA((3,)),
            pltpu.SemaphoreType.DMA,
            pltpu.SemaphoreType.DMA((4,)),
            pltpu.SemaphoreType.DMA((2, 8)),
            pltpu.SemaphoreType.DMA((2, 8)),
            pltpu.SemaphoreType.DMA((2, messages)),
            pltpu.SemaphoreType.DMA((2, messages)),
        ],
        compiler_params=pltpu.CompilerParams(
            collective_id=0, has_side_effects=True, vmem_limit_bytes=62 * 1024 * 1024
        ),
        cost_estimate=pl.CostEstimate(
            flops=6 * 4 * 2 * KDIM * KDIM * 512, bytes_accessed=10_000_000, transcendentals=0
        ),
        name="filter_twice",
    )(
        filter_window,
        record_target,
        coarse_states,
        padded_table(),
        mass_scale,
        potential,
        cell_matrix,
    )
    states = dot_nt(filtered, inverse)
    return (states.reshape(rows_x, rows_y, rows_z, STATES), gram_matrix)


def solution(mesh):
    in_specs = (
        P(("dx", "dy"), None, None),
        P(("dx", "dy")),
        P(),
        P("dx", "dy", None),
        P("dx", "dy", None),
        P(),
    )
    out_specs = (P("dx", "dy", None, None), P())
    return jax.shard_map(local, mesh=mesh, in_specs=in_specs, out_specs=out_specs, check_vma=False)
```

```python
import functools

import jax
import jax.numpy as jnp
import numpy as np
from jax import lax
from jax.experimental import pallas as pl
from jax.experimental.pallas import tpu as pltpu
from jax.sharding import PartitionSpec as P

ORDER = 6
COARSE_ORDER = 4
CHEB_DEGREE = 3
POINTS = ORDER + 1
COUNT_Z = 4
SLOT = 8
COLUMN = COUNT_Z * SLOT
ROWS = 12
STATES = 128
PAIRS = 4
KDIM = POINTS * SLOT * SLOT
FACE = SLOT * SLOT
DEPTH = COUNT_Z * ORDER
PAIR = 2 * DEPTH
LINES = ROWS // 2
CELLS = 16
PANEL = 16
CAPACITY = CELLS // 2
COARSE_ROWS = 128
MESH = pl.DeviceIdType.MESH
F32 = jnp.float32
BF16 = jnp.bfloat16


def node_points(degree_value):
    return -np.cos(np.pi * np.arange(degree_value + 1) / degree_value)


def lagrange_table(fine_degree, coarse_degree):
    targets = node_points(fine_degree)
    sources = node_points(coarse_degree)
    matrix = np.ones((fine_degree + 1, coarse_degree + 1))
    for p in range(coarse_degree + 1):
        for m in range(coarse_degree + 1):
            if m != p:
                matrix[:, p] = matrix[:, p] * (targets - sources[m]) / (sources[p] - sources[m])
    owned_rows = matrix[:fine_degree]
    first = owned_rows[:, None, None, :, None, None]
    second = owned_rows[None, :, None, None, :, None]
    third = owned_rows[None, None, :, None, None, :]
    product = first * second * third
    return product.reshape(fine_degree**3, (coarse_degree + 1) ** 3)


def cut_index(value, size):
    assert size & (size - 1) == 0
    return lax.shift_right_logical(value, size.bit_length() - 1), value & (size - 1)


def row_in_slot(shape, axis):
    return lax.broadcasted_iota(jnp.int32, shape, axis) % SLOT


def dot_nn(a, b):
    return lax.dot_general(a, b, (((1,), (0,)), ((), ())), preferred_element_type=F32)


def dot_tn(a, b):
    return lax.dot_general(a, b, (((0,), (0,)), ((), ())), preferred_element_type=F32)


def dot_nt(a, b):
    return lax.dot_general(a, b, (((1,), (1,)), ((), ())), preferred_element_type=F32)


def split_two(value):
    high = value.astype(BF16)
    return high, (value - high.astype(F32)).astype(BF16)


def split_three(value):
    high = value.astype(BF16)
    rest = value - high.astype(F32)
    middle = rest.astype(BF16)
    return high, middle, (rest - middle.astype(F32)).astype(BF16)


def factor_rows(work):
    size = STATES
    sub = lax.broadcasted_iota(jnp.int32, (PANEL, size), 0)
    lane = lax.broadcasted_iota(jnp.int32, (PANEL, size), 1)
    for base in range(0, size, PANEL):
        end = base + PANEL
        left = work[base:end, 0:size]
        right = work[base:end, size : 2 * size]
        columns = [
            jnp.broadcast_to(left[:, base + m : base + m + 1], (PANEL, size)) for m in range(PANEL)
        ]
        for m in range(PANEL):
            pivot = jnp.broadcast_to(columns[m][m : m + 1, :], (PANEL, size))
            scale = lax.rsqrt(pivot)
            below = sub > m
            at = sub == m
            coef = columns[m] * scale
            row_left = jnp.broadcast_to(left[m : m + 1, :], (PANEL, size)) * scale
            row_right = jnp.broadcast_to(right[m : m + 1, :], (PANEL, size)) * scale
            for n in range(m + 1, PANEL):
                entry = jnp.broadcast_to(columns[n][m : m + 1, :], (PANEL, size)) * scale
                columns[n] = jnp.where(below, columns[n] - coef * entry, columns[n])
            left = jnp.where(below, left - coef * row_left, jnp.where(at, row_left, left))
            right = jnp.where(below, right - coef * row_right, jnp.where(at, row_right, right))
        work[base:end, 0:size] = left
        work[base:end, size : 2 * size] = right
        if end < size:
            later = jnp.where(lane >= end, left, 0.0)
            l1, l2, l3 = [v.astype(F32) for v in split_three(later)]
            both = jnp.concatenate([left, right], axis=1)
            b1, b2, b3 = [v.astype(F32) for v in split_three(both)]
            lhs = jnp.concatenate([l1, l1, l2, l1, l3, l2], axis=0).astype(BF16)
            rhs = jnp.concatenate([b1, b2, b1, b3, b1, b2], axis=0).astype(BF16)
            work[end:size, :] = work[end:size, :] - dot_tn(lhs, rhs)[end:size, :]


def filter_kernel(
    size_x,
    size_y,
    node_total,
    window,
    targets,
    coarse,
    table_any,
    mass_any,
    pot_any,
    matrix_any,
    filtered_out,
    inverse_out,
    gram_out,
    mass,
    pot,
    matrix,
    from_x,
    from_y,
    from_xy,
    shrink,
    grow,
    grow_own,
    target_tile,
    table,
    mass_in,
    pot_in,
    cell_matrix,
    slots,
    arrived,
    target_in,
    target_list,
    block,
    total,
    rhs,
    rhs_two,
    rhs_taken,
    send_x,
    send_y,
    take_x,
    take_y,
    back_x,
    back_y,
    back_c,
    got_x,
    got_y,
    got_c,
    split,
    partial,
    piece_in,
    ring_in,
    gram_sum,
    work,
    target_send,
    target_recv,
    list_sems,
    record_send,
    record_recv,
    store_sem,
    fetch_sems,
    send_sems,
    recv_sems,
    sum_send,
    sum_recv,
):
    me_x = lax.axis_index("dx")
    me_y = lax.axis_index("dy")

    def at(step_x, step_y):
        return (lax.rem(me_x + step_x + size_x, size_x), lax.rem(me_y + step_y + size_y, size_y))

    partners = [at(0, d) for d in range(1, size_y)] + [at(d, 0) for d in range(1, size_x)]
    partners += [at(1, 1), at(-1, -1), at(1, -1), at(-1, 1)]
    barrier = pltpu.get_barrier_semaphore()
    for partner in partners:
        pl.semaphore_signal(barrier, inc=1, device_id=partner, device_id_type=MESH)
    fetches = [
        pltpu.make_async_copy(src, dst, fetch_sems.at[i])
        for i, (src, dst) in enumerate(
            [
                (matrix_any, cell_matrix),
                (mass_any, mass_in),
                (pot_any, pot_in),
                (table_any, table),
            ]
        )
    ]
    for fetch in fetches:
        fetch.start()
    steps = (None, (0, 1), (1, 0), (1, 1))
    ranks = []
    counts = [0, 0, 0, 0]
    for r in range(CELLS):
        device = cut_index(targets[r], CELLS)[0]
        to_x, to_y = cut_index(device, size_y)
        step_x = (to_x - me_x + size_x) & (size_x - 1)
        step_y = (to_y - me_y + size_y) & (size_y - 1)
        bucket = 2 * step_x + step_y
        rank = 0
        for index in range(4):
            rank = jnp.where(bucket == index, counts[index], rank)
            counts[index] = jnp.where(bucket == index, counts[index] + 1, counts[index])
        ranks.append(bucket * CAPACITY + rank)

    def record_of(slot):
        found = 0
        for r in range(CELLS):
            found = jnp.where(ranks[r] == slot, r, found)
        return found & (CELLS - 1)

    last = COARSE_ROWS - 16
    for index in range(3):
        slots[index, :, last:COARSE_ROWS] = jnp.zeros((CAPACITY, 16, STATES), BF16)
    arrived[0:CAPACITY, last:COARSE_ROWS] = jnp.zeros((CAPACITY, 16, STATES), BF16)
    coarse_count = coarse.shape[1]
    tile_lane = lax.broadcasted_iota(jnp.int32, (SLOT, STATES), 1)
    tile = jnp.zeros((SLOT, STATES), jnp.int32)
    for r in range(CELLS):
        tile = jnp.where(tile_lane == r, targets[r], tile)
    target_tile[...] = tile
    pl.semaphore_wait(barrier, len(partners))
    target_copies, record_copies = {}, {}
    for index in (3, 2, 1):
        target_copies[index] = pltpu.make_async_remote_copy(
            src_ref=target_tile,
            dst_ref=target_in.at[index - 1],
            send_sem=target_send.at[index - 1],
            recv_sem=target_recv.at[index - 1],
            device_id=at(*steps[index]),
            device_id_type=MESH,
        )
        target_copies[index].start()
    for index in (3, 2, 1):
        for k in range(CAPACITY):
            slots[index - 1, k, 0:coarse_count] = coarse[record_of(index * CAPACITY + k)]
        record_copies[index] = pltpu.make_async_remote_copy(
            src_ref=slots.at[index - 1],
            dst_ref=arrived.at[pl.ds(index * CAPACITY, CAPACITY)],
            send_sem=record_send.at[index - 1],
            recv_sem=record_recv.at[index - 1],
            device_id=at(*steps[index]),
            device_id_type=MESH,
        )
        record_copies[index].start()
    for k in range(CAPACITY):
        arrived[k, 0:coarse_count] = coarse[record_of(k)]

    for fetch in fetches:
        fetch.wait()
    place_nodes(mass_in, pot_in, mass, pot)
    spread_matrix(cell_matrix, matrix, from_x, from_y, from_xy)
    line_tables(shrink, grow, grow_own)
    block[1] = jnp.zeros(block.shape[1:], F32)

    for index in (3, 2, 1):
        target_copies[index].wait()
    lists = [
        pltpu.make_async_copy(target_in.at[i], target_list.at[i], list_sems.at[i]) for i in range(3)
    ]
    for copy in lists:
        copy.start()
    for copy in lists:
        copy.wait()
    own = me_x * size_y + me_y
    places = [0] * CELLS
    for index in range(4):
        seen = 0
        for r in range(CELLS):
            target = targets[r] if index == 0 else target_list[index - 1, 0, r]
            device, cell = cut_index(target, CELLS)
            hit = device == own
            cell = jnp.where(hit, cell, -1)
            slot = index * CAPACITY + seen
            for g in range(CELLS):
                places[g] = jnp.where(cell == g, slot, places[g])
            seen = jnp.where(hit, seen + 1, seen)
    places = [p & (4 * CAPACITY - 1) for p in places]
    for index in (3, 2, 1):
        record_copies[index].wait()
    slot_row = row_in_slot((COLUMN, STATES), 0)
    for e in range(2):
        for f in range(2):
            for h in range(COUNT_Z):
                rhs[0:COARSE_ROWS, h * STATES : (h + 1) * STATES] = arrived[
                    places[(2 * e + f) * COUNT_Z + h]
                ]
            fine = dot_nn(table[...], rhs[0:COARSE_ROWS, :]).astype(BF16).astype(F32)
            for a in range(ORDER):
                for b in range(ORDER):
                    first = (a * ORDER + b) * SLOT
                    lines = [
                        fine[first : first + SLOT, h * STATES : (h + 1) * STATES]
                        for h in range(COUNT_Z)
                    ]
                    lines = jnp.concatenate(lines, axis=0)
                    again = pltpu.roll(lines, COLUMN - SLOT + ORDER, 0)
                    block[0, e * ORDER + a, f * ORDER + b] = jnp.where(
                        slot_row == ORDER, again, lines
                    )

    low = window[0]
    high = window[1]
    center = (low + high) / 2.0
    radius = (high - low) / 2.0

    def remote(turn, index, src, dst, step_x, step_y):
        return pltpu.make_async_remote_copy(
            src_ref=src,
            dst_ref=dst,
            send_sem=send_sems.at[turn, index],
            recv_sem=recv_sems.at[turn, index],
            device_id=at(step_x, step_y),
            device_id_type=MESH,
        )

    zeros = jnp.zeros((SLOT, STATES), F32)

    def pack(first, second):
        return jnp.concatenate([first, second], axis=0).astype(BF16)

    def add_product(product, e, f, points_x, points_y, written):
        for a in range(points_x):
            for b in range(points_y):
                first = (a * SLOT + b) * SLOT
                x, y = e * ORDER + a, f * ORDER + b
                for h in range(COUNT_Z):
                    rows = slice(h * SLOT, (h + 1) * SLOT)
                    part = product[first : first + SLOT, h * STATES : (h + 1) * STATES]
                    if (x, y) in written:
                        part = part + total[x, y, rows]
                    total[x, y, rows] = part
                written.add((x, y))

    def gather(q, e, f, out, lane):
        points_x = POINTS if e == 0 else ORDER
        for a in range(points_x):
            x = e * ORDER + a
            for h in range(COUNT_Z):
                rows = slice(h * SLOT, (h + 1) * SLOT)
                chunks = []
                for b in range(POINTS):
                    y = f * ORDER + b
                    own = y < ROWS
                    chunks.append(mass[x, y, rows] * block[q, x, y, rows] if own else zeros)
                chunks.append(chunks[0] if f == 0 else zeros)
                for i in range(PAIRS):
                    tile = pack(chunks[2 * i], chunks[2 * i + 1])
                    copies = [a, POINTS] if (a == 0 and e == 0) else [a]
                    for place in copies:
                        first = (place * PAIRS + i) * 2 * SLOT
                        lanes = slice(lane + h * STATES, lane + (h + 1) * STATES)
                        out[first : first + 2 * SLOT, lanes] = tile

    def taken_rows(base, lines, h):
        chunks = [line[h * SLOT : (h + 1) * SLOT] if line is not None else zeros for line in lines]
        for i in range(PAIRS):
            first = base + i * 2 * SLOT
            rhs_taken[first : first + 2 * SLOT, h * STATES : (h + 1) * STATES] = pack(
                chunks[2 * i], chunks[2 * i + 1]
            )

    def taken_column(e, f, factor, runs, points_x, points_y, written):
        for index, lines in enumerate(runs):
            for h in range(COUNT_Z):
                taken_rows(index * FACE, lines, h)
        depth = FACE * len(runs)
        product = dot_nn(factor[:, 0:depth], rhs_taken[0:depth, :])
        add_product(product, e, f, points_x, points_y, written)

    def narrow(lines, out):
        wide = lines.astype(BF16).reshape(LINES, 2 * COLUMN, STATES)
        wide = jnp.concatenate([wide[i] for i in range(LINES)], axis=1)
        packed = dot_nn(shrink[...], wide).astype(BF16)
        for i in range(LINES):
            out[i] = packed[:, i * STATES : (i + 1) * STATES]

    def widen(pairs, rows_of_slot):
        wide = dot_nn(rows_of_slot[...], jnp.concatenate(pairs, axis=1))
        lines = []
        for i in range(len(pairs)):
            for half in range(2):
                lines.append(
                    wide[half * COLUMN : (half + 1) * COLUMN, i * STATES : (i + 1) * STATES]
                )
        return lines

    def folded(raw):
        axis = raw.ndim - 2
        first = row_in_slot(raw.shape, axis) == 0
        return raw + jnp.where(first, pltpu.roll(raw, SLOT - ORDER, axis), 0.0)

    def finish(q, index, alpha, beta):
        raw = total[index]
        slot_row = row_in_slot(raw.shape, 1)
        summed = folded(raw)
        again = pltpu.roll(summed, COLUMN - SLOT + ORDER, 1)
        full = jnp.where(slot_row < ORDER, summed, jnp.where(slot_row == ORDER, again, 0.0))
        value = block[(q,) + index]
        result = mass[index] * full + (pot[index] - center) * value
        block[(1 - q,) + index] = alpha * result - beta * block[(1 - q,) + index]

    def one_apply(t):
        q = t % 2
        first = (t % CHEB_DEGREE) == 0
        alpha = jnp.where(first, 1.0, 2.0) / radius
        beta = jnp.where(first, 0.0, 1.0)
        quarter = LINES // 2
        half = pl.ds(quarter, quarter)
        values = [
            remote(q, 0, send_x, take_x.at[q, pl.ds(quarter, LINES)], -1, 0),
            remote(q, 1, send_x.at[half], take_x.at[q, pl.ds(0, quarter)], -1, 1),
            remote(
                q, 2, send_x.at[pl.ds(0, 1)], take_x.at[q, pl.ds(quarter + LINES, 1)], -1, -1
            ),
            remote(q, 3, send_y.at[half], take_y.at[q, pl.ds(0, quarter)], 1, -1),
            remote(q, 4, send_y, take_y.at[q, pl.ds(quarter, LINES)], 0, -1),
        ]
        sum_x = remote(q, 5, back_x, got_x.at[q], 1, 0)
        sum_y = remote(q, 6, back_y, got_y.at[q], 0, 1)
        sum_c = remote(q, 7, back_c, got_c.at[q], 1, 1)
        narrow(mass[0, 0:ROWS] * block[q, 0, 0:ROWS], send_x)
        for copy in values[0:3]:
            copy.start()
        written = set()
        width = COUNT_Z * STATES
        inner = FACE * ORDER
        gather(q, 1, 0, rhs_two, 0)
        gather(q, 1, 1, rhs_two, width)
        face = dot_nn(matrix[inner : inner + FACE, 0:inner], rhs_two[...])

        def face_line(f, b):
            parts = [
                face[b * SLOT : (b + 1) * SLOT, f * width + h * STATES : f * width + (h + 1) * STATES]
                for h in range(COUNT_Z)
            ]
            return jnp.concatenate(parts, axis=0)

        lines = [face_line(0, b) for b in range(ORDER)]
        lines.append(face_line(0, ORDER) + face_line(1, 0))
        lines += [face_line(1, b) for b in range(1, ORDER)]
        narrow(folded(jnp.stack(lines)), back_x)
        sum_x.start()
        back_c[...] = face_line(1, ORDER).astype(BF16)
        sum_c.start()
        narrow(mass[0:ROWS, 0] * block[q, 0:ROWS, 0], send_y)
        for copy in values[3:5]:
            copy.start()
        product = dot_nn(matrix[0:inner, 0:inner], rhs_two[:, width : 2 * width])
        add_product(product, 1, 1, ORDER, POINTS, written)
        gather(q, 0, 1, rhs, 0)
        add_product(dot_nn(matrix[...], rhs[...]), 0, 1, POINTS, POINTS, written)
        narrow(folded(total[0:ROWS, ROWS]), back_y)
        sum_y.start()
        product = dot_nn(matrix[0:inner, 0:inner], rhs_two[:, 0:width])
        add_product(product, 1, 0, ORDER, POINTS, written)
        gather(q, 0, 0, rhs, 0)
        add_product(dot_nn(matrix[...], rhs[...]), 0, 0, POINTS, POINTS, written)

        @pl.when(t == CHEB_DEGREE)
        def _():
            gather_pieces(0)

        @pl.when(t == CHEB_DEGREE + 1)
        def _():
            gather_rows(0)

        last = 2 * ORDER
        none = [None]
        values[4].wait()
        along_y = widen([take_y[q, i] for i in range(quarter, quarter + LINES)], grow)
        taken_column(0, 1, from_y, [along_y[0:POINTS] + none], POINTS, ORDER, written)

        def interior(x, carry):
            finish(q, (x, pl.ds(1, ROWS - 1)), alpha, beta)
            return carry

        lax.fori_loop(1, ORDER, interior, 0)
        for copy in values[0:4]:
            copy.wait()
        along_x = widen([take_x[q, i] for i in range(quarter + LINES + 1)], grow)
        taken_column(
            1,
            1,
            from_xy,
            [along_x[last : last + POINTS] + none, along_y[ORDER:] + none * 2],
            ORDER,
            ORDER,
            written,
        )
        taken_column(
            1,
            0,
            from_x,
            [along_x[ORDER : last + 1] + none, along_x[0:POINTS] + none],
            ORDER,
            POINTS,
            written,
        )
        lax.fori_loop(ORDER, ROWS, interior, 0)
        behind_y = widen([take_y[q, i] for i in range(quarter)], grow)
        for h in range(COUNT_Z):
            taken_rows(0, behind_y + [along_y[0]] + none, h)
        product = dot_nn(from_y[0:FACE, FACE : 2 * FACE], rhs_taken[0:FACE, :])
        add_product(product, 0, 1, 1, ORDER, written)
        for copy in (sum_c, sum_y, sum_x):
            copy.wait()
        total[0, 0] += got_c[q].astype(F32)
        for x, line in enumerate(widen([got_y[q, i] for i in range(LINES)], grow_own)):
            total[x, 0] += line
        for y, line in enumerate(widen([got_x[q, i] for i in range(LINES)], grow_own)):
            total[0, y] += line
        finish(q, (0, slice(0, ROWS)), alpha, beta)
        finish(q, (slice(1, ROWS), 0), alpha, beta)

    share = STATES // size_y

    def move(p, index, src, dst, device):
        return pltpu.make_async_remote_copy(
            src_ref=src,
            dst_ref=dst,
            send_sem=sum_send.at[p, index],
            recv_sem=sum_recv.at[p, index],
            device_id=device,
            device_id_type=MESH,
        )

    def rows_of(owner):
        return pl.ds(pl.multiple_of(owner * share, SLOT), share)

    mine = rows_of(me_y)

    def piece_copies(p):
        copies = []
        for d in range(1, size_y):
            device = at(0, d)
            src = partial.at[rows_of(device[1])]
            copies.append(move(p, d - 1, src, piece_in.at[p, d - 1], device))
        return copies

    def ring_copies(p):
        own = ring_in.at[p, me_x]
        return [move(p, size_y + d - 2, own, own, at(d, 0)) for d in range(1, size_x)]

    def row_copies(p):
        own = gram_sum.at[p, mine]
        first = size_y + size_x - 3
        return [move(p, first + d, own, own, at(0, d)) for d in range(1, size_y)]

    def gather_pieces(p):
        for copy in piece_copies(p):
            copy.wait()
        piece = partial[mine, :]
        for d in range(1, size_y):
            piece = piece + piece_in[p, d - 1]
        ring_in[p, me_x] = piece
        for copy in ring_copies(p):
            copy.start()

    def gather_rows(p):
        for copy in ring_copies(p):
            copy.wait()
        piece = ring_in[p, 0]
        for d in range(1, size_x):
            piece = piece + ring_in[p, d]
        gram_sum[p, mine] = piece / node_total
        for copy in row_copies(p):
            copy.start()

    def begin_sum(p, q):
        def divide(x, inner):
            value = block[q, x, 0:ROWS]
            value = jnp.concatenate(
                [value[:, h * SLOT : h * SLOT + ORDER] for h in range(COUNT_Z)], axis=1
            )
            high_part, low_part = split_two(value.reshape(ROWS * DEPTH, STATES))
            rows = pl.ds(pl.multiple_of(x * ROWS * DEPTH, ROWS * DEPTH), ROWS * DEPTH)
            split[rows, 0:STATES] = high_part
            split[rows, STATES : 2 * STATES] = low_part
            split[rows, 2 * STATES : 3 * STATES] = high_part
            return inner

        lax.fori_loop(0, ROWS, divide, 0)
        products = dot_tn(split[:, 0:STATES], split[:, 0 : 2 * STATES])
        cross = products[:, STATES : 2 * STATES]
        partial[...] = products[:, 0:STATES] + cross + cross.T
        for copy in piece_copies(p):
            copy.start()

    def end_sum(p):
        for copy in row_copies(p):
            copy.wait()
        work[:, 0:STATES] = gram_sum[p]
        shape = (STATES, STATES)
        diagonal = lax.broadcasted_iota(jnp.int32, shape, 0) == lax.broadcasted_iota(
            jnp.int32, shape, 1
        )
        work[:, STATES : 2 * STATES] = jnp.where(diagonal, 1.0, 0.0)
        factor_rows(work)
        return work[:, STATES : 2 * STATES]

    def step(t, carry):
        @pl.when(t == CHEB_DEGREE)
        def _():
            begin_sum(0, CHEB_DEGREE % 2)

        one_apply(t)

        @pl.when(t == CHEB_DEGREE + 1)
        def _():
            pair = stacked_inverse(end_sum(0))

            def turn(x, inner):
                for index in range(2):
                    value = block[index, x, 0:ROWS].reshape(ROWS * COLUMN, STATES)
                    block[index, x, 0:ROWS] = times_inverse(value, pair).reshape(
                        ROWS, COLUMN, STATES
                    )
                return inner

            lax.fori_loop(0, ROWS, turn, 0)

        return carry

    lax.fori_loop(0, 2 * CHEB_DEGREE, step, 0)
    begin_sum(1, 0)
    store = pltpu.make_async_copy(split, filtered_out, store_sem)
    store.start()
    gather_pieces(1)
    gather_rows(1)
    inverse = end_sum(1)
    high_part, low_part = split_two(inverse)
    inverse_out[...] = jnp.concatenate([high_part, high_part, low_part], axis=1)
    gram_out[...] = gram_sum[1]
    store.wait()


def stacked_inverse(inverse):
    high, low = split_two(inverse)
    return jnp.concatenate(
        [jnp.concatenate([high, high], axis=1), jnp.concatenate([low, low], axis=1)], axis=0
    )


def times_inverse(value, pair):
    high, low = split_two(value)
    both = dot_nt(jnp.concatenate([high, low], axis=1), pair)
    return both[:, 0:STATES] + both[:, STATES : 2 * STATES]


def place_nodes(mass_in, pot_in, mass, pot):
    width = 3 * DEPTH
    row = lax.broadcasted_iota(jnp.int32, (COLUMN, width), 0)
    lane = lax.broadcasted_iota(jnp.int32, (COLUMN, width), 1)
    within = row % SLOT
    source = lax.rem((row // SLOT) * ORDER + within, DEPTH)
    pick = jnp.where((lax.rem(lane, DEPTH) == source) & (within < POINTS), 1.0, 0.0)
    ones = jnp.ones((width, STATES), BF16)

    def one(x, carry):
        for values, out in ((mass_in, mass), (pot_in, pot)):
            parts = [v.astype(F32) for v in split_three(values[x])]
            parts = jnp.concatenate(parts, axis=1)
            spread = [
                jnp.broadcast_to(parts[y : y + 1, :], (COLUMN, width)) * pick for y in range(ROWS)
            ]
            lines = dot_nn(jnp.concatenate(spread, axis=0).astype(BF16), ones)
            out[x, 0:ROWS] = lines.reshape(ROWS, COLUMN, STATES)
        return carry

    lax.fori_loop(0, ROWS, one, 0, unroll=2)
    mass[ROWS] = jnp.ones(mass.shape[1:], F32)
    mass[0:ROWS, ROWS] = jnp.ones((ROWS, COLUMN, STATES), F32)


def line_tables(shrink, grow, grow_own):
    row = lax.broadcasted_iota(jnp.int32, (PAIR, 2 * COLUMN), 0)
    col = lax.broadcasted_iota(jnp.int32, (PAIR, 2 * COLUMN), 1)
    z = row % DEPTH
    chosen = (row // DEPTH) * COLUMN + (z // ORDER) * SLOT + z % ORDER
    shrink[...] = jnp.where(col == chosen, 1.0, 0.0).astype(BF16)
    row = lax.broadcasted_iota(jnp.int32, (2 * COLUMN, PAIR), 0)
    col = lax.broadcasted_iota(jnp.int32, (2 * COLUMN, PAIR), 1)
    c = row % SLOT
    z = (((row // SLOT) % COUNT_Z) * ORDER + c) % DEPTH
    same = col == (row // COLUMN) * DEPTH + z
    grow[...] = jnp.where(same & (c < POINTS), 1.0, 0.0).astype(BF16)
    grow_own[...] = jnp.where(same & (c < ORDER), 1.0, 0.0).astype(BF16)


def spread_matrix(cell_matrix, matrix, from_x, from_y, from_xy):
    nodes = POINTS**3
    row = lax.broadcasted_iota(jnp.int32, (KDIM, nodes), 0)
    col = lax.broadcasted_iota(jnp.int32, (KDIM, nodes), 1)
    b = (row // SLOT) % SLOT
    c = row % SLOT
    source = (row // FACE) * POINTS * POINTS + b * POINTS + c
    pick = jnp.where((col == source) & (b < POINTS) & (c < POINTS), 1.0, 0.0).astype(BF16)
    half = dot_nn(pick, cell_matrix[...]).astype(BF16)
    full = dot_nt(half, pick)
    width = SLOT * FACE
    full = jnp.concatenate([full, jnp.zeros((KDIM, FACE), F32)], axis=1)
    lane = lax.broadcasted_iota(jnp.int32, (FACE, width), 1)
    at_x = lane // FACE == POINTS
    at_y = (lane // SLOT) % SLOT == POINTS

    def seen(rows, shift, mask):
        return jnp.where(mask[0 : rows.shape[0]], pltpu.roll(rows, shift, 1), 0.0)

    last_y = [full[a * FACE + ORDER * SLOT : a * FACE + POINTS * SLOT] for a in range(POINTS)]
    last_x = full[ORDER * FACE : POINTS * FACE]
    groups = []
    for a in range(POINTS):
        group = full[a * FACE : (a + 1) * FACE]
        first = group[0:SLOT] + seen(last_y[a], SLOT, at_y & (~at_x))
        if a == 0:
            first = first + seen(last_y[ORDER], FACE + SLOT, at_y & at_x)
        group = jnp.concatenate([first, group[SLOT:]], axis=0)
        if a == 0:
            group = group + seen(last_x, FACE, at_x & (~at_y))
        groups.append(group)
    matrix[...] = jnp.concatenate(groups, axis=0).astype(BF16)

    row = lax.broadcasted_iota(jnp.int32, (KDIM, FACE), 0)
    col = lax.broadcasted_iota(jnp.int32, (KDIM, FACE), 1)
    face_x = jnp.where(row == ORDER * FACE + col, 1.0, 0.0)
    face_y = jnp.where(row == (col // SLOT) * FACE + ORDER * SLOT + col % SLOT, 1.0, 0.0)
    faces = jnp.concatenate([face_x, face_y], axis=1).astype(BF16)
    both = dot_nn(full[:, 0:KDIM].astype(BF16), faces)
    from_xy[...] = both.astype(BF16)
    low = lax.broadcasted_iota(jnp.int32, (FACE, 2 * FACE), 1) < FACE
    groups = []
    for a in range(POINTS):
        group = both[a * FACE : (a + 1) * FACE]
        moved = jnp.concatenate(
            [group[ORDER * SLOT : POINTS * SLOT], jnp.zeros((FACE - SLOT, 2 * FACE), F32)], axis=0
        )
        groups.append(jnp.where(low, group, pltpu.roll(moved, FACE, 1)))
    from_x[...] = jnp.concatenate(groups, axis=0).astype(BF16)
    groups = []
    for a in range(POINTS):
        group = pltpu.roll(both[a * FACE : (a + 1) * FACE], FACE, 1)
        moved = both[ORDER * FACE : POINTS * FACE] if a == 0 else jnp.zeros_like(group)
        groups.append(jnp.where(low, group, moved))
    from_y[...] = jnp.concatenate(groups, axis=0).astype(BF16)


def padded_table():
    table = lagrange_table(ORDER, COARSE_ORDER).astype(np.float32)
    table = table.reshape(ORDER * ORDER, ORDER, -1)
    table = np.pad(table, ((0, 0), (0, SLOT - ORDER), (0, COARSE_ROWS - table.shape[-1])))
    return jnp.asarray(table.reshape(-1, COARSE_ROWS), F32).astype(BF16)


def local(coarse_states, record_target, cell_matrix, mass_scale, potential, filter_window):
    rows_x, rows_y, rows_z = mass_scale.shape
    size_x = lax.axis_size("dx")
    size_y = lax.axis_size("dy")
    node_total = float(rows_x * rows_y * rows_z * size_x * size_y)
    padded = (ROWS + 1, ROWS + 1, COLUMN, STATES)
    inside = (ROWS, ROWS, COLUMN, STATES)
    pair = (PAIR, STATES)
    face = (LINES,) + pair
    line = (COLUMN, STATES)
    share = STATES // size_y
    messages = 2 * size_y + size_x - 3
    vmem = pl.BlockSpec(memory_space=pltpu.VMEM)
    filtered, inverse, gram_matrix = pl.pallas_call(
        functools.partial(filter_kernel, size_x, size_y, node_total),
        out_shape=(
            jax.ShapeDtypeStruct((rows_x * rows_y * rows_z, 3 * STATES), BF16),
            jax.ShapeDtypeStruct((STATES, 3 * STATES), BF16),
            jax.ShapeDtypeStruct((STATES, STATES), F32),
        ),
        in_specs=[pl.BlockSpec(memory_space=pltpu.SMEM)] * 2
        + [vmem]
        + [pl.BlockSpec(memory_space=pl.ANY)] * 4,
        out_specs=(pl.BlockSpec(memory_space=pl.ANY), vmem, vmem),
        scratch_shapes=[
            pltpu.VMEM(padded, F32),
            pltpu.VMEM(inside, F32),
            pltpu.VMEM((KDIM, SLOT * FACE), BF16),
            pltpu.VMEM((KDIM, 2 * FACE), BF16),
            pltpu.VMEM((KDIM, 2 * FACE), BF16),
            pltpu.VMEM((KDIM, 2 * FACE), BF16),
            pltpu.VMEM((PAIR, 2 * COLUMN), BF16),
            pltpu.VMEM((2 * COLUMN, PAIR), BF16),
            pltpu.VMEM((2 * COLUMN, PAIR), BF16),
            pltpu.VMEM((SLOT, STATES), jnp.int32),
            pltpu.VMEM((ORDER * ORDER * SLOT, COARSE_ROWS), BF16),
            pltpu.VMEM(mass_scale.shape, F32),
            pltpu.VMEM(potential.shape, F32),
            pltpu.VMEM(cell_matrix.shape, BF16),
            pltpu.VMEM((3, CAPACITY, COARSE_ROWS, STATES), BF16),
            pltpu.VMEM((4 * CAPACITY, COARSE_ROWS, STATES), BF16),
            pltpu.VMEM((3, SLOT, STATES), jnp.int32),
            pltpu.SMEM((3, SLOT, STATES), jnp.int32),
            pltpu.VMEM((2,) + padded, F32),
            pltpu.VMEM(padded, F32),
            pltpu.VMEM((SLOT * FACE, COUNT_Z * STATES), BF16),
            pltpu.VMEM((ORDER * FACE, 2 * COUNT_Z * STATES), BF16),
            pltpu.VMEM((2 * FACE, COUNT_Z * STATES), BF16),
            pltpu.VMEM(face, BF16),
            pltpu.VMEM(face, BF16),
            pltpu.VMEM((2, LINES // 2 + LINES + 1) + pair, BF16),
            pltpu.VMEM((2, LINES // 2 + LINES) + pair, BF16),
            pltpu.VMEM(face, BF16),
            pltpu.VMEM(face, BF16),
            pltpu.VMEM(line, BF16),
            pltpu.VMEM((2,) + face, BF16),
            pltpu.VMEM((2,) + face, BF16),
            pltpu.VMEM((2,) + line, BF16),
            pltpu.VMEM((ROWS * ROWS * DEPTH, 3 * STATES), BF16),
            pltpu.VMEM((STATES, STATES), F32),
            pltpu.VMEM((2, size_y - 1, share, STATES), F32),
            pltpu.VMEM((2, size_x, share, STATES), F32),
            pltpu.VMEM((2, STATES, STATES), F32),
            pltpu.VMEM((STATES, 2 * STATES), F32),
            pltpu.SemaphoreType.DMA((3,)),
            pltpu.SemaphoreType.DMA((3,)),
            pltpu.SemaphoreType.DMA((3,)),
            pltpu.SemaphoreType.DMA((3,)),
            pltpu.SemaphoreType.DMA((3,)),
            pltpu.SemaphoreType.DMA,
            pltpu.SemaphoreType.DMA((4,)),
            pltpu.SemaphoreType.DMA((2, 8)),
            pltpu.SemaphoreType.DMA((2, 8)),
            pltpu.SemaphoreType.DMA((2, messages)),
            pltpu.SemaphoreType.DMA((2, messages)),
        ],
        compiler_params=pltpu.CompilerParams(
            collective_id=0, has_side_effects=True, vmem_limit_bytes=62 * 1024 * 1024
        ),
        cost_estimate=pl.CostEstimate(
            flops=6 * 4 * 2 * KDIM * KDIM * 512, bytes_accessed=10_000_000, transcendentals=0
        ),
        name="filter_twice",
    )(
        filter_window,
        record_target,
        coarse_states,
        padded_table(),
        mass_scale,
        potential,
        cell_matrix,
    )
    states = dot_nt(filtered, inverse)
    return (states.reshape(rows_x, rows_y, rows_z, STATES), gram_matrix)


def solution(mesh):
    in_specs = (
        P(("dx", "dy"), None, None),
        P(("dx", "dy")),
        P(),
        P("dx", "dy", None),
        P("dx", "dy", None),
        P(),
    )
    out_specs = (P("dx", "dy", None, None), P())
    return jax.shard_map(local, mesh=mesh, in_specs=in_specs, out_specs=out_specs, check_vma=False)
```

```python
import functools

import jax
import jax.numpy as jnp
import numpy as np
from jax import lax
from jax.experimental import pallas as pl
from jax.experimental.pallas import tpu as pltpu
from jax.sharding import PartitionSpec as P

ORDER = 6
COARSE_ORDER = 4
CHEB_DEGREE = 3
POINTS = ORDER + 1
COUNT_Z = 4
SLOT = 8
COLUMN = COUNT_Z * SLOT
ROWS = 12
STATES = 128
PAIRS = 4
KDIM = POINTS * SLOT * SLOT
FACE = SLOT * SLOT
DEPTH = COUNT_Z * ORDER
PAIR = 2 * DEPTH
LINES = ROWS // 2
CELLS = 16
PANEL = 16
CAPACITY = CELLS // 2
COARSE_ROWS = 128
MESH = pl.DeviceIdType.MESH
F32 = jnp.float32
BF16 = jnp.bfloat16


def node_points(degree_value):
    return -np.cos(np.pi * np.arange(degree_value + 1) / degree_value)


def lagrange_table(fine_degree, coarse_degree):
    targets = node_points(fine_degree)
    sources = node_points(coarse_degree)
    matrix = np.ones((fine_degree + 1, coarse_degree + 1))
    for p in range(coarse_degree + 1):
        for m in range(coarse_degree + 1):
            if m != p:
                matrix[:, p] = matrix[:, p] * (targets - sources[m]) / (sources[p] - sources[m])
    owned_rows = matrix[:fine_degree]
    first = owned_rows[:, None, None, :, None, None]
    second = owned_rows[None, :, None, None, :, None]
    third = owned_rows[None, None, :, None, None, :]
    product = first * second * third
    return product.reshape(fine_degree**3, (coarse_degree + 1) ** 3)


def cut_index(value, size):
    assert size & (size - 1) == 0
    return lax.shift_right_logical(value, size.bit_length() - 1), value & (size - 1)


def row_in_slot(shape, axis):
    return lax.broadcasted_iota(jnp.int32, shape, axis) % SLOT


def dot_nn(a, b):
    return lax.dot_general(a, b, (((1,), (0,)), ((), ())), preferred_element_type=F32)


def dot_tn(a, b):
    return lax.dot_general(a, b, (((0,), (0,)), ((), ())), preferred_element_type=F32)


def dot_nt(a, b):
    return lax.dot_general(a, b, (((1,), (1,)), ((), ())), preferred_element_type=F32)


def split_two(value):
    high = value.astype(BF16)
    return high, (value - high.astype(F32)).astype(BF16)


def split_three(value):
    high = value.astype(BF16)
    rest = value - high.astype(F32)
    middle = rest.astype(BF16)
    return high, middle, (rest - middle.astype(F32)).astype(BF16)


def factor_rows(work):
    size = STATES
    sub = lax.broadcasted_iota(jnp.int32, (PANEL, size), 0)
    lane = lax.broadcasted_iota(jnp.int32, (PANEL, size), 1)
    for base in range(0, size, PANEL):
        end = base + PANEL
        left = work[base:end, 0:size]
        right = work[base:end, size : 2 * size]
        columns = [
            jnp.broadcast_to(left[:, base + m : base + m + 1], (PANEL, size)) for m in range(PANEL)
        ]
        for m in range(PANEL):
            pivot = jnp.broadcast_to(columns[m][m : m + 1, :], (PANEL, size))
            scale = lax.rsqrt(pivot)
            below = sub > m
            at = sub == m
            coef = columns[m] * scale
            row_left = jnp.broadcast_to(left[m : m + 1, :], (PANEL, size)) * scale
            row_right = jnp.broadcast_to(right[m : m + 1, :], (PANEL, size)) * scale
            for n in range(m + 1, PANEL):
                entry = jnp.broadcast_to(columns[n][m : m + 1, :], (PANEL, size)) * scale
                columns[n] = jnp.where(below, columns[n] - coef * entry, columns[n])
            left = jnp.where(below, left - coef * row_left, jnp.where(at, row_left, left))
            right = jnp.where(below, right - coef * row_right, jnp.where(at, row_right, right))
        work[base:end, 0:size] = left
        work[base:end, size : 2 * size] = right
        if end < size:
            later = jnp.where(lane >= end, left, 0.0)
            l1, l2, l3 = [v.astype(F32) for v in split_three(later)]
            both = jnp.concatenate([left, right], axis=1)
            b1, b2, b3 = [v.astype(F32) for v in split_three(both)]
            lhs = jnp.concatenate([l1, l1, l2, l1, l3, l2], axis=0).astype(BF16)
            rhs = jnp.concatenate([b1, b2, b1, b3, b1, b2], axis=0).astype(BF16)
            work[end:size, :] = work[end:size, :] - dot_tn(lhs, rhs)[end:size, :]


def filter_kernel(
    size_x,
    size_y,
    node_total,
    window,
    targets,
    coarse_any,
    table_any,
    mass_any,
    pot_any,
    matrix_any,
    filtered_out,
    inverse_out,
    gram_out,
    mass,
    pot,
    matrix,
    from_x,
    from_y,
    from_xy,
    shrink,
    grow,
    grow_own,
    target_tile,
    table,
    mass_in,
    pot_in,
    cell_matrix,
    coarse_rows,
    coarse,
    slots,
    arrived,
    target_in,
    target_list,
    block,
    total,
    rhs,
    rhs_two,
    rhs_taken,
    send_x,
    send_y,
    take_x,
    take_y,
    back_x,
    back_y,
    back_c,
    got_x,
    got_y,
    got_c,
    split,
    partial,
    piece_in,
    ring_in,
    gram_sum,
    work,
    target_send,
    target_recv,
    list_sems,
    record_send,
    record_recv,
    store_sem,
    fetch_sems,
    send_sems,
    recv_sems,
    sum_send,
    sum_recv,
):
    me_x = lax.axis_index("dx")
    me_y = lax.axis_index("dy")

    def at(step_x, step_y):
        return (lax.rem(me_x + step_x + size_x, size_x), lax.rem(me_y + step_y + size_y, size_y))

    partners = [at(0, d) for d in range(1, size_y)] + [at(d, 0) for d in range(1, size_x)]
    partners += [at(1, 1), at(-1, -1), at(1, -1), at(-1, 1)]
    barrier = pltpu.get_barrier_semaphore()
    for partner in partners:
        pl.semaphore_signal(barrier, inc=1, device_id=partner, device_id_type=MESH)
    fetches = [
        pltpu.make_async_copy(src, dst, fetch_sems.at[i])
        for i, (src, dst) in enumerate(
            [
                (matrix_any, cell_matrix),
                (mass_any, mass_in),
                (pot_any, pot_in),
                (table_any, table),
                (coarse_any, coarse_rows),
            ]
        )
    ]
    for fetch in fetches:
        fetch.start()
    steps = (None, (0, 1), (1, 0), (1, 1))
    ranks = []
    counts = [0, 0, 0, 0]
    for r in range(CELLS):
        device = cut_index(targets[r], CELLS)[0]
        to_x, to_y = cut_index(device, size_y)
        step_x = (to_x - me_x + size_x) & (size_x - 1)
        step_y = (to_y - me_y + size_y) & (size_y - 1)
        bucket = 2 * step_x + step_y
        rank = 0
        for index in range(4):
            rank = jnp.where(bucket == index, counts[index], rank)
            counts[index] = jnp.where(bucket == index, counts[index] + 1, counts[index])
        ranks.append(bucket * CAPACITY + rank)

    def record_of(slot):
        found = 0
        for r in range(CELLS):
            found = jnp.where(ranks[r] == slot, r, found)
        return found & (CELLS - 1)

    fetches[4].wait()
    coarse_count = coarse_rows.shape[0]
    coarse[:, COARSE_ROWS - 16 :] = jnp.zeros((CELLS, 16, STATES), BF16)
    for half in range(2):
        group = slice(half * SLOT, (half + 1) * SLOT)
        turned = jnp.swapaxes(coarse_rows[...].astype(F32)[:, group], 0, 1)
        coarse[group, 0:coarse_count] = turned.astype(BF16)
    for index in (3, 2, 1):
        for k in range(CAPACITY):
            slots[index - 1, k] = coarse[record_of(index * CAPACITY + k)]
    tile_lane = lax.broadcasted_iota(jnp.int32, (SLOT, STATES), 1)
    tile = jnp.zeros((SLOT, STATES), jnp.int32)
    for r in range(CELLS):
        tile = jnp.where(tile_lane == r, targets[r], tile)
    target_tile[...] = tile
    pl.semaphore_wait(barrier, len(partners))
    target_copies, record_copies = {}, {}
    for index in (3, 2, 1):
        target_copies[index] = pltpu.make_async_remote_copy(
            src_ref=target_tile,
            dst_ref=target_in.at[index - 1],
            send_sem=target_send.at[index - 1],
            recv_sem=target_recv.at[index - 1],
            device_id=at(*steps[index]),
            device_id_type=MESH,
        )
        target_copies[index].start()
    for index in (3, 2, 1):
        record_copies[index] = pltpu.make_async_remote_copy(
            src_ref=slots.at[index - 1],
            dst_ref=arrived.at[pl.ds(index * CAPACITY, CAPACITY)],
            send_sem=record_send.at[index - 1],
            recv_sem=record_recv.at[index - 1],
            device_id=at(*steps[index]),
            device_id_type=MESH,
        )
        record_copies[index].start()
    for k in range(CAPACITY):
        arrived[k] = coarse[record_of(k)]

    for fetch in fetches[0:4]:
        fetch.wait()
    place_nodes(mass_in, pot_in, mass, pot)
    spread_matrix(cell_matrix, matrix, from_x, from_y, from_xy)
    line_tables(shrink, grow, grow_own)
    block[1] = jnp.zeros(block.shape[1:], F32)

    for index in (3, 2, 1):
        target_copies[index].wait()
    lists = [
        pltpu.make_async_copy(target_in.at[i], target_list.at[i], list_sems.at[i]) for i in range(3)
    ]
    for copy in lists:
        copy.start()
    for copy in lists:
        copy.wait()
    own = me_x * size_y + me_y
    places = [0] * CELLS
    for index in range(4):
        seen = 0
        for r in range(CELLS):
            target = targets[r] if index == 0 else target_list[index - 1, 0, r]
            device, cell = cut_index(target, CELLS)
            hit = device == own
            cell = jnp.where(hit, cell, -1)
            slot = index * CAPACITY + seen
            for g in range(CELLS):
                places[g] = jnp.where(cell == g, slot, places[g])
            seen = jnp.where(hit, seen + 1, seen)
    places = [p & (4 * CAPACITY - 1) for p in places]
    for index in (3, 2, 1):
        record_copies[index].wait()
    slot_row = row_in_slot((COLUMN, STATES), 0)
    for e in range(2):
        for f in range(2):
            for h in range(COUNT_Z):
                rhs[0:COARSE_ROWS, h * STATES : (h + 1) * STATES] = arrived[
                    places[(2 * e + f) * COUNT_Z + h]
                ]
            fine = dot_nn(table[...], rhs[0:COARSE_ROWS, :]).astype(BF16).astype(F32)
            for a in range(ORDER):
                for b in range(ORDER):
                    first = (a * ORDER + b) * SLOT
                    lines = [
                        fine[first : first + SLOT, h * STATES : (h + 1) * STATES]
                        for h in range(COUNT_Z)
                    ]
                    lines = jnp.concatenate(lines, axis=0)
                    again = pltpu.roll(lines, COLUMN - SLOT + ORDER, 0)
                    block[0, e * ORDER + a, f * ORDER + b] = jnp.where(
                        slot_row == ORDER, again, lines
                    )

    low = window[0]
    high = window[1]
    center = (low + high) / 2.0
    radius = (high - low) / 2.0

    def remote(turn, index, src, dst, step_x, step_y):
        return pltpu.make_async_remote_copy(
            src_ref=src,
            dst_ref=dst,
            send_sem=send_sems.at[turn, index],
            recv_sem=recv_sems.at[turn, index],
            device_id=at(step_x, step_y),
            device_id_type=MESH,
        )

    zeros = jnp.zeros((SLOT, STATES), F32)

    def pack(first, second):
        return jnp.concatenate([first, second], axis=0).astype(BF16)

    def add_product(product, e, f, points_x, points_y, written):
        for a in range(points_x):
            for b in range(points_y):
                first = (a * SLOT + b) * SLOT
                x, y = e * ORDER + a, f * ORDER + b
                for h in range(COUNT_Z):
                    rows = slice(h * SLOT, (h + 1) * SLOT)
                    part = product[first : first + SLOT, h * STATES : (h + 1) * STATES]
                    if (x, y) in written:
                        part = part + total[x, y, rows]
                    total[x, y, rows] = part
                written.add((x, y))

    def gather(q, e, f, out, lane):
        points_x = POINTS if e == 0 else ORDER
        for a in range(points_x):
            x = e * ORDER + a
            for h in range(COUNT_Z):
                rows = slice(h * SLOT, (h + 1) * SLOT)
                chunks = []
                for b in range(POINTS):
                    y = f * ORDER + b
                    own = y < ROWS
                    chunks.append(mass[x, y, rows] * block[q, x, y, rows] if own else zeros)
                chunks.append(chunks[0] if f == 0 else zeros)
                for i in range(PAIRS):
                    tile = pack(chunks[2 * i], chunks[2 * i + 1])
                    copies = [a, POINTS] if (a == 0 and e == 0) else [a]
                    for place in copies:
                        first = (place * PAIRS + i) * 2 * SLOT
                        lanes = slice(lane + h * STATES, lane + (h + 1) * STATES)
                        out[first : first + 2 * SLOT, lanes] = tile

    def taken_rows(base, lines, h):
        chunks = [line[h * SLOT : (h + 1) * SLOT] if line is not None else zeros for line in lines]
        for i in range(PAIRS):
            first = base + i * 2 * SLOT
            rhs_taken[first : first + 2 * SLOT, h * STATES : (h + 1) * STATES] = pack(
                chunks[2 * i], chunks[2 * i + 1]
            )

    def taken_column(e, f, factor, runs, points_x, points_y, written):
        for index, lines in enumerate(runs):
            for h in range(COUNT_Z):
                taken_rows(index * FACE, lines, h)
        depth = FACE * len(runs)
        product = dot_nn(factor[:, 0:depth], rhs_taken[0:depth, :])
        add_product(product, e, f, points_x, points_y, written)

    def narrow(lines, out):
        wide = lines.astype(BF16).reshape(LINES, 2 * COLUMN, STATES)
        wide = jnp.concatenate([wide[i] for i in range(LINES)], axis=1)
        packed = dot_nn(shrink[...], wide).astype(BF16)
        for i in range(LINES):
            out[i] = packed[:, i * STATES : (i + 1) * STATES]

    def widen(pairs, rows_of_slot):
        wide = dot_nn(rows_of_slot[...], jnp.concatenate(pairs, axis=1))
        lines = []
        for i in range(len(pairs)):
            for half in range(2):
                lines.append(
                    wide[half * COLUMN : (half + 1) * COLUMN, i * STATES : (i + 1) * STATES]
                )
        return lines

    def folded(raw):
        axis = raw.ndim - 2
        first = row_in_slot(raw.shape, axis) == 0
        return raw + jnp.where(first, pltpu.roll(raw, SLOT - ORDER, axis), 0.0)

    def finish(q, index, alpha, beta):
        raw = total[index]
        slot_row = row_in_slot(raw.shape, 1)
        summed = folded(raw)
        again = pltpu.roll(summed, COLUMN - SLOT + ORDER, 1)
        full = jnp.where(slot_row < ORDER, summed, jnp.where(slot_row == ORDER, again, 0.0))
        value = block[(q,) + index]
        result = mass[index] * full + (pot[index] - center) * value
        block[(1 - q,) + index] = alpha * result - beta * block[(1 - q,) + index]

    def one_apply(t):
        q = t % 2
        first = (t % CHEB_DEGREE) == 0
        alpha = jnp.where(first, 1.0, 2.0) / radius
        beta = jnp.where(first, 0.0, 1.0)
        quarter = LINES // 2
        half = pl.ds(quarter, quarter)
        values = [
            remote(q, 0, send_x, take_x.at[q, pl.ds(quarter, LINES)], -1, 0),
            remote(q, 1, send_x.at[half], take_x.at[q, pl.ds(0, quarter)], -1, 1),
            remote(
                q, 2, send_x.at[pl.ds(0, 1)], take_x.at[q, pl.ds(quarter + LINES, 1)], -1, -1
            ),
            remote(q, 3, send_y.at[half], take_y.at[q, pl.ds(0, quarter)], 1, -1),
            remote(q, 4, send_y, take_y.at[q, pl.ds(quarter, LINES)], 0, -1),
        ]
        sum_x = remote(q, 5, back_x, got_x.at[q], 1, 0)
        sum_y = remote(q, 6, back_y, got_y.at[q], 0, 1)
        sum_c = remote(q, 7, back_c, got_c.at[q], 1, 1)
        narrow(mass[0, 0:ROWS] * block[q, 0, 0:ROWS], send_x)
        for copy in values[0:3]:
            copy.start()
        written = set()
        width = COUNT_Z * STATES
        inner = FACE * ORDER
        gather(q, 1, 0, rhs_two, 0)
        gather(q, 1, 1, rhs_two, width)
        face = dot_nn(matrix[inner : inner + FACE, 0:inner], rhs_two[...])

        def face_line(f, b):
            parts = [
                face[b * SLOT : (b + 1) * SLOT, f * width + h * STATES : f * width + (h + 1) * STATES]
                for h in range(COUNT_Z)
            ]
            return jnp.concatenate(parts, axis=0)

        lines = [face_line(0, b) for b in range(ORDER)]
        lines.append(face_line(0, ORDER) + face_line(1, 0))
        lines += [face_line(1, b) for b in range(1, ORDER)]
        narrow(folded(jnp.stack(lines)), back_x)
        sum_x.start()
        back_c[...] = face_line(1, ORDER).astype(BF16)
        sum_c.start()
        narrow(mass[0:ROWS, 0] * block[q, 0:ROWS, 0], send_y)
        for copy in values[3:5]:
            copy.start()
        product = dot_nn(matrix[0:inner, 0:inner], rhs_two[:, width : 2 * width])
        add_product(product, 1, 1, ORDER, POINTS, written)
        gather(q, 0, 1, rhs, 0)
        add_product(dot_nn(matrix[...], rhs[...]), 0, 1, POINTS, POINTS, written)
        narrow(folded(total[0:ROWS, ROWS]), back_y)
        sum_y.start()
        product = dot_nn(matrix[0:inner, 0:inner], rhs_two[:, 0:width])
        add_product(product, 1, 0, ORDER, POINTS, written)
        gather(q, 0, 0, rhs, 0)
        add_product(dot_nn(matrix[...], rhs[...]), 0, 0, POINTS, POINTS, written)

        @pl.when(t == CHEB_DEGREE)
        def _():
            gather_pieces(0)

        @pl.when(t == CHEB_DEGREE + 1)
        def _():
            gather_rows(0)

        last = 2 * ORDER
        none = [None]
        values[4].wait()
        along_y = widen([take_y[q, i] for i in range(quarter, quarter + LINES)], grow)
        taken_column(0, 1, from_y, [along_y[0:POINTS] + none], POINTS, ORDER, written)

        def interior(x, carry):
            finish(q, (x, pl.ds(1, ROWS - 1)), alpha, beta)
            return carry

        lax.fori_loop(1, ORDER, interior, 0)
        for copy in values[0:4]:
            copy.wait()
        along_x = widen([take_x[q, i] for i in range(quarter + LINES + 1)], grow)
        taken_column(
            1,
            1,
            from_xy,
            [along_x[last : last + POINTS] + none, along_y[ORDER:] + none * 2],
            ORDER,
            ORDER,
            written,
        )
        taken_column(
            1,
            0,
            from_x,
            [along_x[ORDER : last + 1] + none, along_x[0:POINTS] + none],
            ORDER,
            POINTS,
            written,
        )
        lax.fori_loop(ORDER, ROWS, interior, 0)
        behind_y = widen([take_y[q, i] for i in range(quarter)], grow)
        for h in range(COUNT_Z):
            taken_rows(0, behind_y + [along_y[0]] + none, h)
        product = dot_nn(from_y[0:FACE, FACE : 2 * FACE], rhs_taken[0:FACE, :])
        add_product(product, 0, 1, 1, ORDER, written)
        for copy in (sum_c, sum_y, sum_x):
            copy.wait()
        total[0, 0] += got_c[q].astype(F32)
        for x, line in enumerate(widen([got_y[q, i] for i in range(LINES)], grow_own)):
            total[x, 0] += line
        for y, line in enumerate(widen([got_x[q, i] for i in range(LINES)], grow_own)):
            total[0, y] += line
        finish(q, (0, slice(0, ROWS)), alpha, beta)
        finish(q, (slice(1, ROWS), 0), alpha, beta)

    share = STATES // size_y

    def move(p, index, src, dst, device):
        return pltpu.make_async_remote_copy(
            src_ref=src,
            dst_ref=dst,
            send_sem=sum_send.at[p, index],
            recv_sem=sum_recv.at[p, index],
            device_id=device,
            device_id_type=MESH,
        )

    def rows_of(owner):
        return pl.ds(pl.multiple_of(owner * share, SLOT), share)

    mine = rows_of(me_y)

    def piece_copies(p):
        copies = []
        for d in range(1, size_y):
            device = at(0, d)
            src = partial.at[rows_of(device[1])]
            copies.append(move(p, d - 1, src, piece_in.at[p, d - 1], device))
        return copies

    def ring_copies(p):
        own = ring_in.at[p, me_x]
        return [move(p, size_y + d - 2, own, own, at(d, 0)) for d in range(1, size_x)]

    def row_copies(p):
        own = gram_sum.at[p, mine]
        first = size_y + size_x - 3
        return [move(p, first + d, own, own, at(0, d)) for d in range(1, size_y)]

    def gather_pieces(p):
        for copy in piece_copies(p):
            copy.wait()
        piece = partial[mine, :]
        for d in range(1, size_y):
            piece = piece + piece_in[p, d - 1]
        ring_in[p, me_x] = piece
        for copy in ring_copies(p):
            copy.start()

    def gather_rows(p):
        for copy in ring_copies(p):
            copy.wait()
        piece = ring_in[p, 0]
        for d in range(1, size_x):
            piece = piece + ring_in[p, d]
        gram_sum[p, mine] = piece / node_total
        for copy in row_copies(p):
            copy.start()

    def begin_sum(p, q):
        def divide(x, inner):
            value = block[q, x, 0:ROWS]
            value = jnp.concatenate(
                [value[:, h * SLOT : h * SLOT + ORDER] for h in range(COUNT_Z)], axis=1
            )
            high_part, low_part = split_two(value.reshape(ROWS * DEPTH, STATES))
            rows = pl.ds(pl.multiple_of(x * ROWS * DEPTH, ROWS * DEPTH), ROWS * DEPTH)
            split[rows, 0:STATES] = high_part
            split[rows, STATES : 2 * STATES] = low_part
            split[rows, 2 * STATES : 3 * STATES] = high_part
            return inner

        lax.fori_loop(0, ROWS, divide, 0)
        products = dot_tn(split[:, 0:STATES], split[:, 0 : 2 * STATES])
        cross = products[:, STATES : 2 * STATES]
        partial[...] = products[:, 0:STATES] + cross + cross.T
        for copy in piece_copies(p):
            copy.start()

    def end_sum(p):
        for copy in row_copies(p):
            copy.wait()
        work[:, 0:STATES] = gram_sum[p]
        shape = (STATES, STATES)
        diagonal = lax.broadcasted_iota(jnp.int32, shape, 0) == lax.broadcasted_iota(
            jnp.int32, shape, 1
        )
        work[:, STATES : 2 * STATES] = jnp.where(diagonal, 1.0, 0.0)
        factor_rows(work)
        return work[:, STATES : 2 * STATES]

    def step(t, carry):
        @pl.when(t == CHEB_DEGREE)
        def _():
            begin_sum(0, CHEB_DEGREE % 2)

        one_apply(t)

        @pl.when(t == CHEB_DEGREE + 1)
        def _():
            pair = stacked_inverse(end_sum(0))

            def turn(x, inner):
                for index in range(2):
                    value = block[index, x, 0:ROWS].reshape(ROWS * COLUMN, STATES)
                    block[index, x, 0:ROWS] = times_inverse(value, pair).reshape(
                        ROWS, COLUMN, STATES
                    )
                return inner

            lax.fori_loop(0, ROWS, turn, 0)

        return carry

    lax.fori_loop(0, 2 * CHEB_DEGREE, step, 0)
    begin_sum(1, 0)
    store = pltpu.make_async_copy(split, filtered_out, store_sem)
    store.start()
    gather_pieces(1)
    gather_rows(1)
    inverse = end_sum(1)
    high_part, low_part = split_two(inverse)
    inverse_out[...] = jnp.concatenate([high_part, high_part, low_part], axis=1)
    gram_out[...] = gram_sum[1]
    store.wait()


def stacked_inverse(inverse):
    high, low = split_two(inverse)
    return jnp.concatenate(
        [jnp.concatenate([high, high], axis=1), jnp.concatenate([low, low], axis=1)], axis=0
    )


def times_inverse(value, pair):
    high, low = split_two(value)
    both = dot_nt(jnp.concatenate([high, low], axis=1), pair)
    return both[:, 0:STATES] + both[:, STATES : 2 * STATES]


def place_nodes(mass_in, pot_in, mass, pot):
    width = 3 * DEPTH
    row = lax.broadcasted_iota(jnp.int32, (COLUMN, width), 0)
    lane = lax.broadcasted_iota(jnp.int32, (COLUMN, width), 1)
    within = row % SLOT
    source = lax.rem((row // SLOT) * ORDER + within, DEPTH)
    pick = jnp.where((lax.rem(lane, DEPTH) == source) & (within < POINTS), 1.0, 0.0)
    ones = jnp.ones((width, STATES), BF16)

    def one(x, carry):
        for values, out in ((mass_in, mass), (pot_in, pot)):
            parts = [v.astype(F32) for v in split_three(values[x])]
            parts = jnp.concatenate(parts, axis=1)
            spread = [
                jnp.broadcast_to(parts[y : y + 1, :], (COLUMN, width)) * pick for y in range(ROWS)
            ]
            lines = dot_nn(jnp.concatenate(spread, axis=0).astype(BF16), ones)
            out[x, 0:ROWS] = lines.reshape(ROWS, COLUMN, STATES)
        return carry

    lax.fori_loop(0, ROWS, one, 0, unroll=2)
    mass[ROWS] = jnp.ones(mass.shape[1:], F32)
    mass[0:ROWS, ROWS] = jnp.ones((ROWS, COLUMN, STATES), F32)


def line_tables(shrink, grow, grow_own):
    row = lax.broadcasted_iota(jnp.int32, (PAIR, 2 * COLUMN), 0)
    col = lax.broadcasted_iota(jnp.int32, (PAIR, 2 * COLUMN), 1)
    z = row % DEPTH
    chosen = (row // DEPTH) * COLUMN + (z // ORDER) * SLOT + z % ORDER
    shrink[...] = jnp.where(col == chosen, 1.0, 0.0).astype(BF16)
    row = lax.broadcasted_iota(jnp.int32, (2 * COLUMN, PAIR), 0)
    col = lax.broadcasted_iota(jnp.int32, (2 * COLUMN, PAIR), 1)
    c = row % SLOT
    z = (((row // SLOT) % COUNT_Z) * ORDER + c) % DEPTH
    same = col == (row // COLUMN) * DEPTH + z
    grow[...] = jnp.where(same & (c < POINTS), 1.0, 0.0).astype(BF16)
    grow_own[...] = jnp.where(same & (c < ORDER), 1.0, 0.0).astype(BF16)


def spread_matrix(cell_matrix, matrix, from_x, from_y, from_xy):
    nodes = POINTS**3
    row = lax.broadcasted_iota(jnp.int32, (KDIM, nodes), 0)
    col = lax.broadcasted_iota(jnp.int32, (KDIM, nodes), 1)
    b = (row // SLOT) % SLOT
    c = row % SLOT
    source = (row // FACE) * POINTS * POINTS + b * POINTS + c
    pick = jnp.where((col == source) & (b < POINTS) & (c < POINTS), 1.0, 0.0).astype(BF16)
    half = dot_nn(pick, cell_matrix[...]).astype(BF16)
    full = dot_nt(half, pick)
    width = SLOT * FACE
    full = jnp.concatenate([full, jnp.zeros((KDIM, FACE), F32)], axis=1)
    lane = lax.broadcasted_iota(jnp.int32, (FACE, width), 1)
    at_x = lane // FACE == POINTS
    at_y = (lane // SLOT) % SLOT == POINTS

    def seen(rows, shift, mask):
        return jnp.where(mask[0 : rows.shape[0]], pltpu.roll(rows, shift, 1), 0.0)

    last_y = [full[a * FACE + ORDER * SLOT : a * FACE + POINTS * SLOT] for a in range(POINTS)]
    last_x = full[ORDER * FACE : POINTS * FACE]
    groups = []
    for a in range(POINTS):
        group = full[a * FACE : (a + 1) * FACE]
        first = group[0:SLOT] + seen(last_y[a], SLOT, at_y & (~at_x))
        if a == 0:
            first = first + seen(last_y[ORDER], FACE + SLOT, at_y & at_x)
        group = jnp.concatenate([first, group[SLOT:]], axis=0)
        if a == 0:
            group = group + seen(last_x, FACE, at_x & (~at_y))
        groups.append(group)
    matrix[...] = jnp.concatenate(groups, axis=0).astype(BF16)

    row = lax.broadcasted_iota(jnp.int32, (KDIM, FACE), 0)
    col = lax.broadcasted_iota(jnp.int32, (KDIM, FACE), 1)
    face_x = jnp.where(row == ORDER * FACE + col, 1.0, 0.0)
    face_y = jnp.where(row == (col // SLOT) * FACE + ORDER * SLOT + col % SLOT, 1.0, 0.0)
    faces = jnp.concatenate([face_x, face_y], axis=1).astype(BF16)
    both = dot_nn(full[:, 0:KDIM].astype(BF16), faces)
    from_xy[...] = both.astype(BF16)
    low = lax.broadcasted_iota(jnp.int32, (FACE, 2 * FACE), 1) < FACE
    groups = []
    for a in range(POINTS):
        group = both[a * FACE : (a + 1) * FACE]
        moved = jnp.concatenate(
            [group[ORDER * SLOT : POINTS * SLOT], jnp.zeros((FACE - SLOT, 2 * FACE), F32)], axis=0
        )
        groups.append(jnp.where(low, group, pltpu.roll(moved, FACE, 1)))
    from_x[...] = jnp.concatenate(groups, axis=0).astype(BF16)
    groups = []
    for a in range(POINTS):
        group = pltpu.roll(both[a * FACE : (a + 1) * FACE], FACE, 1)
        moved = both[ORDER * FACE : POINTS * FACE] if a == 0 else jnp.zeros_like(group)
        groups.append(jnp.where(low, group, moved))
    from_y[...] = jnp.concatenate(groups, axis=0).astype(BF16)


def padded_table():
    table = lagrange_table(ORDER, COARSE_ORDER).astype(np.float32)
    table = table.reshape(ORDER * ORDER, ORDER, -1)
    table = np.pad(table, ((0, 0), (0, SLOT - ORDER), (0, COARSE_ROWS - table.shape[-1])))
    return jnp.asarray(table.reshape(-1, COARSE_ROWS), F32).astype(BF16)


def local(coarse_states, record_target, cell_matrix, mass_scale, potential, filter_window):
    rows_x, rows_y, rows_z = mass_scale.shape
    size_x = lax.axis_size("dx")
    size_y = lax.axis_size("dy")
    node_total = float(rows_x * rows_y * rows_z * size_x * size_y)
    padded = (ROWS + 1, ROWS + 1, COLUMN, STATES)
    inside = (ROWS, ROWS, COLUMN, STATES)
    pair = (PAIR, STATES)
    face = (LINES,) + pair
    line = (COLUMN, STATES)
    share = STATES // size_y
    messages = 2 * size_y + size_x - 3
    by_row = coarse_states.transpose(1, 0, 2)
    vmem = pl.BlockSpec(memory_space=pltpu.VMEM)
    filtered, inverse, gram_matrix = pl.pallas_call(
        functools.partial(filter_kernel, size_x, size_y, node_total),
        out_shape=(
            jax.ShapeDtypeStruct((rows_x * rows_y * rows_z, 3 * STATES), BF16),
            jax.ShapeDtypeStruct((STATES, 3 * STATES), BF16),
            jax.ShapeDtypeStruct((STATES, STATES), F32),
        ),
        in_specs=[pl.BlockSpec(memory_space=pltpu.SMEM)] * 2
        + [pl.BlockSpec(memory_space=pl.ANY)] * 5,
        out_specs=(pl.BlockSpec(memory_space=pl.ANY), vmem, vmem),
        scratch_shapes=[
            pltpu.VMEM(padded, F32),
            pltpu.VMEM(inside, F32),
            pltpu.VMEM((KDIM, SLOT * FACE), BF16),
            pltpu.VMEM((KDIM, 2 * FACE), BF16),
            pltpu.VMEM((KDIM, 2 * FACE), BF16),
            pltpu.VMEM((KDIM, 2 * FACE), BF16),
            pltpu.VMEM((PAIR, 2 * COLUMN), BF16),
            pltpu.VMEM((2 * COLUMN, PAIR), BF16),
            pltpu.VMEM((2 * COLUMN, PAIR), BF16),
            pltpu.VMEM((SLOT, STATES), jnp.int32),
            pltpu.VMEM((ORDER * ORDER * SLOT, COARSE_ROWS), BF16),
            pltpu.VMEM(mass_scale.shape, F32),
            pltpu.VMEM(potential.shape, F32),
            pltpu.VMEM(cell_matrix.shape, BF16),
            pltpu.VMEM(by_row.shape, BF16),
            pltpu.VMEM((CELLS, COARSE_ROWS, STATES), BF16),
            pltpu.VMEM((3, CAPACITY, COARSE_ROWS, STATES), BF16),
            pltpu.VMEM((4 * CAPACITY, COARSE_ROWS, STATES), BF16),
            pltpu.VMEM((3, SLOT, STATES), jnp.int32),
            pltpu.SMEM((3, SLOT, STATES), jnp.int32),
            pltpu.VMEM((2,) + padded, F32),
            pltpu.VMEM(padded, F32),
            pltpu.VMEM((SLOT * FACE, COUNT_Z * STATES), BF16),
            pltpu.VMEM((ORDER * FACE, 2 * COUNT_Z * STATES), BF16),
            pltpu.VMEM((2 * FACE, COUNT_Z * STATES), BF16),
            pltpu.VMEM(face, BF16),
            pltpu.VMEM(face, BF16),
            pltpu.VMEM((2, LINES // 2 + LINES + 1) + pair, BF16),
            pltpu.VMEM((2, LINES // 2 + LINES) + pair, BF16),
            pltpu.VMEM(face, BF16),
            pltpu.VMEM(face, BF16),
            pltpu.VMEM(line, BF16),
            pltpu.VMEM((2,) + face, BF16),
            pltpu.VMEM((2,) + face, BF16),
            pltpu.VMEM((2,) + line, BF16),
            pltpu.VMEM((ROWS * ROWS * DEPTH, 3 * STATES), BF16),
            pltpu.VMEM((STATES, STATES), F32),
            pltpu.VMEM((2, size_y - 1, share, STATES), F32),
            pltpu.VMEM((2, size_x, share, STATES), F32),
            pltpu.VMEM((2, STATES, STATES), F32),
            pltpu.VMEM((STATES, 2 * STATES), F32),
            pltpu.SemaphoreType.DMA((3,)),
            pltpu.SemaphoreType.DMA((3,)),
            pltpu.SemaphoreType.DMA((3,)),
            pltpu.SemaphoreType.DMA((3,)),
            pltpu.SemaphoreType.DMA((3,)),
            pltpu.SemaphoreType.DMA,
            pltpu.SemaphoreType.DMA((5,)),
            pltpu.SemaphoreType.DMA((2, 8)),
            pltpu.SemaphoreType.DMA((2, 8)),
            pltpu.SemaphoreType.DMA((2, messages)),
            pltpu.SemaphoreType.DMA((2, messages)),
        ],
        compiler_params=pltpu.CompilerParams(
            collective_id=0, has_side_effects=True, vmem_limit_bytes=62 * 1024 * 1024
        ),
        cost_estimate=pl.CostEstimate(
            flops=6 * 4 * 2 * KDIM * KDIM * 512, bytes_accessed=10_000_000, transcendentals=0
        ),
        name="filter_twice",
    )(
        filter_window,
        record_target,
        by_row,
        padded_table(),
        mass_scale,
        potential,
        cell_matrix,
    )
    states = dot_nt(filtered, inverse)
    return (states.reshape(rows_x, rows_y, rows_z, STATES), gram_matrix)


def solution(mesh):
    in_specs = (
        P(("dx", "dy"), None, None),
        P(("dx", "dy")),
        P(),
        P("dx", "dy", None),
        P("dx", "dy", None),
        P(),
    )
    out_specs = (P("dx", "dy", None, None), P())
    return jax.shard_map(local, mesh=mesh, in_specs=in_specs, out_specs=out_specs, check_vma=False)
```

```python
import functools

import jax
import jax.numpy as jnp
import numpy as np
from jax import lax
from jax.experimental import pallas as pl
from jax.experimental.pallas import tpu as pltpu
from jax.sharding import PartitionSpec as P

ORDER = 6
COARSE_ORDER = 4
CHEB_DEGREE = 3
POINTS = ORDER + 1
COUNT_Z = 4
SLOT = 8
COLUMN = COUNT_Z * SLOT
ROWS = 12
STATES = 128
PAIRS = 4
KDIM = POINTS * SLOT * SLOT
FACE = SLOT * SLOT
DEPTH = COUNT_Z * ORDER
PAIR = 2 * DEPTH
LINES = ROWS // 2
CELLS = 16
PANEL = 16
CAPACITY = CELLS // 2
COARSE_ROWS = 128
MESH = pl.DeviceIdType.MESH
F32 = jnp.float32
BF16 = jnp.bfloat16


def node_points(degree_value):
    return -np.cos(np.pi * np.arange(degree_value + 1) / degree_value)


def lagrange_table(fine_degree, coarse_degree):
    targets = node_points(fine_degree)
    sources = node_points(coarse_degree)
    matrix = np.ones((fine_degree + 1, coarse_degree + 1))
    for p in range(coarse_degree + 1):
        for m in range(coarse_degree + 1):
            if m != p:
                matrix[:, p] = matrix[:, p] * (targets - sources[m]) / (sources[p] - sources[m])
    owned_rows = matrix[:fine_degree]
    first = owned_rows[:, None, None, :, None, None]
    second = owned_rows[None, :, None, None, :, None]
    third = owned_rows[None, None, :, None, None, :]
    product = first * second * third
    return product.reshape(fine_degree**3, (coarse_degree + 1) ** 3)


def cut_index(value, size):
    assert size & (size - 1) == 0
    return lax.shift_right_logical(value, size.bit_length() - 1), value & (size - 1)


def row_in_slot(shape, axis):
    return lax.broadcasted_iota(jnp.int32, shape, axis) % SLOT


def dot_nn(a, b):
    return lax.dot_general(a, b, (((1,), (0,)), ((), ())), preferred_element_type=F32)


def dot_tn(a, b):
    return lax.dot_general(a, b, (((0,), (0,)), ((), ())), preferred_element_type=F32)


def dot_nt(a, b):
    return lax.dot_general(a, b, (((1,), (1,)), ((), ())), preferred_element_type=F32)


def split_two(value):
    high = value.astype(BF16)
    return high, (value - high.astype(F32)).astype(BF16)


def split_three(value):
    high = value.astype(BF16)
    rest = value - high.astype(F32)
    middle = rest.astype(BF16)
    return high, middle, (rest - middle.astype(F32)).astype(BF16)


def factor_rows(work):
    size = STATES
    sub = lax.broadcasted_iota(jnp.int32, (PANEL, size), 0)
    lane = lax.broadcasted_iota(jnp.int32, (PANEL, size), 1)
    for base in range(0, size, PANEL):
        end = base + PANEL
        left = work[base:end, 0:size]
        right = work[base:end, size : 2 * size]
        columns = [
            jnp.broadcast_to(left[:, base + m : base + m + 1], (PANEL, size)) for m in range(PANEL)
        ]
        for m in range(PANEL):
            pivot = jnp.broadcast_to(columns[m][m : m + 1, :], (PANEL, size))
            scale = lax.rsqrt(pivot)
            below = sub > m
            at = sub == m
            coef = columns[m] * scale
            row_left = jnp.broadcast_to(left[m : m + 1, :], (PANEL, size)) * scale
            row_right = jnp.broadcast_to(right[m : m + 1, :], (PANEL, size)) * scale
            for n in range(m + 1, PANEL):
                entry = jnp.broadcast_to(columns[n][m : m + 1, :], (PANEL, size)) * scale
                columns[n] = jnp.where(below, columns[n] - coef * entry, columns[n])
            left = jnp.where(below, left - coef * row_left, jnp.where(at, row_left, left))
            right = jnp.where(below, right - coef * row_right, jnp.where(at, row_right, right))
        work[base:end, 0:size] = left
        work[base:end, size : 2 * size] = right
        if end < size:
            later = jnp.where(lane >= end, left, 0.0)
            l1, l2, l3 = [v.astype(F32) for v in split_three(later)]
            both = jnp.concatenate([left, right], axis=1)
            b1, b2, b3 = [v.astype(F32) for v in split_three(both)]
            lhs = jnp.concatenate([l1, l1, l2, l1, l3, l2], axis=0).astype(BF16)
            rhs = jnp.concatenate([b1, b2, b1, b3, b1, b2], axis=0).astype(BF16)
            work[end:size, :] = work[end:size, :] - dot_tn(lhs, rhs)[end:size, :]


def filter_kernel(
    size_x,
    size_y,
    node_total,
    window,
    targets,
    coarse_any,
    table_any,
    mass_any,
    pot_any,
    matrix_any,
    filtered_out,
    inverse_out,
    gram_out,
    mass,
    pot,
    matrix,
    from_x,
    from_y,
    from_xy,
    shrink,
    grow,
    grow_own,
    target_tile,
    table,
    mass_in,
    pot_in,
    cell_matrix,
    coarse_rows,
    coarse,
    slots,
    arrived,
    target_in,
    target_list,
    block,
    total,
    rhs,
    rhs_two,
    rhs_taken,
    send_x,
    send_y,
    take_x,
    take_y,
    back_x,
    back_y,
    back_c,
    got_x,
    got_y,
    got_c,
    split,
    partial,
    piece_in,
    ring_in,
    gram_sum,
    work,
    target_send,
    target_recv,
    list_sems,
    record_send,
    record_recv,
    store_sem,
    fetch_sems,
    send_sems,
    recv_sems,
    sum_send,
    sum_recv,
):
    me_x = lax.axis_index("dx")
    me_y = lax.axis_index("dy")

    def at(step_x, step_y):
        return (lax.rem(me_x + step_x + size_x, size_x), lax.rem(me_y + step_y + size_y, size_y))

    partners = [at(0, d) for d in range(1, size_y)] + [at(d, 0) for d in range(1, size_x)]
    partners += [at(1, 1), at(-1, -1), at(1, -1), at(-1, 1)]
    barrier = pltpu.get_barrier_semaphore()
    for partner in partners:
        pl.semaphore_signal(barrier, inc=1, device_id=partner, device_id_type=MESH)
    fetches = [
        pltpu.make_async_copy(src, dst, fetch_sems.at[i])
        for i, (src, dst) in enumerate(
            [
                (matrix_any, cell_matrix),
                (mass_any, mass_in),
                (pot_any, pot_in),
                (table_any, table),
                (coarse_any, coarse_rows),
            ]
        )
    ]
    for fetch in fetches:
        fetch.start()
    steps = (None, (0, 1), (1, 0), (1, 1))
    ranks = []
    counts = [0, 0, 0, 0]
    for r in range(CELLS):
        device = cut_index(targets[r], CELLS)[0]
        to_x, to_y = cut_index(device, size_y)
        step_x = (to_x - me_x + size_x) & (size_x - 1)
        step_y = (to_y - me_y + size_y) & (size_y - 1)
        bucket = 2 * step_x + step_y
        rank = 0
        for index in range(4):
            rank = jnp.where(bucket == index, counts[index], rank)
            counts[index] = jnp.where(bucket == index, counts[index] + 1, counts[index])
        ranks.append(bucket * CAPACITY + rank)

    def record_of(slot):
        found = 0
        for r in range(CELLS):
            found = jnp.where(ranks[r] == slot, r, found)
        return found & (CELLS - 1)

    fetches[4].wait()
    coarse_count = coarse_rows.shape[0]
    coarse[:, COARSE_ROWS - 16 :] = jnp.zeros((CELLS, 16, STATES), BF16)
    for half in range(2):
        group = slice(half * SLOT, (half + 1) * SLOT)
        turned = jnp.swapaxes(coarse_rows[...].astype(F32)[:, group], 0, 1)
        coarse[group, 0:coarse_count] = turned.astype(BF16)
    for index in (3, 2, 1):
        for k in range(CAPACITY):
            slots[index - 1, k] = coarse[record_of(index * CAPACITY + k)]
    tile_lane = lax.broadcasted_iota(jnp.int32, (SLOT, STATES), 1)
    tile = jnp.zeros((SLOT, STATES), jnp.int32)
    for r in range(CELLS):
        tile = jnp.where(tile_lane == r, targets[r], tile)
    target_tile[...] = tile
    pl.semaphore_wait(barrier, len(partners))
    target_copies, record_copies = {}, {}
    for index in (3, 2, 1):
        target_copies[index] = pltpu.make_async_remote_copy(
            src_ref=target_tile,
            dst_ref=target_in.at[index - 1],
            send_sem=target_send.at[index - 1],
            recv_sem=target_recv.at[index - 1],
            device_id=at(*steps[index]),
            device_id_type=MESH,
        )
        target_copies[index].start()
    for index in (3, 2, 1):
        record_copies[index] = pltpu.make_async_remote_copy(
            src_ref=slots.at[index - 1],
            dst_ref=arrived.at[pl.ds(index * CAPACITY, CAPACITY)],
            send_sem=record_send.at[index - 1],
            recv_sem=record_recv.at[index - 1],
            device_id=at(*steps[index]),
            device_id_type=MESH,
        )
        record_copies[index].start()
    for k in range(CAPACITY):
        arrived[k] = coarse[record_of(k)]

    for fetch in fetches[0:4]:
        fetch.wait()
    place_nodes(mass_in, pot_in, mass, pot)
    spread_matrix(cell_matrix, matrix, from_x, from_y, from_xy)
    line_tables(shrink, grow, grow_own)
    block[1] = jnp.zeros(block.shape[1:], F32)

    for index in (3, 2, 1):
        target_copies[index].wait()
    lists = [
        pltpu.make_async_copy(target_in.at[i], target_list.at[i], list_sems.at[i]) for i in range(3)
    ]
    for copy in lists:
        copy.start()
    for copy in lists:
        copy.wait()
    own = me_x * size_y + me_y
    places = [0] * CELLS
    for index in range(4):
        seen = 0
        for r in range(CELLS):
            target = targets[r] if index == 0 else target_list[index - 1, 0, r]
            device, cell = cut_index(target, CELLS)
            hit = device == own
            cell = jnp.where(hit, cell, -1)
            slot = index * CAPACITY + seen
            for g in range(CELLS):
                places[g] = jnp.where(cell == g, slot, places[g])
            seen = jnp.where(hit, seen + 1, seen)
    places = [p & (4 * CAPACITY - 1) for p in places]
    for index in (3, 2, 1):
        record_copies[index].wait()
    slot_row = row_in_slot((COLUMN, STATES), 0)
    for e in range(2):
        for f in range(2):
            for h in range(COUNT_Z):
                rhs[0:COARSE_ROWS, h * STATES : (h + 1) * STATES] = arrived[
                    places[(2 * e + f) * COUNT_Z + h]
                ]
            fine = dot_nn(table[...], rhs[0:COARSE_ROWS, :]).astype(BF16).astype(F32)
            for a in range(ORDER):
                for b in range(ORDER):
                    first = (a * ORDER + b) * SLOT
                    lines = [
                        fine[first : first + SLOT, h * STATES : (h + 1) * STATES]
                        for h in range(COUNT_Z)
                    ]
                    lines = jnp.concatenate(lines, axis=0)
                    again = pltpu.roll(lines, COLUMN - SLOT + ORDER, 0)
                    block[0, e * ORDER + a, f * ORDER + b] = jnp.where(
                        slot_row == ORDER, again, lines
                    )

    low = window[0]
    high = window[1]
    center = (low + high) / 2.0
    radius = (high - low) / 2.0

    def remote(turn, index, src, dst, step_x, step_y):
        return pltpu.make_async_remote_copy(
            src_ref=src,
            dst_ref=dst,
            send_sem=send_sems.at[turn, index],
            recv_sem=recv_sems.at[turn, index],
            device_id=at(step_x, step_y),
            device_id_type=MESH,
        )

    zeros = jnp.zeros((SLOT, STATES), F32)

    def pack(first, second):
        return jnp.concatenate([first, second], axis=0).astype(BF16)

    def add_product(product, e, f, points_x, points_y, written):
        for a in range(points_x):
            for b in range(points_y):
                first = (a * SLOT + b) * SLOT
                x, y = e * ORDER + a, f * ORDER + b
                for h in range(COUNT_Z):
                    rows = slice(h * SLOT, (h + 1) * SLOT)
                    part = product[first : first + SLOT, h * STATES : (h + 1) * STATES]
                    if (x, y) in written:
                        part = part + total[x, y, rows]
                    total[x, y, rows] = part
                written.add((x, y))

    def gather(q, e, f, out, lane):
        points_x = POINTS if e == 0 else ORDER
        for a in range(points_x):
            x = e * ORDER + a
            for h in range(COUNT_Z):
                rows = slice(h * SLOT, (h + 1) * SLOT)
                chunks = []
                for b in range(POINTS):
                    y = f * ORDER + b
                    own = y < ROWS
                    chunks.append(mass[x, y, rows] * block[q, x, y, rows] if own else zeros)
                chunks.append(chunks[0] if f == 0 else zeros)
                for i in range(PAIRS):
                    tile = pack(chunks[2 * i], chunks[2 * i + 1])
                    copies = [a, POINTS] if (a == 0 and e == 0) else [a]
                    for place in copies:
                        first = (place * PAIRS + i) * 2 * SLOT
                        lanes = slice(lane + h * STATES, lane + (h + 1) * STATES)
                        out[first : first + 2 * SLOT, lanes] = tile

    def taken_rows(base, lines, h):
        chunks = [line[h * SLOT : (h + 1) * SLOT] if line is not None else zeros for line in lines]
        for i in range(PAIRS):
            first = base + i * 2 * SLOT
            rhs_taken[first : first + 2 * SLOT, h * STATES : (h + 1) * STATES] = pack(
                chunks[2 * i], chunks[2 * i + 1]
            )

    def taken_column(e, f, factor, runs, points_x, points_y, written):
        for index, lines in enumerate(runs):
            for h in range(COUNT_Z):
                taken_rows(index * FACE, lines, h)
        depth = FACE * len(runs)
        product = dot_nn(factor[:, 0:depth], rhs_taken[0:depth, :])
        add_product(product, e, f, points_x, points_y, written)

    def narrow(lines, out):
        wide = lines.astype(BF16).reshape(LINES, 2 * COLUMN, STATES)
        wide = jnp.concatenate([wide[i] for i in range(LINES)], axis=1)
        packed = dot_nn(shrink[...], wide).astype(BF16)
        for i in range(LINES):
            out[i] = packed[:, i * STATES : (i + 1) * STATES]

    def widen(pairs, rows_of_slot):
        wide = dot_nn(rows_of_slot[...], jnp.concatenate(pairs, axis=1))
        lines = []
        for i in range(len(pairs)):
            for half in range(2):
                lines.append(
                    wide[half * COLUMN : (half + 1) * COLUMN, i * STATES : (i + 1) * STATES]
                )
        return lines

    def folded(raw):
        axis = raw.ndim - 2
        first = row_in_slot(raw.shape, axis) == 0
        return raw + jnp.where(first, pltpu.roll(raw, SLOT - ORDER, axis), 0.0)

    def finish(q, index, alpha, beta):
        raw = total[index]
        slot_row = row_in_slot(raw.shape, 1)
        summed = folded(raw)
        again = pltpu.roll(summed, COLUMN - SLOT + ORDER, 1)
        full = jnp.where(slot_row < ORDER, summed, jnp.where(slot_row == ORDER, again, 0.0))
        value = block[(q,) + index]
        result = mass[index] * full + (pot[index] - center) * value
        block[(1 - q,) + index] = alpha * result - beta * block[(1 - q,) + index]

    width = COUNT_Z * STATES

    def gather_ahead(q):
        gather(q, 1, 0, rhs_two, 0)
        gather(q, 1, 1, rhs_two, width)

    def one_apply(t):
        q = t % 2
        first = (t % CHEB_DEGREE) == 0
        alpha = jnp.where(first, 1.0, 2.0) / radius
        beta = jnp.where(first, 0.0, 1.0)
        quarter = LINES // 2
        half = pl.ds(quarter, quarter)
        values = [
            remote(q, 0, send_x, take_x.at[q, pl.ds(quarter, LINES)], -1, 0),
            remote(q, 1, send_x.at[half], take_x.at[q, pl.ds(0, quarter)], -1, 1),
            remote(
                q, 2, send_x.at[pl.ds(0, 1)], take_x.at[q, pl.ds(quarter + LINES, 1)], -1, -1
            ),
            remote(q, 3, send_y.at[half], take_y.at[q, pl.ds(0, quarter)], 1, -1),
            remote(q, 4, send_y, take_y.at[q, pl.ds(quarter, LINES)], 0, -1),
        ]
        sum_x = remote(q, 5, back_x, got_x.at[q], 1, 0)
        sum_y = remote(q, 6, back_y, got_y.at[q], 0, 1)
        sum_c = remote(q, 7, back_c, got_c.at[q], 1, 1)
        narrow(mass[0, 0:ROWS] * block[q, 0, 0:ROWS], send_x)
        for copy in values[0:3]:
            copy.start()
        written = set()
        inner = FACE * ORDER
        face = dot_nn(matrix[inner : inner + FACE, 0:inner], rhs_two[...])

        def face_line(f, b):
            parts = [
                face[b * SLOT : (b + 1) * SLOT, f * width + h * STATES : f * width + (h + 1) * STATES]
                for h in range(COUNT_Z)
            ]
            return jnp.concatenate(parts, axis=0)

        lines = [face_line(0, b) for b in range(ORDER)]
        lines.append(face_line(0, ORDER) + face_line(1, 0))
        lines += [face_line(1, b) for b in range(1, ORDER)]
        narrow(folded(jnp.stack(lines)), back_x)
        sum_x.start()
        back_c[...] = face_line(1, ORDER).astype(BF16)
        sum_c.start()
        narrow(mass[0:ROWS, 0] * block[q, 0:ROWS, 0], send_y)
        for copy in values[3:5]:
            copy.start()
        product = dot_nn(matrix[0:inner, 0:inner], rhs_two[:, width : 2 * width])
        add_product(product, 1, 1, ORDER, POINTS, written)
        gather(q, 0, 1, rhs, 0)
        add_product(dot_nn(matrix[...], rhs[...]), 0, 1, POINTS, POINTS, written)
        narrow(folded(total[0:ROWS, ROWS]), back_y)
        sum_y.start()
        product = dot_nn(matrix[0:inner, 0:inner], rhs_two[:, 0:width])
        add_product(product, 1, 0, ORDER, POINTS, written)
        gather(q, 0, 0, rhs, 0)
        add_product(dot_nn(matrix[...], rhs[...]), 0, 0, POINTS, POINTS, written)

        @pl.when(t == CHEB_DEGREE)
        def _():
            gather_pieces(0)

        @pl.when(t == CHEB_DEGREE + 1)
        def _():
            gather_rows(0)

        last = 2 * ORDER
        none = [None]
        values[4].wait()
        along_y = widen([take_y[q, i] for i in range(quarter, quarter + LINES)], grow)
        taken_column(0, 1, from_y, [along_y[0:POINTS] + none], POINTS, ORDER, written)

        def interior(x, carry):
            finish(q, (x, pl.ds(1, ROWS - 1)), alpha, beta)
            return carry

        lax.fori_loop(1, ORDER, interior, 0)
        for copy in values[0:4]:
            copy.wait()
        along_x = widen([take_x[q, i] for i in range(quarter + LINES + 1)], grow)
        taken_column(
            1,
            1,
            from_xy,
            [along_x[last : last + POINTS] + none, along_y[ORDER:] + none * 2],
            ORDER,
            ORDER,
            written,
        )
        taken_column(
            1,
            0,
            from_x,
            [along_x[ORDER : last + 1] + none, along_x[0:POINTS] + none],
            ORDER,
            POINTS,
            written,
        )
        lax.fori_loop(ORDER, ROWS, interior, 0)
        behind_y = widen([take_y[q, i] for i in range(quarter)], grow)
        for h in range(COUNT_Z):
            taken_rows(0, behind_y + [along_y[0]] + none, h)
        product = dot_nn(from_y[0:FACE, FACE : 2 * FACE], rhs_taken[0:FACE, :])
        add_product(product, 0, 1, 1, ORDER, written)
        sum_y.wait()
        for x, line in enumerate(widen([got_y[q, i] for i in range(LINES)], grow_own)):
            total[x, 0] += line
        finish(q, (slice(1, ROWS), 0), alpha, beta)
        gather_ahead(1 - q)
        for copy in (sum_c, sum_x):
            copy.wait()
        total[0, 0] += got_c[q].astype(F32)
        for y, line in enumerate(widen([got_x[q, i] for i in range(LINES)], grow_own)):
            total[0, y] += line
        finish(q, (0, slice(0, ROWS)), alpha, beta)

    share = STATES // size_y

    def move(p, index, src, dst, device):
        return pltpu.make_async_remote_copy(
            src_ref=src,
            dst_ref=dst,
            send_sem=sum_send.at[p, index],
            recv_sem=sum_recv.at[p, index],
            device_id=device,
            device_id_type=MESH,
        )

    def rows_of(owner):
        return pl.ds(pl.multiple_of(owner * share, SLOT), share)

    mine = rows_of(me_y)

    def piece_copies(p):
        copies = []
        for d in range(1, size_y):
            device = at(0, d)
            src = partial.at[rows_of(device[1])]
            copies.append(move(p, d - 1, src, piece_in.at[p, d - 1], device))
        return copies

    def ring_copies(p):
        own = ring_in.at[p, me_x]
        return [move(p, size_y + d - 2, own, own, at(d, 0)) for d in range(1, size_x)]

    def row_copies(p):
        own = gram_sum.at[p, mine]
        first = size_y + size_x - 3
        return [move(p, first + d, own, own, at(0, d)) for d in range(1, size_y)]

    def gather_pieces(p):
        for copy in piece_copies(p):
            copy.wait()
        piece = partial[mine, :]
        for d in range(1, size_y):
            piece = piece + piece_in[p, d - 1]
        ring_in[p, me_x] = piece
        for copy in ring_copies(p):
            copy.start()

    def gather_rows(p):
        for copy in ring_copies(p):
            copy.wait()
        piece = ring_in[p, 0]
        for d in range(1, size_x):
            piece = piece + ring_in[p, d]
        gram_sum[p, mine] = piece / node_total
        for copy in row_copies(p):
            copy.start()

    def begin_sum(p, q):
        def divide(x, inner):
            value = block[q, x, 0:ROWS]
            value = jnp.concatenate(
                [value[:, h * SLOT : h * SLOT + ORDER] for h in range(COUNT_Z)], axis=1
            )
            high_part, low_part = split_two(value.reshape(ROWS * DEPTH, STATES))
            rows = pl.ds(pl.multiple_of(x * ROWS * DEPTH, ROWS * DEPTH), ROWS * DEPTH)
            split[rows, 0:STATES] = high_part
            split[rows, STATES : 2 * STATES] = low_part
            split[rows, 2 * STATES : 3 * STATES] = high_part
            return inner

        lax.fori_loop(0, ROWS, divide, 0)
        products = dot_tn(split[:, 0:STATES], split[:, 0 : 2 * STATES])
        cross = products[:, STATES : 2 * STATES]
        partial[...] = products[:, 0:STATES] + cross + cross.T
        for copy in piece_copies(p):
            copy.start()

    def end_sum(p):
        for copy in row_copies(p):
            copy.wait()
        work[:, 0:STATES] = gram_sum[p]
        shape = (STATES, STATES)
        diagonal = lax.broadcasted_iota(jnp.int32, shape, 0) == lax.broadcasted_iota(
            jnp.int32, shape, 1
        )
        work[:, STATES : 2 * STATES] = jnp.where(diagonal, 1.0, 0.0)
        factor_rows(work)
        return work[:, STATES : 2 * STATES]

    def step(t, carry):
        @pl.when(t == CHEB_DEGREE)
        def _():
            begin_sum(0, CHEB_DEGREE % 2)

        one_apply(t)

        @pl.when(t == CHEB_DEGREE + 1)
        def _():
            pair = stacked_inverse(end_sum(0))

            def turn(x, inner):
                for index in range(2):
                    value = block[index, x, 0:ROWS].reshape(ROWS * COLUMN, STATES)
                    block[index, x, 0:ROWS] = times_inverse(value, pair).reshape(
                        ROWS, COLUMN, STATES
                    )
                return inner

            lax.fori_loop(0, ROWS, turn, 0)
            gather_ahead((CHEB_DEGREE + 2) % 2)

        return carry

    gather_ahead(0)
    lax.fori_loop(0, 2 * CHEB_DEGREE, step, 0)
    begin_sum(1, 0)
    store = pltpu.make_async_copy(split, filtered_out, store_sem)
    store.start()
    gather_pieces(1)
    gather_rows(1)
    inverse = end_sum(1)
    high_part, low_part = split_two(inverse)
    inverse_out[...] = jnp.concatenate([high_part, high_part, low_part], axis=1)
    gram_out[...] = gram_sum[1]
    store.wait()


def stacked_inverse(inverse):
    high, low = split_two(inverse)
    return jnp.concatenate(
        [jnp.concatenate([high, high], axis=1), jnp.concatenate([low, low], axis=1)], axis=0
    )


def times_inverse(value, pair):
    high, low = split_two(value)
    both = dot_nt(jnp.concatenate([high, low], axis=1), pair)
    return both[:, 0:STATES] + both[:, STATES : 2 * STATES]


def place_nodes(mass_in, pot_in, mass, pot):
    width = 3 * DEPTH
    row = lax.broadcasted_iota(jnp.int32, (COLUMN, width), 0)
    lane = lax.broadcasted_iota(jnp.int32, (COLUMN, width), 1)
    within = row % SLOT
    source = lax.rem((row // SLOT) * ORDER + within, DEPTH)
    pick = jnp.where((lax.rem(lane, DEPTH) == source) & (within < POINTS), 1.0, 0.0)
    ones = jnp.ones((width, STATES), BF16)

    def one(x, carry):
        for values, out in ((mass_in, mass), (pot_in, pot)):
            parts = [v.astype(F32) for v in split_three(values[x])]
            parts = jnp.concatenate(parts, axis=1)
            spread = [
                jnp.broadcast_to(parts[y : y + 1, :], (COLUMN, width)) * pick for y in range(ROWS)
            ]
            lines = dot_nn(jnp.concatenate(spread, axis=0).astype(BF16), ones)
            out[x, 0:ROWS] = lines.reshape(ROWS, COLUMN, STATES)
        return carry

    lax.fori_loop(0, ROWS, one, 0, unroll=2)
    mass[ROWS] = jnp.ones(mass.shape[1:], F32)
    mass[0:ROWS, ROWS] = jnp.ones((ROWS, COLUMN, STATES), F32)


def line_tables(shrink, grow, grow_own):
    row = lax.broadcasted_iota(jnp.int32, (PAIR, 2 * COLUMN), 0)
    col = lax.broadcasted_iota(jnp.int32, (PAIR, 2 * COLUMN), 1)
    z = row % DEPTH
    chosen = (row // DEPTH) * COLUMN + (z // ORDER) * SLOT + z % ORDER
    shrink[...] = jnp.where(col == chosen, 1.0, 0.0).astype(BF16)
    row = lax.broadcasted_iota(jnp.int32, (2 * COLUMN, PAIR), 0)
    col = lax.broadcasted_iota(jnp.int32, (2 * COLUMN, PAIR), 1)
    c = row % SLOT
    z = (((row // SLOT) % COUNT_Z) * ORDER + c) % DEPTH
    same = col == (row // COLUMN) * DEPTH + z
    grow[...] = jnp.where(same & (c < POINTS), 1.0, 0.0).astype(BF16)
    grow_own[...] = jnp.where(same & (c < ORDER), 1.0, 0.0).astype(BF16)


def spread_matrix(cell_matrix, matrix, from_x, from_y, from_xy):
    nodes = POINTS**3
    row = lax.broadcasted_iota(jnp.int32, (KDIM, nodes), 0)
    col = lax.broadcasted_iota(jnp.int32, (KDIM, nodes), 1)
    b = (row // SLOT) % SLOT
    c = row % SLOT
    source = (row // FACE) * POINTS * POINTS + b * POINTS + c
    pick = jnp.where((col == source) & (b < POINTS) & (c < POINTS), 1.0, 0.0).astype(BF16)
    half = dot_nn(pick, cell_matrix[...]).astype(BF16)
    full = dot_nt(half, pick)
    width = SLOT * FACE
    full = jnp.concatenate([full, jnp.zeros((KDIM, FACE), F32)], axis=1)
    lane = lax.broadcasted_iota(jnp.int32, (FACE, width), 1)
    at_x = lane // FACE == POINTS
    at_y = (lane // SLOT) % SLOT == POINTS

    def seen(rows, shift, mask):
        return jnp.where(mask[0 : rows.shape[0]], pltpu.roll(rows, shift, 1), 0.0)

    last_y = [full[a * FACE + ORDER * SLOT : a * FACE + POINTS * SLOT] for a in range(POINTS)]
    last_x = full[ORDER * FACE : POINTS * FACE]
    groups = []
    for a in range(POINTS):
        group = full[a * FACE : (a + 1) * FACE]
        first = group[0:SLOT] + seen(last_y[a], SLOT, at_y & (~at_x))
        if a == 0:
            first = first + seen(last_y[ORDER], FACE + SLOT, at_y & at_x)
        group = jnp.concatenate([first, group[SLOT:]], axis=0)
        if a == 0:
            group = group + seen(last_x, FACE, at_x & (~at_y))
        groups.append(group)
    matrix[...] = jnp.concatenate(groups, axis=0).astype(BF16)

    row = lax.broadcasted_iota(jnp.int32, (KDIM, FACE), 0)
    col = lax.broadcasted_iota(jnp.int32, (KDIM, FACE), 1)
    face_x = jnp.where(row == ORDER * FACE + col, 1.0, 0.0)
    face_y = jnp.where(row == (col // SLOT) * FACE + ORDER * SLOT + col % SLOT, 1.0, 0.0)
    faces = jnp.concatenate([face_x, face_y], axis=1).astype(BF16)
    both = dot_nn(full[:, 0:KDIM].astype(BF16), faces)
    from_xy[...] = both.astype(BF16)
    low = lax.broadcasted_iota(jnp.int32, (FACE, 2 * FACE), 1) < FACE
    groups = []
    for a in range(POINTS):
        group = both[a * FACE : (a + 1) * FACE]
        moved = jnp.concatenate(
            [group[ORDER * SLOT : POINTS * SLOT], jnp.zeros((FACE - SLOT, 2 * FACE), F32)], axis=0
        )
        groups.append(jnp.where(low, group, pltpu.roll(moved, FACE, 1)))
    from_x[...] = jnp.concatenate(groups, axis=0).astype(BF16)
    groups = []
    for a in range(POINTS):
        group = pltpu.roll(both[a * FACE : (a + 1) * FACE], FACE, 1)
        moved = both[ORDER * FACE : POINTS * FACE] if a == 0 else jnp.zeros_like(group)
        groups.append(jnp.where(low, group, moved))
    from_y[...] = jnp.concatenate(groups, axis=0).astype(BF16)


def padded_table():
    table = lagrange_table(ORDER, COARSE_ORDER).astype(np.float32)
    table = table.reshape(ORDER * ORDER, ORDER, -1)
    table = np.pad(table, ((0, 0), (0, SLOT - ORDER), (0, COARSE_ROWS - table.shape[-1])))
    return jnp.asarray(table.reshape(-1, COARSE_ROWS), F32).astype(BF16)


def local(coarse_states, record_target, cell_matrix, mass_scale, potential, filter_window):
    rows_x, rows_y, rows_z = mass_scale.shape
    size_x = lax.axis_size("dx")
    size_y = lax.axis_size("dy")
    node_total = float(rows_x * rows_y * rows_z * size_x * size_y)
    padded = (ROWS + 1, ROWS + 1, COLUMN, STATES)
    inside = (ROWS, ROWS, COLUMN, STATES)
    pair = (PAIR, STATES)
    face = (LINES,) + pair
    line = (COLUMN, STATES)
    share = STATES // size_y
    messages = 2 * size_y + size_x - 3
    by_row = coarse_states.transpose(1, 0, 2)
    vmem = pl.BlockSpec(memory_space=pltpu.VMEM)
    filtered, inverse, gram_matrix = pl.pallas_call(
        functools.partial(filter_kernel, size_x, size_y, node_total),
        out_shape=(
            jax.ShapeDtypeStruct((rows_x * rows_y * rows_z, 3 * STATES), BF16),
            jax.ShapeDtypeStruct((STATES, 3 * STATES), BF16),
            jax.ShapeDtypeStruct((STATES, STATES), F32),
        ),
        in_specs=[pl.BlockSpec(memory_space=pltpu.SMEM)] * 2
        + [pl.BlockSpec(memory_space=pl.ANY)] * 5,
        out_specs=(pl.BlockSpec(memory_space=pl.ANY), vmem, vmem),
        scratch_shapes=[
            pltpu.VMEM(padded, F32),
            pltpu.VMEM(inside, F32),
            pltpu.VMEM((KDIM, SLOT * FACE), BF16),
            pltpu.VMEM((KDIM, 2 * FACE), BF16),
            pltpu.VMEM((KDIM, 2 * FACE), BF16),
            pltpu.VMEM((KDIM, 2 * FACE), BF16),
            pltpu.VMEM((PAIR, 2 * COLUMN), BF16),
            pltpu.VMEM((2 * COLUMN, PAIR), BF16),
            pltpu.VMEM((2 * COLUMN, PAIR), BF16),
            pltpu.VMEM((SLOT, STATES), jnp.int32),
            pltpu.VMEM((ORDER * ORDER * SLOT, COARSE_ROWS), BF16),
            pltpu.VMEM(mass_scale.shape, F32),
            pltpu.VMEM(potential.shape, F32),
            pltpu.VMEM(cell_matrix.shape, BF16),
            pltpu.VMEM(by_row.shape, BF16),
            pltpu.VMEM((CELLS, COARSE_ROWS, STATES), BF16),
            pltpu.VMEM((3, CAPACITY, COARSE_ROWS, STATES), BF16),
            pltpu.VMEM((4 * CAPACITY, COARSE_ROWS, STATES), BF16),
            pltpu.VMEM((3, SLOT, STATES), jnp.int32),
            pltpu.SMEM((3, SLOT, STATES), jnp.int32),
            pltpu.VMEM((2,) + padded, F32),
            pltpu.VMEM(padded, F32),
            pltpu.VMEM((SLOT * FACE, COUNT_Z * STATES), BF16),
            pltpu.VMEM((ORDER * FACE, 2 * COUNT_Z * STATES), BF16),
            pltpu.VMEM((2 * FACE, COUNT_Z * STATES), BF16),
            pltpu.VMEM(face, BF16),
            pltpu.VMEM(face, BF16),
            pltpu.VMEM((2, LINES // 2 + LINES + 1) + pair, BF16),
            pltpu.VMEM((2, LINES // 2 + LINES) + pair, BF16),
            pltpu.VMEM(face, BF16),
            pltpu.VMEM(face, BF16),
            pltpu.VMEM(line, BF16),
            pltpu.VMEM((2,) + face, BF16),
            pltpu.VMEM((2,) + face, BF16),
            pltpu.VMEM((2,) + line, BF16),
            pltpu.VMEM((ROWS * ROWS * DEPTH, 3 * STATES), BF16),
            pltpu.VMEM((STATES, STATES), F32),
            pltpu.VMEM((2, size_y - 1, share, STATES), F32),
            pltpu.VMEM((2, size_x, share, STATES), F32),
            pltpu.VMEM((2, STATES, STATES), F32),
            pltpu.VMEM((STATES, 2 * STATES), F32),
            pltpu.SemaphoreType.DMA((3,)),
            pltpu.SemaphoreType.DMA((3,)),
            pltpu.SemaphoreType.DMA((3,)),
            pltpu.SemaphoreType.DMA((3,)),
            pltpu.SemaphoreType.DMA((3,)),
            pltpu.SemaphoreType.DMA,
            pltpu.SemaphoreType.DMA((5,)),
            pltpu.SemaphoreType.DMA((2, 8)),
            pltpu.SemaphoreType.DMA((2, 8)),
            pltpu.SemaphoreType.DMA((2, messages)),
            pltpu.SemaphoreType.DMA((2, messages)),
        ],
        compiler_params=pltpu.CompilerParams(
            collective_id=0, has_side_effects=True, vmem_limit_bytes=62 * 1024 * 1024
        ),
        cost_estimate=pl.CostEstimate(
            flops=6 * 4 * 2 * KDIM * KDIM * 512, bytes_accessed=10_000_000, transcendentals=0
        ),
        name="filter_twice",
    )(
        filter_window,
        record_target,
        by_row,
        padded_table(),
        mass_scale,
        potential,
        cell_matrix,
    )
    states = dot_nt(filtered, inverse)
    return (states.reshape(rows_x, rows_y, rows_z, STATES), gram_matrix)


def solution(mesh):
    in_specs = (
        P(("dx", "dy"), None, None),
        P(("dx", "dy")),
        P(),
        P("dx", "dy", None),
        P("dx", "dy", None),
        P(),
    )
    out_specs = (P("dx", "dy", None, None), P())
    return jax.shard_map(local, mesh=mesh, in_specs=in_specs, out_specs=out_specs, check_vma=False)
```

```python
import functools

import jax
import jax.numpy as jnp
import numpy as np
from jax import lax
from jax.experimental import pallas as pl
from jax.experimental.pallas import tpu as pltpu
from jax.sharding import PartitionSpec as P

ORDER = 6
COARSE_ORDER = 4
CHEB_DEGREE = 3
POINTS = ORDER + 1
COUNT_Z = 4
SLOT = 8
COLUMN = COUNT_Z * SLOT
ROWS = 12
STATES = 128
PAIRS = 4
KDIM = POINTS * SLOT * SLOT
FACE = SLOT * SLOT
DEPTH = COUNT_Z * ORDER
PAIR = 2 * DEPTH
LINES = ROWS // 2
CELLS = 16
PANEL = 16
CAPACITY = CELLS // 2
COARSE_ROWS = 128
MESH = pl.DeviceIdType.MESH
F32 = jnp.float32
BF16 = jnp.bfloat16


def node_points(degree_value):
    return -np.cos(np.pi * np.arange(degree_value + 1) / degree_value)


def lagrange_table(fine_degree, coarse_degree):
    targets = node_points(fine_degree)
    sources = node_points(coarse_degree)
    matrix = np.ones((fine_degree + 1, coarse_degree + 1))
    for p in range(coarse_degree + 1):
        for m in range(coarse_degree + 1):
            if m != p:
                matrix[:, p] = matrix[:, p] * (targets - sources[m]) / (sources[p] - sources[m])
    owned_rows = matrix[:fine_degree]
    first = owned_rows[:, None, None, :, None, None]
    second = owned_rows[None, :, None, None, :, None]
    third = owned_rows[None, None, :, None, None, :]
    product = first * second * third
    return product.reshape(fine_degree**3, (coarse_degree + 1) ** 3)


def cut_index(value, size):
    assert size & (size - 1) == 0
    return lax.shift_right_logical(value, size.bit_length() - 1), value & (size - 1)


def row_in_slot(shape, axis):
    return lax.broadcasted_iota(jnp.int32, shape, axis) % SLOT


def dot_nn(a, b):
    return lax.dot_general(a, b, (((1,), (0,)), ((), ())), preferred_element_type=F32)


def dot_tn(a, b):
    return lax.dot_general(a, b, (((0,), (0,)), ((), ())), preferred_element_type=F32)


def dot_nt(a, b):
    return lax.dot_general(a, b, (((1,), (1,)), ((), ())), preferred_element_type=F32)


def split_two(value):
    high = value.astype(BF16)
    return high, (value - high.astype(F32)).astype(BF16)


def split_three(value):
    high = value.astype(BF16)
    rest = value - high.astype(F32)
    middle = rest.astype(BF16)
    return high, middle, (rest - middle.astype(F32)).astype(BF16)


def factor_rows(work):
    size = STATES
    sub = lax.broadcasted_iota(jnp.int32, (PANEL, size), 0)
    lane = lax.broadcasted_iota(jnp.int32, (PANEL, size), 1)
    for base in range(0, size, PANEL):
        end = base + PANEL
        left = work[base:end, 0:size]
        right = work[base:end, size : 2 * size]
        columns = [
            jnp.broadcast_to(left[:, base + m : base + m + 1], (PANEL, size)) for m in range(PANEL)
        ]
        for m in range(PANEL):
            pivot = jnp.broadcast_to(columns[m][m : m + 1, :], (PANEL, size))
            scale = lax.rsqrt(pivot)
            below = sub > m
            at = sub == m
            coef = columns[m] * scale
            row_left = jnp.broadcast_to(left[m : m + 1, :], (PANEL, size)) * scale
            row_right = jnp.broadcast_to(right[m : m + 1, :], (PANEL, size)) * scale
            for n in range(m + 1, PANEL):
                entry = jnp.broadcast_to(columns[n][m : m + 1, :], (PANEL, size)) * scale
                columns[n] = jnp.where(below, columns[n] - coef * entry, columns[n])
            left = jnp.where(below, left - coef * row_left, jnp.where(at, row_left, left))
            right = jnp.where(below, right - coef * row_right, jnp.where(at, row_right, right))
        work[base:end, 0:size] = left
        work[base:end, size : 2 * size] = right
        if end < size:
            later = jnp.where(lane >= end, left, 0.0)
            l1, l2, l3 = [v.astype(F32) for v in split_three(later)]
            both = jnp.concatenate([left, right], axis=1)
            b1, b2, b3 = [v.astype(F32) for v in split_three(both)]
            lhs = jnp.concatenate([l1, l1, l2, l1, l3, l2], axis=0).astype(BF16)
            rhs = jnp.concatenate([b1, b2, b1, b3, b1, b2], axis=0).astype(BF16)
            work[end:size, :] = work[end:size, :] - dot_tn(lhs, rhs)[end:size, :]


def filter_kernel(
    size_x,
    size_y,
    node_total,
    window,
    targets,
    coarse_any,
    table_any,
    mass_any,
    pot_any,
    matrix_any,
    filtered_out,
    inverse_out,
    gram_out,
    mass,
    pot,
    matrix,
    from_x,
    from_y,
    from_xy,
    shrink,
    grow,
    grow_own,
    target_tile,
    table,
    mass_in,
    pot_in,
    cell_matrix,
    coarse_rows,
    coarse,
    slots,
    arrived,
    target_in,
    target_list,
    block,
    total,
    rhs,
    rhs_two,
    rhs_taken,
    send_x,
    send_y,
    take_x,
    take_y,
    back_x,
    back_y,
    back_c,
    got_x,
    got_y,
    got_c,
    split,
    partial,
    piece_in,
    ring_in,
    gram_sum,
    work,
    target_send,
    target_recv,
    list_sems,
    record_send,
    record_recv,
    store_sem,
    fetch_sems,
    send_sems,
    recv_sems,
    sum_send,
    sum_recv,
):
    me_x = lax.axis_index("dx")
    me_y = lax.axis_index("dy")

    def at(step_x, step_y):
        return (lax.rem(me_x + step_x + size_x, size_x), lax.rem(me_y + step_y + size_y, size_y))

    partners = [at(0, d) for d in range(1, size_y)] + [at(d, 0) for d in range(1, size_x)]
    partners += [at(1, 1), at(-1, -1), at(1, -1), at(-1, 1)]
    barrier = pltpu.get_barrier_semaphore()
    for partner in partners:
        pl.semaphore_signal(barrier, inc=1, device_id=partner, device_id_type=MESH)
    fetches = [
        pltpu.make_async_copy(src, dst, fetch_sems.at[i])
        for i, (src, dst) in enumerate(
            [
                (matrix_any, cell_matrix),
                (mass_any, mass_in),
                (pot_any, pot_in),
                (table_any, table),
                (coarse_any, coarse_rows),
            ]
        )
    ]
    for fetch in fetches:
        fetch.start()
    steps = (None, (0, 1), (1, 0), (1, 1))
    ranks = []
    counts = [0, 0, 0, 0]
    for r in range(CELLS):
        device = cut_index(targets[r], CELLS)[0]
        to_x, to_y = cut_index(device, size_y)
        step_x = (to_x - me_x + size_x) & (size_x - 1)
        step_y = (to_y - me_y + size_y) & (size_y - 1)
        bucket = 2 * step_x + step_y
        rank = 0
        for index in range(4):
            rank = jnp.where(bucket == index, counts[index], rank)
            counts[index] = jnp.where(bucket == index, counts[index] + 1, counts[index])
        ranks.append(bucket * CAPACITY + rank)

    def record_of(slot):
        found = 0
        for r in range(CELLS):
            found = jnp.where(ranks[r] == slot, r, found)
        return found & (CELLS - 1)

    fetches[4].wait()
    coarse_count = coarse_rows.shape[0]
    coarse[:, COARSE_ROWS - 16 :] = jnp.zeros((CELLS, 16, STATES), BF16)
    for half in range(2):
        group = slice(half * SLOT, (half + 1) * SLOT)
        turned = jnp.swapaxes(coarse_rows[...].astype(F32)[:, group], 0, 1)
        coarse[group, 0:coarse_count] = turned.astype(BF16)
    for index in (3, 2, 1):
        for k in range(CAPACITY):
            slots[index - 1, k] = coarse[record_of(index * CAPACITY + k)]
    tile_lane = lax.broadcasted_iota(jnp.int32, (SLOT, STATES), 1)
    tile = jnp.zeros((SLOT, STATES), jnp.int32)
    for r in range(CELLS):
        tile = jnp.where(tile_lane == r, targets[r], tile)
    target_tile[...] = tile
    pl.semaphore_wait(barrier, len(partners))
    target_copies, record_copies = {}, {}
    for index in (3, 2, 1):
        target_copies[index] = pltpu.make_async_remote_copy(
            src_ref=target_tile,
            dst_ref=target_in.at[index - 1],
            send_sem=target_send.at[index - 1],
            recv_sem=target_recv.at[index - 1],
            device_id=at(*steps[index]),
            device_id_type=MESH,
        )
        target_copies[index].start()
    for index in (3, 2, 1):
        record_copies[index] = pltpu.make_async_remote_copy(
            src_ref=slots.at[index - 1],
            dst_ref=arrived.at[pl.ds(index * CAPACITY, CAPACITY)],
            send_sem=record_send.at[index - 1],
            recv_sem=record_recv.at[index - 1],
            device_id=at(*steps[index]),
            device_id_type=MESH,
        )
        record_copies[index].start()
    for k in range(CAPACITY):
        arrived[k] = coarse[record_of(k)]

    for fetch in fetches[0:4]:
        fetch.wait()
    place_nodes(mass_in, pot_in, mass, pot)
    spread_matrix(cell_matrix, matrix, from_x, from_y, from_xy)
    line_tables(shrink, grow, grow_own)
    block[1] = jnp.zeros(block.shape[1:], F32)

    for index in (3, 2, 1):
        target_copies[index].wait()
    lists = [
        pltpu.make_async_copy(target_in.at[i], target_list.at[i], list_sems.at[i]) for i in range(3)
    ]
    for copy in lists:
        copy.start()
    for copy in lists:
        copy.wait()
    own = me_x * size_y + me_y
    places = [0] * CELLS
    for index in range(4):
        seen = 0
        for r in range(CELLS):
            target = targets[r] if index == 0 else target_list[index - 1, 0, r]
            device, cell = cut_index(target, CELLS)
            hit = device == own
            cell = jnp.where(hit, cell, -1)
            slot = index * CAPACITY + seen
            for g in range(CELLS):
                places[g] = jnp.where(cell == g, slot, places[g])
            seen = jnp.where(hit, seen + 1, seen)
    places = [p & (4 * CAPACITY - 1) for p in places]
    for index in (3, 2, 1):
        record_copies[index].wait()
    slot_row = row_in_slot((COLUMN, STATES), 0)
    for e in range(2):
        for f in range(2):
            for h in range(COUNT_Z):
                rhs[0:COARSE_ROWS, h * STATES : (h + 1) * STATES] = arrived[
                    places[(2 * e + f) * COUNT_Z + h]
                ]
            fine = dot_nn(table[...], rhs[0:COARSE_ROWS, :]).astype(BF16).astype(F32)
            for a in range(ORDER):
                for b in range(ORDER):
                    first = (a * ORDER + b) * SLOT
                    lines = [
                        fine[first : first + SLOT, h * STATES : (h + 1) * STATES]
                        for h in range(COUNT_Z)
                    ]
                    lines = jnp.concatenate(lines, axis=0)
                    again = pltpu.roll(lines, COLUMN - SLOT + ORDER, 0)
                    block[0, e * ORDER + a, f * ORDER + b] = jnp.where(
                        slot_row == ORDER, again, lines
                    )

    low = window[0]
    high = window[1]
    center = (low + high) / 2.0
    radius = (high - low) / 2.0

    def remote(turn, index, src, dst, step_x, step_y):
        return pltpu.make_async_remote_copy(
            src_ref=src,
            dst_ref=dst,
            send_sem=send_sems.at[turn, index],
            recv_sem=recv_sems.at[turn, index],
            device_id=at(step_x, step_y),
            device_id_type=MESH,
        )

    zeros = jnp.zeros((SLOT, STATES), F32)

    def pack(first, second):
        return jnp.concatenate([first, second], axis=0).astype(BF16)

    def add_product(product, e, f, points_x, points_y, written):
        for a in range(points_x):
            for b in range(points_y):
                first = (a * SLOT + b) * SLOT
                x, y = e * ORDER + a, f * ORDER + b
                for h in range(COUNT_Z):
                    rows = slice(h * SLOT, (h + 1) * SLOT)
                    part = product[first : first + SLOT, h * STATES : (h + 1) * STATES]
                    if (x, y) in written:
                        part = part + total[x, y, rows]
                    total[x, y, rows] = part
                written.add((x, y))

    def gather(q, e, f, out, lane):
        points_x = POINTS if e == 0 else ORDER
        for a in range(points_x):
            x = e * ORDER + a
            for h in range(COUNT_Z):
                rows = slice(h * SLOT, (h + 1) * SLOT)
                chunks = []
                for b in range(POINTS):
                    y = f * ORDER + b
                    own = y < ROWS
                    chunks.append(mass[x, y, rows] * block[q, x, y, rows] if own else zeros)
                chunks.append(chunks[0] if f == 0 else zeros)
                for i in range(PAIRS):
                    tile = pack(chunks[2 * i], chunks[2 * i + 1])
                    copies = [a, POINTS] if (a == 0 and e == 0) else [a]
                    for place in copies:
                        first = (place * PAIRS + i) * 2 * SLOT
                        lanes = slice(lane + h * STATES, lane + (h + 1) * STATES)
                        out[first : first + 2 * SLOT, lanes] = tile

    def taken_rows(base, lines, h):
        chunks = [line[h * SLOT : (h + 1) * SLOT] if line is not None else zeros for line in lines]
        for i in range(PAIRS):
            first = base + i * 2 * SLOT
            rhs_taken[first : first + 2 * SLOT, h * STATES : (h + 1) * STATES] = pack(
                chunks[2 * i], chunks[2 * i + 1]
            )

    def taken_column(e, f, factor, runs, points_x, points_y, written):
        for index, lines in enumerate(runs):
            for h in range(COUNT_Z):
                taken_rows(index * FACE, lines, h)
        depth = FACE * len(runs)
        product = dot_nn(factor[:, 0:depth], rhs_taken[0:depth, :])
        add_product(product, e, f, points_x, points_y, written)

    def narrow(lines, out):
        wide = lines.astype(BF16).reshape(LINES, 2 * COLUMN, STATES)
        wide = jnp.concatenate([wide[i] for i in range(LINES)], axis=1)
        packed = dot_nn(shrink[...], wide).astype(BF16)
        for i in range(LINES):
            out[i] = packed[:, i * STATES : (i + 1) * STATES]

    def widen(pairs, rows_of_slot):
        wide = dot_nn(rows_of_slot[...], jnp.concatenate(pairs, axis=1))
        lines = []
        for i in range(len(pairs)):
            for half in range(2):
                lines.append(
                    wide[half * COLUMN : (half + 1) * COLUMN, i * STATES : (i + 1) * STATES]
                )
        return lines

    def folded(raw):
        axis = raw.ndim - 2
        first = row_in_slot(raw.shape, axis) == 0
        return raw + jnp.where(first, pltpu.roll(raw, SLOT - ORDER, axis), 0.0)

    def finish(q, index, alpha, beta):
        raw = total[index]
        slot_row = row_in_slot(raw.shape, 1)
        summed = folded(raw)
        again = pltpu.roll(summed, COLUMN - SLOT + ORDER, 1)
        full = jnp.where(slot_row < ORDER, summed, jnp.where(slot_row == ORDER, again, 0.0))
        value = block[(q,) + index]
        result = mass[index] * full + (pot[index] - center) * value
        block[(1 - q,) + index] = alpha * result - beta * block[(1 - q,) + index]

    def one_apply(t):
        q = t % 2
        first = (t % CHEB_DEGREE) == 0
        alpha = jnp.where(first, 1.0, 2.0) / radius
        beta = jnp.where(first, 0.0, 1.0)
        quarter = LINES // 2
        half = pl.ds(quarter, quarter)
        values = [
            remote(q, 0, send_x, take_x.at[q, pl.ds(quarter, LINES)], -1, 0),
            remote(q, 1, send_x.at[half], take_x.at[q, pl.ds(0, quarter)], -1, 1),
            remote(
                q, 2, send_x.at[pl.ds(0, 1)], take_x.at[q, pl.ds(quarter + LINES, 1)], -1, -1
            ),
            remote(q, 3, send_y.at[half], take_y.at[q, pl.ds(0, quarter)], 1, -1),
            remote(q, 4, send_y, take_y.at[q, pl.ds(quarter, LINES)], 0, -1),
        ]
        sum_x = remote(q, 5, back_x, got_x.at[q], 1, 0)
        sum_y = remote(q, 6, back_y, got_y.at[q], 0, 1)
        sum_c = remote(q, 7, back_c, got_c.at[q], 1, 1)
        narrow(mass[0, 0:ROWS] * block[q, 0, 0:ROWS], send_x)
        for copy in values[0:3]:
            copy.start()
        written = set()
        width = COUNT_Z * STATES
        inner = FACE * ORDER
        gather(q, 1, 0, rhs_two, 0)
        gather(q, 1, 1, rhs_two, width)
        face = dot_nn(matrix[inner : inner + FACE, 0:inner], rhs_two[...])

        def face_line(f, b):
            parts = [
                face[b * SLOT : (b + 1) * SLOT, f * width + h * STATES : f * width + (h + 1) * STATES]
                for h in range(COUNT_Z)
            ]
            return jnp.concatenate(parts, axis=0)

        lines = [face_line(0, b) for b in range(ORDER)]
        lines.append(face_line(0, ORDER) + face_line(1, 0))
        lines += [face_line(1, b) for b in range(1, ORDER)]
        narrow(folded(jnp.stack(lines)), back_x)
        sum_x.start()
        back_c[...] = face_line(1, ORDER).astype(BF16)
        sum_c.start()
        narrow(mass[0:ROWS, 0] * block[q, 0:ROWS, 0], send_y)
        for copy in values[3:5]:
            copy.start()
        product = dot_nn(matrix[0:inner, 0:inner], rhs_two[:, width : 2 * width])
        add_product(product, 1, 1, ORDER, POINTS, written)
        gather(q, 0, 1, rhs, 0)
        add_product(dot_nn(matrix[...], rhs[...]), 0, 1, POINTS, POINTS, written)
        narrow(folded(total[0:ROWS, ROWS]), back_y)
        sum_y.start()
        product = dot_nn(matrix[0:inner, 0:inner], rhs_two[:, 0:width])
        add_product(product, 1, 0, ORDER, POINTS, written)
        gather(q, 0, 0, rhs, 0)
        add_product(dot_nn(matrix[...], rhs[...]), 0, 0, POINTS, POINTS, written)

        @pl.when(t == CHEB_DEGREE)
        def _():
            gather_pieces(0)

        @pl.when(t == CHEB_DEGREE + 1)
        def _():
            gather_rows(0)

        last = 2 * ORDER
        none = [None]
        values[4].wait()
        along_y = widen([take_y[q, i] for i in range(quarter, quarter + LINES)], grow)
        taken_column(0, 1, from_y, [along_y[0:POINTS] + none], POINTS, ORDER, written)

        def interior(x, carry):
            finish(q, (x, pl.ds(1, ROWS - 1)), alpha, beta)
            return carry

        lax.fori_loop(1, ORDER, interior, 0)
        for copy in values[0:4]:
            copy.wait()
        along_x = widen([take_x[q, i] for i in range(quarter + LINES + 1)], grow)
        taken_column(
            1,
            1,
            from_xy,
            [along_x[last : last + POINTS] + none, along_y[ORDER:] + none * 2],
            ORDER,
            ORDER,
            written,
        )
        taken_column(
            1,
            0,
            from_x,
            [along_x[ORDER : last + 1] + none, along_x[0:POINTS] + none],
            ORDER,
            POINTS,
            written,
        )
        lax.fori_loop(ORDER, ROWS, interior, 0)
        behind_y = widen([take_y[q, i] for i in range(quarter)], grow)
        for h in range(COUNT_Z):
            taken_rows(0, behind_y + [along_y[0]] + none, h)
        product = dot_nn(from_y[0:FACE, FACE : 2 * FACE], rhs_taken[0:FACE, :])
        add_product(product, 0, 1, 1, ORDER, written)
        sum_y.wait()
        for x, line in enumerate(widen([got_y[q, i] for i in range(LINES)], grow_own)):
            total[x, 0] += line
        finish(q, (slice(1, ROWS), 0), alpha, beta)
        for copy in (sum_c, sum_x):
            copy.wait()
        total[0, 0] += got_c[q].astype(F32)
        for y, line in enumerate(widen([got_x[q, i] for i in range(LINES)], grow_own)):
            total[0, y] += line
        finish(q, (0, slice(0, ROWS)), alpha, beta)

    share = STATES // size_y

    def move(p, index, src, dst, device):
        return pltpu.make_async_remote_copy(
            src_ref=src,
            dst_ref=dst,
            send_sem=sum_send.at[p, index],
            recv_sem=sum_recv.at[p, index],
            device_id=device,
            device_id_type=MESH,
        )

    def rows_of(owner):
        return pl.ds(pl.multiple_of(owner * share, SLOT), share)

    mine = rows_of(me_y)

    def piece_copies(p):
        copies = []
        for d in range(1, size_y):
            device = at(0, d)
            src = partial.at[rows_of(device[1])]
            copies.append(move(p, d - 1, src, piece_in.at[p, d - 1], device))
        return copies

    def ring_copies(p):
        own = ring_in.at[p, me_x]
        return [move(p, size_y + d - 2, own, own, at(d, 0)) for d in range(1, size_x)]

    def row_copies(p):
        own = gram_sum.at[p, mine]
        first = size_y + size_x - 3
        return [move(p, first + d, own, own, at(0, d)) for d in range(1, size_y)]

    def gather_pieces(p):
        for copy in piece_copies(p):
            copy.wait()
        piece = partial[mine, :]
        for d in range(1, size_y):
            piece = piece + piece_in[p, d - 1]
        ring_in[p, me_x] = piece
        for copy in ring_copies(p):
            copy.start()

    def gather_rows(p):
        for copy in ring_copies(p):
            copy.wait()
        piece = ring_in[p, 0]
        for d in range(1, size_x):
            piece = piece + ring_in[p, d]
        gram_sum[p, mine] = piece / node_total
        for copy in row_copies(p):
            copy.start()

    def begin_sum(p, q):
        def divide(x, inner):
            value = block[q, x, 0:ROWS]
            value = jnp.concatenate(
                [value[:, h * SLOT : h * SLOT + ORDER] for h in range(COUNT_Z)], axis=1
            )
            high_part, low_part = split_two(value.reshape(ROWS * DEPTH, STATES))
            rows = pl.ds(pl.multiple_of(x * ROWS * DEPTH, ROWS * DEPTH), ROWS * DEPTH)
            split[rows, 0:STATES] = high_part
            split[rows, STATES : 2 * STATES] = low_part
            split[rows, 2 * STATES : 3 * STATES] = high_part
            return inner

        lax.fori_loop(0, ROWS, divide, 0)
        products = dot_tn(split[:, 0:STATES], split[:, 0 : 2 * STATES])
        cross = products[:, STATES : 2 * STATES]
        partial[...] = products[:, 0:STATES] + cross + cross.T
        for copy in piece_copies(p):
            copy.start()

    def end_sum(p):
        for copy in row_copies(p):
            copy.wait()
        work[:, 0:STATES] = gram_sum[p]
        shape = (STATES, STATES)
        diagonal = lax.broadcasted_iota(jnp.int32, shape, 0) == lax.broadcasted_iota(
            jnp.int32, shape, 1
        )
        work[:, STATES : 2 * STATES] = jnp.where(diagonal, 1.0, 0.0)
        factor_rows(work)
        return work[:, STATES : 2 * STATES]

    def step(t, carry):
        @pl.when(t == CHEB_DEGREE)
        def _():
            begin_sum(0, CHEB_DEGREE % 2)

        one_apply(t)

        @pl.when(t == CHEB_DEGREE + 1)
        def _():
            pair = stacked_inverse(end_sum(0))

            def turn(x, inner):
                for index in range(2):
                    value = block[index, x, 0:ROWS].reshape(ROWS * COLUMN, STATES)
                    block[index, x, 0:ROWS] = times_inverse(value, pair).reshape(
                        ROWS, COLUMN, STATES
                    )
                return inner

            lax.fori_loop(0, ROWS, turn, 0)

        return carry

    lax.fori_loop(0, 2 * CHEB_DEGREE, step, 0)
    begin_sum(1, 0)
    store = pltpu.make_async_copy(split, filtered_out, store_sem)
    store.start()
    gather_pieces(1)
    gather_rows(1)
    inverse = end_sum(1)
    high_part, low_part = split_two(inverse)
    inverse_out[...] = jnp.concatenate([high_part, high_part, low_part], axis=1)
    gram_out[...] = gram_sum[1]
    store.wait()


def stacked_inverse(inverse):
    high, low = split_two(inverse)
    return jnp.concatenate(
        [jnp.concatenate([high, high], axis=1), jnp.concatenate([low, low], axis=1)], axis=0
    )


def times_inverse(value, pair):
    high, low = split_two(value)
    both = dot_nt(jnp.concatenate([high, low], axis=1), pair)
    return both[:, 0:STATES] + both[:, STATES : 2 * STATES]


def place_nodes(mass_in, pot_in, mass, pot):
    width = 3 * DEPTH
    row = lax.broadcasted_iota(jnp.int32, (COLUMN, width), 0)
    lane = lax.broadcasted_iota(jnp.int32, (COLUMN, width), 1)
    within = row % SLOT
    source = lax.rem((row // SLOT) * ORDER + within, DEPTH)
    pick = jnp.where((lax.rem(lane, DEPTH) == source) & (within < POINTS), 1.0, 0.0)
    ones = jnp.ones((width, STATES), BF16)

    def one(x, carry):
        for values, out in ((mass_in, mass), (pot_in, pot)):
            parts = [v.astype(F32) for v in split_three(values[x])]
            parts = jnp.concatenate(parts, axis=1)
            spread = [
                jnp.broadcast_to(parts[y : y + 1, :], (COLUMN, width)) * pick for y in range(ROWS)
            ]
            lines = dot_nn(jnp.concatenate(spread, axis=0).astype(BF16), ones)
            out[x, 0:ROWS] = lines.reshape(ROWS, COLUMN, STATES)
        return carry

    lax.fori_loop(0, ROWS, one, 0, unroll=2)
    mass[ROWS] = jnp.ones(mass.shape[1:], F32)
    mass[0:ROWS, ROWS] = jnp.ones((ROWS, COLUMN, STATES), F32)


def line_tables(shrink, grow, grow_own):
    row = lax.broadcasted_iota(jnp.int32, (PAIR, 2 * COLUMN), 0)
    col = lax.broadcasted_iota(jnp.int32, (PAIR, 2 * COLUMN), 1)
    z = row % DEPTH
    chosen = (row // DEPTH) * COLUMN + (z // ORDER) * SLOT + z % ORDER
    shrink[...] = jnp.where(col == chosen, 1.0, 0.0).astype(BF16)
    row = lax.broadcasted_iota(jnp.int32, (2 * COLUMN, PAIR), 0)
    col = lax.broadcasted_iota(jnp.int32, (2 * COLUMN, PAIR), 1)
    c = row % SLOT
    z = (((row // SLOT) % COUNT_Z) * ORDER + c) % DEPTH
    same = col == (row // COLUMN) * DEPTH + z
    grow[...] = jnp.where(same & (c < POINTS), 1.0, 0.0).astype(BF16)
    grow_own[...] = jnp.where(same & (c < ORDER), 1.0, 0.0).astype(BF16)


def spread_matrix(cell_matrix, matrix, from_x, from_y, from_xy):
    nodes = POINTS**3
    row = lax.broadcasted_iota(jnp.int32, (KDIM, nodes), 0)
    col = lax.broadcasted_iota(jnp.int32, (KDIM, nodes), 1)
    b = (row // SLOT) % SLOT
    c = row % SLOT
    source = (row // FACE) * POINTS * POINTS + b * POINTS + c
    pick = jnp.where((col == source) & (b < POINTS) & (c < POINTS), 1.0, 0.0).astype(BF16)
    half = dot_nn(pick, cell_matrix[...]).astype(BF16)
    full = dot_nt(half, pick)
    width = SLOT * FACE
    full = jnp.concatenate([full, jnp.zeros((KDIM, FACE), F32)], axis=1)
    lane = lax.broadcasted_iota(jnp.int32, (FACE, width), 1)
    at_x = lane // FACE == POINTS
    at_y = (lane // SLOT) % SLOT == POINTS

    def seen(rows, shift, mask):
        return jnp.where(mask[0 : rows.shape[0]], pltpu.roll(rows, shift, 1), 0.0)

    last_y = [full[a * FACE + ORDER * SLOT : a * FACE + POINTS * SLOT] for a in range(POINTS)]
    last_x = full[ORDER * FACE : POINTS * FACE]
    groups = []
    for a in range(POINTS):
        group = full[a * FACE : (a + 1) * FACE]
        first = group[0:SLOT] + seen(last_y[a], SLOT, at_y & (~at_x))
        if a == 0:
            first = first + seen(last_y[ORDER], FACE + SLOT, at_y & at_x)
        group = jnp.concatenate([first, group[SLOT:]], axis=0)
        if a == 0:
            group = group + seen(last_x, FACE, at_x & (~at_y))
        groups.append(group)
    matrix[...] = jnp.concatenate(groups, axis=0).astype(BF16)

    row = lax.broadcasted_iota(jnp.int32, (KDIM, FACE), 0)
    col = lax.broadcasted_iota(jnp.int32, (KDIM, FACE), 1)
    face_x = jnp.where(row == ORDER * FACE + col, 1.0, 0.0)
    face_y = jnp.where(row == (col // SLOT) * FACE + ORDER * SLOT + col % SLOT, 1.0, 0.0)
    faces = jnp.concatenate([face_x, face_y], axis=1).astype(BF16)
    both = dot_nn(full[:, 0:KDIM].astype(BF16), faces)
    from_xy[...] = both.astype(BF16)
    low = lax.broadcasted_iota(jnp.int32, (FACE, 2 * FACE), 1) < FACE
    groups = []
    for a in range(POINTS):
        group = both[a * FACE : (a + 1) * FACE]
        moved = jnp.concatenate(
            [group[ORDER * SLOT : POINTS * SLOT], jnp.zeros((FACE - SLOT, 2 * FACE), F32)], axis=0
        )
        groups.append(jnp.where(low, group, pltpu.roll(moved, FACE, 1)))
    from_x[...] = jnp.concatenate(groups, axis=0).astype(BF16)
    groups = []
    for a in range(POINTS):
        group = pltpu.roll(both[a * FACE : (a + 1) * FACE], FACE, 1)
        moved = both[ORDER * FACE : POINTS * FACE] if a == 0 else jnp.zeros_like(group)
        groups.append(jnp.where(low, group, moved))
    from_y[...] = jnp.concatenate(groups, axis=0).astype(BF16)


def padded_table():
    table = lagrange_table(ORDER, COARSE_ORDER).astype(np.float32)
    table = table.reshape(ORDER * ORDER, ORDER, -1)
    table = np.pad(table, ((0, 0), (0, SLOT - ORDER), (0, COARSE_ROWS - table.shape[-1])))
    return jnp.asarray(table.reshape(-1, COARSE_ROWS), F32).astype(BF16)


def local(coarse_states, record_target, cell_matrix, mass_scale, potential, filter_window):
    rows_x, rows_y, rows_z = mass_scale.shape
    size_x = lax.axis_size("dx")
    size_y = lax.axis_size("dy")
    node_total = float(rows_x * rows_y * rows_z * size_x * size_y)
    padded = (ROWS + 1, ROWS + 1, COLUMN, STATES)
    inside = (ROWS, ROWS, COLUMN, STATES)
    pair = (PAIR, STATES)
    face = (LINES,) + pair
    line = (COLUMN, STATES)
    share = STATES // size_y
    messages = 2 * size_y + size_x - 3
    by_row = coarse_states.transpose(1, 0, 2)
    vmem = pl.BlockSpec(memory_space=pltpu.VMEM)
    filtered, inverse, gram_matrix = pl.pallas_call(
        functools.partial(filter_kernel, size_x, size_y, node_total),
        out_shape=(
            jax.ShapeDtypeStruct((rows_x * rows_y * rows_z, 3 * STATES), BF16),
            jax.ShapeDtypeStruct((STATES, 3 * STATES), BF16),
            jax.ShapeDtypeStruct((STATES, STATES), F32),
        ),
        in_specs=[pl.BlockSpec(memory_space=pltpu.SMEM)] * 2
        + [pl.BlockSpec(memory_space=pl.ANY)] * 5,
        out_specs=(pl.BlockSpec(memory_space=pl.ANY), vmem, vmem),
        scratch_shapes=[
            pltpu.VMEM(padded, F32),
            pltpu.VMEM(inside, F32),
            pltpu.VMEM((KDIM, SLOT * FACE), BF16),
            pltpu.VMEM((KDIM, 2 * FACE), BF16),
            pltpu.VMEM((KDIM, 2 * FACE), BF16),
            pltpu.VMEM((KDIM, 2 * FACE), BF16),
            pltpu.VMEM((PAIR, 2 * COLUMN), BF16),
            pltpu.VMEM((2 * COLUMN, PAIR), BF16),
            pltpu.VMEM((2 * COLUMN, PAIR), BF16),
            pltpu.VMEM((SLOT, STATES), jnp.int32),
            pltpu.VMEM((ORDER * ORDER * SLOT, COARSE_ROWS), BF16),
            pltpu.VMEM(mass_scale.shape, F32),
            pltpu.VMEM(potential.shape, F32),
            pltpu.VMEM(cell_matrix.shape, BF16),
            pltpu.VMEM(by_row.shape, BF16),
            pltpu.VMEM((CELLS, COARSE_ROWS, STATES), BF16),
            pltpu.VMEM((3, CAPACITY, COARSE_ROWS, STATES), BF16),
            pltpu.VMEM((4 * CAPACITY, COARSE_ROWS, STATES), BF16),
            pltpu.VMEM((3, SLOT, STATES), jnp.int32),
            pltpu.SMEM((3, SLOT, STATES), jnp.int32),
            pltpu.VMEM((2,) + padded, F32),
            pltpu.VMEM(padded, F32),
            pltpu.VMEM((SLOT * FACE, COUNT_Z * STATES), BF16),
            pltpu.VMEM((ORDER * FACE, 2 * COUNT_Z * STATES), BF16),
            pltpu.VMEM((2 * FACE, COUNT_Z * STATES), BF16),
            pltpu.VMEM(face, BF16),
            pltpu.VMEM(face, BF16),
            pltpu.VMEM((2, LINES // 2 + LINES + 1) + pair, BF16),
            pltpu.VMEM((2, LINES // 2 + LINES) + pair, BF16),
            pltpu.VMEM(face, BF16),
            pltpu.VMEM(face, BF16),
            pltpu.VMEM(line, BF16),
            pltpu.VMEM((2,) + face, BF16),
            pltpu.VMEM((2,) + face, BF16),
            pltpu.VMEM((2,) + line, BF16),
            pltpu.VMEM((ROWS * ROWS * DEPTH, 3 * STATES), BF16),
            pltpu.VMEM((STATES, STATES), F32),
            pltpu.VMEM((2, size_y - 1, share, STATES), F32),
            pltpu.VMEM((2, size_x, share, STATES), F32),
            pltpu.VMEM((2, STATES, STATES), F32),
            pltpu.VMEM((STATES, 2 * STATES), F32),
            pltpu.SemaphoreType.DMA((3,)),
            pltpu.SemaphoreType.DMA((3,)),
            pltpu.SemaphoreType.DMA((3,)),
            pltpu.SemaphoreType.DMA((3,)),
            pltpu.SemaphoreType.DMA((3,)),
            pltpu.SemaphoreType.DMA,
            pltpu.SemaphoreType.DMA((5,)),
            pltpu.SemaphoreType.DMA((2, 8)),
            pltpu.SemaphoreType.DMA((2, 8)),
            pltpu.SemaphoreType.DMA((2, messages)),
            pltpu.SemaphoreType.DMA((2, messages)),
        ],
        compiler_params=pltpu.CompilerParams(
            collective_id=0, has_side_effects=True, vmem_limit_bytes=62 * 1024 * 1024
        ),
        cost_estimate=pl.CostEstimate(
            flops=6 * 4 * 2 * KDIM * KDIM * 512, bytes_accessed=10_000_000, transcendentals=0
        ),
        name="filter_twice",
    )(
        filter_window,
        record_target,
        by_row,
        padded_table(),
        mass_scale,
        potential,
        cell_matrix,
    )
    states = dot_nt(filtered, inverse)
    return (states.reshape(rows_x, rows_y, rows_z, STATES), gram_matrix)


def solution(mesh):
    in_specs = (
        P(("dx", "dy"), None, None),
        P(("dx", "dy")),
        P(),
        P("dx", "dy", None),
        P("dx", "dy", None),
        P(),
    )
    out_specs = (P("dx", "dy", None, None), P())
    return jax.shard_map(local, mesh=mesh, in_specs=in_specs, out_specs=out_specs, check_vma=False)
```
